32 devices in a mesh: ep: 8 (over z, x), hp: 4 (over y, core).
Axes of the slice: x: 2, y: 2, z: 4, core: 2. Of those that a mesh axis runs over, the one named last changes fastest.
Arguments:
- tokens: bfloat16 [8192, 1280], P(('ep', 'hp')), may hold values from -6 to 6
- attn_gain: bfloat16 [1280], P('hp'), may hold values from 0.5 to 1.5
- query_weight: bfloat16 [1280, 1280], P('hp'), may hold values from -0.15625 to 0.15625
- key_weight: bfloat16 [1280, 1280], P('hp'), may hold values from -0.15625 to 0.15625
- value_weight: bfloat16 [1280, 1280], P('hp'), may hold values from -0.15625 to 0.15625
- out_weight: bfloat16 [1280, 1280], P('hp'), may hold values from -2.5 to 2.5
- ffn_gain: bfloat16 [1280], P('hp'), may hold values from 0.5 to 1.5
- router_weight: bfloat16 [1280, 16], P('hp'), may hold values from -0.078125 to 0.078125
- shared_gate: bfloat16 [1280, 896], P('hp'), may hold values from -0.15625 to 0.15625
- shared_up: bfloat16 [1280, 896], P('hp'), may hold values from -0.15625 to 0.15625
- shared_down: bfloat16 [896, 1280], P('hp'), may hold values from -0.1875 to 0.1875
- expert_gate: bfloat16 [16, 1280, 896], P('ep', None, 'hp'), may hold values from -0.15625 to 0.15625
- expert_up: bfloat16 [16, 1280, 896], P('ep', None, 'hp'), may hold values from -0.15625 to 0.15625
- expert_down: bfloat16 [16, 896, 1280], P('ep', 'hp'), may hold values from -0.75 to 0.75
- routes: int32 [8192, 7], P(('ep', 'hp')), may hold values from 0 to 15, all different within a row; in each aligned block of 256 rows (0 to 255, 256 to 511, ...) at most 140 rows name the same one
- keep_mask: int32 [8192, 7], P(('ep', 'hp')), may hold values 0 or 1
- cotangent: bfloat16 [8192, 1280], P(('ep', 'hp')), may hold values from -6 to 6
Outputs:
- layer_out: bfloat16 [8192, 1280], P(('ep', 'hp'))
- tokens_grad: float32 [8192, 1280], P(('ep', 'hp'))
- attn_gain_grad: float32 [1280], P('hp')
- query_grad: float32 [1280, 1280], P('hp')
- key_grad: float32 [1280, 1280], P('hp')
- value_grad: float32 [1280, 1280], P('hp')
- out_grad: float32 [1280, 1280], P('hp')
- ffn_gain_grad: float32 [1280], P('hp')
- router_grad: float32 [1280, 16], P('hp')
- shared_gate_grad: float32 [1280, 896], P('hp')
- shared_up_grad: float32 [1280, 896], P('hp')
- shared_down_grad: float32 [896, 1280], P('hp')
- expert_gate_grad: float32 [16, 1280, 896], P('ep', None, 'hp')
- expert_up_grad: float32 [16, 1280, 896], P('ep', None, 'hp')
- expert_down_grad: float32 [16, 896, 1280], P('ep', 'hp')
- expert_counts: int32 [16], P('hp')
The draws below stay inside these ranges and needn't reach their ends.
Inputs may be any that keep to these rules, and one draw needn't show every extreme that they name: `routes`: each row names 7 different experts. Within each device's 256 rows no expert is named more than 140 times, and in some device's rows one expert is named exactly 140 times.
All inputs are finite; a program needn't handle non-finite values. No bound on the sum of `keep_mask` on one device may be relied on, other than what follows from the above.
Results may differ from the reference program's by a relative error of at most 0.024.
Values may be sent and summed in bfloat16 or wider, within the bound.
A program may use at most 384 MiB of HBM per device.

```python
import math
import jax
import jax.numpy as jnp
import numpy as np
from jax import lax

D = 1280
H = 10
HD = 128
FF = 896
TOP = 7
TOK_DEV = 256
EXPERTS = 16
SEQ = 1024
TOKENS = 8192
CAP = 140


def place_ends(drawn, key, smallest, largest):
    extent = drawn.shape
    place = [jax.random.randint(jax.random.fold_in(key, axis), (), 0, extent[axis]) for axis in range(len(extent))]
    drawn = drawn.at[tuple(place)].set(smallest)
    longest = extent.index(max(extent))
    place[longest] = (place[longest] + 1) % extent[longest]
    return drawn.at[tuple(place)].set(largest)


def levels(rng, extent, pieces, low, top_value):
    def one(dim, shards_of):
        heights = jax.random.uniform(jax.random.fold_in(jax.random.fold_in(rng, 6), dim), (shards_of,), jnp.float32, low / len(pieces), top_value / len(pieces))
        return jnp.repeat(jnp.exp(heights), extent[dim] // shards_of).reshape((-1,) + (1,) * (len(extent) - dim - 1))

    factor_of = one(*pieces[0])
    for cut in pieces[1:]:
        factor_of = factor_of * one(*cut)
    return factor_of


def routed_block(own_key, own, number, rows, amount, top, most, lean):
    ranking = jax.random.permutation(own_key, amount)
    packed, usual = load_shares(amount, rows * top, most, lean, True), load_shares(amount, rows * top, most, lean, False)
    places = jnp.arange(amount)

    def named(sizes, rotation):
        used = int((sizes > 0).sum())
        fixed = max(1, used // 4)
        passed = fixed + (places - fixed + rotation * (used - fixed)) % max(1, amount - fixed)
        return jnp.zeros((amount,), jnp.int32).at[ranking[jnp.where(places < fixed, places, passed)]].set(jnp.asarray(sizes, jnp.int32))

    sizes = jnp.where(number % 4 == 0, named(packed, number // 4), named(usual, number - number // 4 - 1))
    mixed = jax.random.permutation(jax.random.fold_in(own, 3), amount)
    donor, taker = mixed[0:amount // 2 * 2:2], mixed[1:amount // 2 * 2:2]
    room = jnp.minimum(sizes[donor] - 1, most - sizes[taker]) // 2
    room = jnp.where((donor == ranking[0]) | (taker == ranking[0]) | (sizes[taker] == 0), 0, jnp.maximum(room, 0))
    passed = jax.random.randint(jax.random.fold_in(own, 4), (amount // 2,), 0, 1 << 20) % (room + 1)
    sizes = sizes.at[donor].add(-passed).at[taker].add(passed)
    items = jnp.searchsorted(jnp.cumsum(sizes), jnp.arange(rows * top), side="right").astype(jnp.int32)
    table = items.reshape(top, rows).T
    table = table[jax.random.permutation(jax.random.fold_in(own, 1), rows)]
    rotation = jax.random.randint(jax.random.fold_in(own, 2), (rows, 1), 0, top)
    return jnp.take_along_axis(table, (jnp.arange(top)[None, :] + rotation) % top, axis=1)


def load_shares(number_of, total, most, skew, full):
    loads = [(1 << 20) // math.isqrt(grade ** skew) + 1 for grade in range(1, number_of + 1)]
    largest = most if full else min(most, max(-(-total // number_of), total * loads[0] // sum(loads)))
    least = 1 if total - largest >= number_of - 1 else 0
    given, surplus = [largest] + [least] * (number_of - 1), total - largest - least * (number_of - 1)
    while surplus > 0:
        movable = [i for i in range(1, number_of) if given[i] < largest] or [i for i in range(1, number_of) if given[i] < most]
        mass, remaining = sum([loads[i] for i in movable]), surplus
        for i in movable:
            more = min(most - given[i], max(1, remaining * loads[i] // mass), surplus)
            given[i] = given[i] + more
            surplus = surplus - more
    return np.array(given)


def centred(stream_key, dims, scale, reach, cuts=(), kind=jnp.bfloat16):
    factor_of = levels(stream_key, dims, cuts, -0.22, 0.18) if cuts else 1.0
    array = jax.random.normal(stream_key, dims, jnp.float32) * scale * factor_of
    return jnp.minimum(jnp.maximum(array, -reach), reach).astype(kind)


def setup_inputs(seed: int = 0) -> dict:
    key_of = jax.random.split(jax.random.key(seed), 18)
    tokens = centred(key_of[0], (TOKENS, D), 1.0, 6.0, ((0, 32),))
    attn_gain = jnp.clip(1.0 + 0.1 * jax.random.normal(key_of[1], (D,), jnp.float32), 0.5, 1.5).astype(jnp.bfloat16)
    query_weight = centred(key_of[2], (D, H * HD), D ** -0.5, 0.15625, ((0, 4),))
    key_weight = centred(key_of[3], (D, H * HD), D ** -0.5, 0.15625, ((0, 4),))
    value_weight = centred(key_of[4], (D, H * HD), D ** -0.5, 0.15625, ((0, 4),))
    out_weight = centred(key_of[5], (H * HD, D), (max(4 * H * HD // SEQ, 1)) ** -0.5, 2.5, ((0, 4),))
    ffn_gain = jnp.clip(1.0 + 0.1 * jax.random.normal(key_of[6], (D,), jnp.float32), 0.5, 1.5).astype(jnp.bfloat16)
    router_weight = centred(key_of[7], (D, EXPERTS), (4 * D) ** -0.5, 0.078125, ((0, 4),))
    shared_gate = centred(key_of[8], (D, FF), D ** -0.5, 0.15625, ((0, 4),))
    shared_up = centred(key_of[9], (D, FF), D ** -0.5, 0.15625, ((0, 4),))
    shared_down = centred(key_of[10], (FF, D), FF ** -0.5, 0.1875, ((0, 4),))
    expert_gate = centred(key_of[11], (EXPERTS, D, FF), D ** -0.5, 0.15625, ((0, 8), (2, 4)))
    expert_up = centred(key_of[12], (EXPERTS, D, FF), D ** -0.5, 0.15625, ((0, 8), (2, 4)))
    expert_down = centred(key_of[13], (EXPERTS, FF, D), (max(FF // 16, 1)) ** -0.5, 0.75, ((0, 8), (1, 4)))
    routes_keys = jax.random.split(jax.random.fold_in(key_of[14], 1), TOKENS // TOK_DEV)
    routes_turns = jax.random.permutation(jax.random.fold_in(key_of[14], 3), TOKENS // TOK_DEV)
    routes = jax.vmap(lambda own, number: routed_block(jax.random.fold_in(key_of[14], 2), own, number, TOK_DEV, EXPERTS, TOP, CAP, 1))(routes_keys, routes_turns).reshape((TOKENS, TOP))
    keep_mask = place_ends((jax.random.randint(key_of[15], (TOKENS, TOP), 0, 8) < 7).astype(jnp.int32), jax.random.fold_in(key_of[15], 1), 0, 1)
    cotangent = centred(key_of[16], (TOKENS, D), 1.0, 6.0, ((0, 32),))
    return dict(tokens=tokens, attn_gain=attn_gain, query_weight=query_weight, key_weight=key_weight, value_weight=value_weight, out_weight=out_weight, ffn_gain=ffn_gain, router_weight=router_weight, shared_gate=shared_gate, shared_up=shared_up, shared_down=shared_down, expert_gate=expert_gate, expert_up=expert_up, expert_down=expert_down, routes=routes, keep_mask=keep_mask, cotangent=cotangent)


@jax.custom_vjp
def low(v):
    return lax.optimization_barrier(v.astype(jnp.bfloat16)).astype(jnp.float32)

@jax.custom_vjp
def low_back(v):
    return v

def low_keep(v):
    return (low(v), None)

def low_pass(kept, grad):
    return (grad,)

def back_keep(v):
    return (v, None)

def back_low(kept, grad):
    return (low(grad),)
low.defvjp(low_keep, low_pass)
low_back.defvjp(back_keep, back_low)
epsilon = 1e-06
highest = lax.Precision.HIGHEST

def matmul(left, right):
    return jnp.dot(left, right, precision=highest, preferred_element_type=jnp.float32)

def rms_scale(values, gain_vec):
    return values * lax.rsqrt(lax.optimization_barrier(jnp.mean(values * values, axis=-1, keepdims=True)) + epsilon) * gain_vec

def half_turn(values):
    middle_at = values.shape[-1] // 2
    return jnp.concatenate([-values[..., middle_at:], values[..., :middle_at]], axis=-1)

def rotary_tables(positions, head_size):
    exponent = jnp.arange(head_size // 2, dtype=jnp.float32) * (2.0 / head_size)
    theta = positions.astype(jnp.float32)[:, None] * jnp.power(10000.0, -exponent)[None, :]
    theta = jnp.concatenate([theta, theta], axis=-1)
    return (jnp.cos(theta)[:, None, :], jnp.sin(theta)[:, None, :])

def rotate(values, cosine, sine):
    return values * cosine + half_turn(values) * sine

def attend(block):
    query, keys, values = block
    raw_scores = low_back(jnp.einsum('qhd,khd->hqk', query, keys, precision=highest))
    position = jnp.arange(SEQ, dtype=jnp.int32)
    allowed = position[None, :] <= position[:, None]
    scores = jnp.where(allowed[None], raw_scores * HD ** (-0.5), -1e+30)
    soft_weights = jax.nn.softmax(scores, axis=-1)
    return jnp.einsum('hqk,khd->qhd', low(soft_weights), values, precision=highest)

def pair_table(routes):
    flat_routes = routes.reshape(-1)
    pair_total = flat_routes.shape[0]
    order = jnp.argsort(flat_routes, stable=True).astype(jnp.int32)
    hits = lax.optimization_barrier(jnp.sum((flat_routes[:, None] == jnp.arange(EXPERTS, dtype=jnp.int32)[None, :]).astype(jnp.int32), axis=0))
    starts = jnp.cumsum(hits) - hits
    rank = jnp.arange(TOKENS // TOK_DEV * CAP, dtype=jnp.int32)
    where_at = jnp.minimum(starts[:, None] + rank[None, :], pair_total - 1)
    return jnp.where(rank[None, :] < hits[:, None], order[where_at], pair_total).astype(jnp.int32)

def widen(values):
    return values.astype(jnp.float32)

def reference(tokens, attn_gain, query_weight, key_weight, value_weight, out_weight, ffn_gain, router_weight, shared_gate, shared_up, shared_down, expert_gate, expert_up, expert_down, routes, keep_mask, cotangent):
    table = pair_table(routes)
    kept = keep_mask.astype(jnp.float32)
    cosine, sine = rotary_tables(jnp.tile(jnp.arange(SEQ, dtype=jnp.int32), TOKENS // SEQ), HD)

    def forward(x_in, gain_one, w_query, w_key, w_value, w_out, gain_two, w_router, s_gate, s_up, s_down, e_gate, e_up, e_down):
        first_in = low(rms_scale(x_in, gain_one))
        query = low(rotate(low_back(matmul(first_in, w_query)).reshape(TOKENS, H, HD), cosine, sine))
        keys = low(rotate(low_back(matmul(first_in, w_key)).reshape(TOKENS, H, HD), cosine, sine))
        values = low(low_back(matmul(first_in, w_value))).reshape(TOKENS, H, HD)
        seq_count = TOKENS // SEQ
        mixed = lax.map(jax.checkpoint(attend), (query.reshape(seq_count, SEQ, H, HD), keys.reshape(seq_count, SEQ, H, HD), values.reshape(seq_count, SEQ, H, HD)))
        mixed = low(low_back(mixed.reshape(TOKENS, H * HD)))
        middle = x_in + low_back(matmul(mixed, w_out))
        second_in = low(rms_scale(middle, gain_two))
        logits = low_back(matmul(second_in, w_router))
        chosen = jnp.take_along_axis(logits, routes, axis=1)
        pair_weight = jax.nn.softmax(chosen, axis=-1) * kept
        shared_act = low(jax.nn.silu(low_back(matmul(second_in, s_gate))) * low_back(matmul(second_in, s_up)))
        shared_res = low_back(matmul(shared_act, s_down))
        padded = jnp.concatenate([second_in, jnp.zeros((1, D), second_in.dtype)], axis=0)

        def run(item):
            gate_w, up_w, down_w, pair_ids = item
            rows_in = low_back(padded[pair_ids // TOP])
            hidden = low(jax.nn.silu(low_back(matmul(rows_in, gate_w))) * low_back(matmul(rows_in, up_w)))
            return low_back(low(matmul(hidden, down_w)))
        outputs = lax.map(jax.checkpoint(run), (e_gate, e_up, e_down, table))
        weight_pad = jnp.concatenate([pair_weight.reshape(-1), jnp.zeros((1,), pair_weight.dtype)], axis=0)
        routed = jnp.zeros((TOKENS + 1, D), outputs.dtype).at[table // TOP].add(weight_pad[table][:, :, None] * outputs)
        return middle + shared_res + routed[:TOKENS]
    result, pullback = jax.vjp(forward, widen(tokens), widen(attn_gain), widen(query_weight), widen(key_weight), widen(value_weight), widen(out_weight), widen(ffn_gain), widen(router_weight), widen(shared_gate), widen(shared_up), widen(shared_down), widen(expert_gate), widen(expert_up), widen(expert_down))
    grads = pullback(cotangent.astype(jnp.float32))
    counts = lax.optimization_barrier(jnp.sum(jnp.where(routes[:, :, None] == jnp.arange(EXPERTS, dtype=jnp.int32)[None, None, :], keep_mask[:, :, None], 0), axis=(0, 1))).astype(jnp.int32)
    return (result.astype(jnp.bfloat16), grads[0], grads[1], grads[2], grads[3], grads[4], grads[5], grads[6], grads[7], grads[8], grads[9], grads[10], grads[11], grads[12], grads[13], counts)
```

```python
import functools

import jax
import jax.numpy as jnp
from jax import lax
from jax.experimental import pallas as pl
from jax.experimental.pallas import tpu as pltpu
from jax.sharding import PartitionSpec as P

H = 10
HD = 128
LANES = 128
BF = jnp.bfloat16
F32 = jnp.float32
epsilon = 1e-06
MIB = 1 << 20


def dot(left, right, over=(1, 0)):
    return lax.dot_general(
        left, right, (((over[0],), (over[1],)), ((), ())), preferred_element_type=F32
    )


def swap_core(v):
    return lax.ppermute(v, "hp", [(i, i ^ 1) for i in range(4)])


def swap_y(v):
    return lax.ppermute(v, "hp", [(i, i ^ 2) for i in range(4)])


def swap_pair(v):
    n = lax.axis_size("ep")
    return lax.ppermute(v, "ep", [(i, i ^ 1) for i in range(n)])


def ring(v):
    n = lax.axis_size("ep")
    return lax.ppermute(v, "ep", [(i, (i + 2) % n) for i in range(n)])


def gather_hp(v):
    far = swap_y(v)
    return [v, swap_core(v), far, swap_core(far)]


def scatter_hp(parts):
    near = swap_core(parts[1].astype(BF)).astype(F32) + parts[0]
    over = swap_core(parts[3].astype(BF)).astype(F32) + parts[2]
    return near + swap_y(over.astype(BF)).astype(F32)


def relative(v, h, axis):
    b = jnp.split(v, 4, axis=axis)
    odd = (h & 1) == 1
    c = [jnp.where(odd, b[i ^ 1], b[i]) for i in range(4)]
    high = (h & 2) == 2
    return jnp.concatenate([jnp.where(high, c[i ^ 2], c[i]) for i in range(4)], axis=axis)


def gather_ep(v):
    stages = lax.axis_size("ep") // 2
    own, out = v, []
    for k in range(stages):
        out.append((own, swap_pair(own)))
        if k < stages - 1:
            own = ring(own)
    return out


def scatter_ep(parts):
    stages = len(parts)
    total = None
    for k in list(range(1, stages)) + [0]:
        here = parts[k][0].astype(F32) + swap_pair(parts[k][1]).astype(F32)
        if total is not None:
            here = here + total.astype(F32)
        total = here if k == 0 else ring(here.astype(BF))
    return total


def sum_ep(v, e):
    n = lax.axis_size("ep")
    stages = n // 2
    x, z = e & 1, e >> 1
    halves = v.reshape(2, v.shape[0] // 2, v.shape[1])
    mine = lax.dynamic_index_in_dim(halves, x, 0, False)
    other = lax.dynamic_index_in_dim(halves, 1 - x, 0, False)
    mine = mine + swap_pair(other.astype(BF)).astype(F32)
    chunks = mine.reshape(stages, mine.shape[0] // stages, mine.shape[1])

    def chunk(back):
        return lax.dynamic_index_in_dim(chunks, (z + stages - back) % stages, 0, False)

    total = chunk(1 % stages)
    for back in list(range(2, stages)) + [0]:
        total = ring(total.astype(BF)).astype(F32) + chunk(back)
    total = total.astype(BF)
    half = jnp.zeros(chunks.shape, BF)
    for back in range(stages):
        half = lax.dynamic_update_index_in_dim(half, total, (z + stages - back) % stages, 0)
        if back < stages - 1:
            total = ring(total)
    half = half.reshape(mine.shape)
    far = swap_pair(half)
    low = jnp.where(x == 0, half, far)
    high = jnp.where(x == 0, far, half)
    return jnp.concatenate([low, high], axis=0).astype(F32)


def sum_all_small(v):
    v = v + swap_core(v)
    v = v + swap_y(v)
    n = lax.axis_size("ep")
    bit = 1
    while bit < n:
        v = v + lax.ppermute(v, "ep", [(i, i ^ bit) for i in range(n)])
        bit *= 2
    return v


def score_mask(h_ref, rows, cols):
    h = h_ref[0]
    at = lax.broadcasted_iota(jnp.int32, (rows, cols), 0) + h * rows
    key = lax.broadcasted_iota(jnp.int32, (rows, cols), 1)
    block = key // rows
    other = jnp.where(
        block == 0, h, jnp.where(block == 1, h ^ 2, jnp.where(block == 2, h ^ 1, h ^ 3))
    )
    return other * rows + key % rows <= at


def attend_kernel(h_ref, q_ref, ka_ref, kb_ref, va_ref, vb_ref, o_ref, lse_ref):
    rows = q_ref.shape[0]
    half = ka_ref.shape[0]
    q = q_ref[...]
    s = jnp.concatenate([dot(q, ka_ref[...], (1, 1)), dot(q, kb_ref[...], (1, 1))], axis=1)
    s = jnp.where(score_mask(h_ref, rows, 2 * half), s * HD ** (-0.5), -1e30)
    top = jnp.max(s, axis=1, keepdims=True)
    p = jnp.exp(s - top)
    total = jnp.sum(p, axis=1, keepdims=True)
    p = (p * (1.0 / total)).astype(BF)
    o = dot(p[:, :half], va_ref[...]) + dot(p[:, half:], vb_ref[...])
    o_ref[...] = o.astype(BF)
    lse_ref[...] = jnp.broadcast_to(top + jnp.log(total), lse_ref.shape)


def attend_back_kernel(
    h_ref,
    q_ref,
    ka_ref,
    kb_ref,
    va_ref,
    vb_ref,
    d_ref,
    lse_ref,
    dq_ref,
    dka_ref,
    dva_ref,
    dkb_ref,
    dvb_ref,
):
    rows = q_ref.shape[0]
    half = ka_ref.shape[0]
    q, d = q_ref[...], d_ref[...]
    s = jnp.concatenate([dot(q, ka_ref[...], (1, 1)), dot(q, kb_ref[...], (1, 1))], axis=1)
    s = jnp.where(score_mask(h_ref, rows, 2 * half), s * HD ** (-0.5), -1e30)
    p = jnp.exp(s - lse_ref[:, 0:1])
    back = jnp.concatenate([dot(d, va_ref[...], (1, 1)), dot(d, vb_ref[...], (1, 1))], axis=1)
    inner = jnp.sum(p * back, axis=1, keepdims=True)
    sb = (p * (back - inner) * HD ** (-0.5)).astype(BF)
    p = p.astype(BF)
    dq_ref[...] = dot(sb[:, :half], ka_ref[...]) + dot(sb[:, half:], kb_ref[...])
    dk = dot(sb, q, (0, 0))
    dv = dot(p, d, (0, 0))
    dka_ref[...] = dk[:half]
    dkb_ref[...] = dk[half:].astype(BF)
    dva_ref[...] = dv[:half]
    dvb_ref[...] = dv[half:].astype(BF)


def head_spec(rows, skip=0):
    return pl.BlockSpec((rows, HD), lambda i, h: (0, i + skip))


def attend(h, q, kv_a, kv_b):
    rows, width = q.shape
    half = kv_a.shape[0]
    flops = 4 * rows * 2 * half * width
    return pl.pallas_call(
        attend_kernel,
        grid_spec=pltpu.PrefetchScalarGridSpec(
            num_scalar_prefetch=1,
            grid=(H,),
            in_specs=[
                head_spec(rows),
                head_spec(half),
                head_spec(half),
                head_spec(half, H),
                head_spec(half, H),
            ],
            out_specs=[head_spec(rows), head_spec(rows)],
        ),
        out_shape=[
            jax.ShapeDtypeStruct((rows, width), BF),
            jax.ShapeDtypeStruct((rows, width), F32),
        ],
        compiler_params=pltpu.CompilerParams(vmem_limit_bytes=40 * MIB),
        cost_estimate=pl.CostEstimate(
            flops=flops, bytes_accessed=8 * MIB, transcendentals=rows * 2 * half * H
        ),
    )(h, q, kv_a, kv_b, kv_a, kv_b)


def attend_back(h, q, kv_a, kv_b, d, lse):
    rows, width = q.shape
    half = kv_a.shape[0]
    flops = 10 * rows * 2 * half * width
    return pl.pallas_call(
        attend_back_kernel,
        grid_spec=pltpu.PrefetchScalarGridSpec(
            num_scalar_prefetch=1,
            grid=(H,),
            in_specs=[
                head_spec(rows),
                head_spec(half),
                head_spec(half),
                head_spec(half, H),
                head_spec(half, H),
                head_spec(rows),
                head_spec(rows),
            ],
            out_specs=[head_spec(rows)] + [head_spec(half)] * 4,
        ),
        out_shape=[
            jax.ShapeDtypeStruct((rows, width), F32),
            jax.ShapeDtypeStruct((half, width), F32),
            jax.ShapeDtypeStruct((half, width), F32),
            jax.ShapeDtypeStruct((half, width), BF),
            jax.ShapeDtypeStruct((half, width), BF),
        ],
        compiler_params=pltpu.CompilerParams(vmem_limit_bytes=40 * MIB),
        cost_estimate=pl.CostEstimate(
            flops=flops, bytes_accessed=16 * MIB, transcendentals=rows * 2 * half * H
        ),
    )(h, q, kv_a, kv_b, kv_a, kv_b, d, lse)


def pick_matrix(meta, col, capacity):
    lane = lax.broadcasted_iota(jnp.int32, meta.shape, 1)
    code = jnp.sum(jnp.where(lane == col, meta.astype(F32), 0.0), axis=1, keepdims=True)
    place = lax.broadcasted_iota(jnp.int32, (meta.shape[0], capacity), 1).astype(F32)
    return jnp.where(code == place, 1.0, 0.0).astype(BF)


def expert_kernel(capacity, total, olds, e_ref, x0_ref, x1_ref, g0_ref, g1_ref, *refs):
    gates, ups, downs = refs[0:4], refs[4:8], refs[8:12]
    sg_ref, su_ref, sd_ref, sgg_old, sdg_old = refs[12:17]
    (
        dx0_ref,
        dx1_ref,
        sgg_ref,
        sdg_ref,
        sa_ref,
        xr_ref,
        gr_ref,
        gi_ref,
        ui_ref,
        wa_ref,
    ) = refs[17 + olds :]
    xs, gs, dxs = (x0_ref, x1_ref), (g0_ref, g1_ref), (dx0_ref, dx1_ref)
    width = sg_ref.shape[0]
    tokens = x0_ref.shape[0]
    c = capacity
    x2 = jnp.concatenate([r[:, :width] for r in xs], axis=0)
    g2 = jnp.concatenate([r[:, :width] for r in gs], axis=0)
    hg, hu = dot(x2, sg_ref[...]), dot(x2, su_ref[...])
    ab = dot(g2, sd_ref[...], (1, 1))
    s = jax.nn.sigmoid(hg)
    silu = hg * s
    act = (silu * hu).astype(BF)
    gi = (ab * hu * (s * (1.0 + hg * (1.0 - s)))).astype(BF)
    ui = (ab * silu).astype(BF)
    sa_ref[0] = act
    gu = jnp.concatenate([gi, ui], axis=1)
    sgg_ref[...] = sgg_old[...] + dot(x2, gu, (0, 0))
    sdg_ref[...] = sdg_old[...] + dot(act, g2, (0, 0))
    dx = dot(gi, sg_ref[...], (1, 1)) + dot(ui, su_ref[...], (1, 1))
    totals = [dx[:tokens], dx[tokens:]]
    metas = [0.0, 0.0]
    lane = lax.broadcasted_iota(jnp.int32, (2 * c, LANES), 1)
    for x in range(2):
        col = 2 * e_ref[0] + x
        picks, weights = [], []
        for j in range(2):
            pick = pick_matrix(gs[j][:, width:], col, c)
            picks.append(pick)
            rows = dot(pick, xs[j][...], (0, 0))
            xr_ref[x, 0, j * c : (j + 1) * c, :] = rows[:, :width].astype(BF)
            weights.append(rows[:, width:])
            gr_ref[x, 0, j * c : (j + 1) * c, :] = dot(pick, gs[j][:, :width], (0, 0)).astype(BF)
        w = jnp.concatenate(weights, axis=0)
        w = jnp.sum(jnp.where(lane == col, w, 0.0), axis=1, keepdims=True)
        xr, gr = xr_ref[x, 0], gr_ref[x, 0]
        dxr = jnp.zeros((2 * c, width), F32)
        wb = jnp.zeros((2 * c, 1), F32)
        for r in range(4):
            wg, wu, wd = gates[r][x], ups[r][x], downs[r][x]
            hg, hu = dot(xr, wg), dot(xr, wu)
            ab = dot(gr, wd, (1, 1))
            s = jax.nn.sigmoid(hg)
            silu = hg * s
            act = silu * hu
            wb = wb + jnp.sum(act * ab, axis=1, keepdims=True)
            ab = ab * w
            gi = (ab * hu * (s * (1.0 + hg * (1.0 - s)))).astype(BF)
            ui = (ab * silu).astype(BF)
            gi_ref[r, x, 0] = gi
            ui_ref[r, x, 0] = ui
            wa_ref[r, x, 0] = (act * w).astype(BF)
            dxr = dxr + dot(gi, wg, (1, 1)) + dot(ui, wu, (1, 1))
        dxr = dxr.astype(BF)
        high = wb.astype(BF).astype(F32)
        meta = jnp.where(lane == col, high, 0.0) + jnp.where(lane == total + col, wb - high, 0.0)
        meta = meta.astype(BF)
        for j in range(2):
            span = slice(j * c, (j + 1) * c)
            totals[j] = totals[j] + dot(picks[j], dxr[span])
            metas[j] = metas[j] + dot(picks[j], meta[span])
    for j in range(2):
        dxs[j][:, :width] = totals[j].astype(BF)
        dxs[j][:, width:] = metas[j].astype(BF)


def expert_out_kernel(capacity, e_ref, g0_ref, g1_ref, wa_ref, sa_ref, *refs):
    downs, sd_ref, outs = refs[0:4], refs[4], refs[5:7]
    width = sd_ref.shape[1]
    tokens = g0_ref.shape[0]
    c = capacity
    gs = (g0_ref, g1_ref)
    shared = dot(sa_ref[0], sd_ref[...])
    totals = [shared[:tokens], shared[tokens:]]
    for x in range(2):
        rows = jnp.zeros((2 * c, width), F32)
        for r in range(4):
            rows = rows + dot(wa_ref[r, x, 0], downs[r][x])
        rows = rows.astype(BF)
        for j in range(2):
            pick = pick_matrix(gs[j][...], 2 * e_ref[0] + x, c)
            totals[j] = totals[j] + dot(pick, rows[j * c : (j + 1) * c])
    for j in range(2):
        outs[j][...] = totals[j].astype(BF)


def whole(shape):
    return pl.BlockSpec(shape, lambda i, e: (0,) * len(shape), pipeline_mode=pl.Buffered(1))


def expert_stage(
    k, stages, capacity, total, e, x_pair, g_pair, gates, ups, downs, sg, su, sd, carry, bufs
):
    tokens, wide = x_pair[0].shape
    width = sg.shape[0]
    hidden = gates[0].shape[2]
    c2 = 2 * capacity
    shared = sg.shape[1]
    olds = 0 if bufs is None else 6
    shapes = [
        ((stages, 2 * tokens, shared), (1, 2 * tokens, shared), (k, 0, 0)),
        ((2, stages, c2, width), (2, 1, c2, width), (0, k, 0, 0)),
        ((2, stages, c2, width), (2, 1, c2, width), (0, k, 0, 0)),
        ((4, 2, stages, c2, hidden), (4, 2, 1, c2, hidden), (0, 0, k, 0, 0)),
        ((4, 2, stages, c2, hidden), (4, 2, 1, c2, hidden), (0, 0, k, 0, 0)),
        ((4, 2, stages, c2, hidden), (4, 2, 1, c2, hidden), (0, 0, k, 0, 0)),
    ]

    def at(block, where):
        return pl.BlockSpec(block, lambda i, e: where)

    ins = [e, *x_pair, *g_pair, *gates, *ups, *downs, sg, su, sd, *carry]
    in_specs = [whole(v.shape) for v in ins[1:]]
    alias = {}
    if bufs is not None:
        for n, b in enumerate(bufs):
            alias[len(ins)] = 4 + n
            ins.append(b)
            in_specs.append(pl.BlockSpec(memory_space=pl.ANY))
    out_shape = [jax.ShapeDtypeStruct((tokens, wide), BF)] * 2 + [
        jax.ShapeDtypeStruct(v.shape, v.dtype) for v in carry
    ]
    out_specs = [whole((tokens, wide))] * 2 + [whole(v.shape) for v in carry]
    for full, block, where in shapes:
        out_shape.append(jax.ShapeDtypeStruct(full, BF))
        out_specs.append(at(block, where))
    outs = pl.pallas_call(
        functools.partial(expert_kernel, capacity, total, olds),
        grid_spec=pltpu.PrefetchScalarGridSpec(
            num_scalar_prefetch=1, grid=(1,), in_specs=in_specs, out_specs=out_specs
        ),
        out_shape=out_shape,
        input_output_aliases=alias,
        compiler_params=pltpu.CompilerParams(vmem_limit_bytes=60 * MIB),
        cost_estimate=pl.CostEstimate(
            flops=20 * c2 * width * 4 * hidden, bytes_accessed=24 * MIB, transcendentals=c2 * 8 * hidden
        ),
    )(*ins)
    return outs[0:2], outs[2:4], outs[4:]


def expert_out(k, capacity, e, g_pair, wa, sa, downs, sd):
    tokens = g_pair[0].shape[0]
    width = sd.shape[1]
    c2 = wa.shape[3]
    last = g_pair[0].shape[1] // LANES - 1
    meta = pl.BlockSpec((tokens, LANES), lambda i, e: (0, last))
    return pl.pallas_call(
        functools.partial(expert_out_kernel, capacity),
        grid_spec=pltpu.PrefetchScalarGridSpec(
            num_scalar_prefetch=1,
            grid=(1,),
            in_specs=[
                meta,
                meta,
                pl.BlockSpec((4, 2, 1, c2, wa.shape[4]), lambda i, e: (0, 0, k, 0, 0)),
                pl.BlockSpec((1,) + sa.shape[1:], lambda i, e: (k, 0, 0)),
            ]
            + [whole(d.shape) for d in downs]
            + [whole(sd.shape)],
            out_specs=[whole((tokens, width))] * 2,
        ),
        out_shape=[jax.ShapeDtypeStruct((tokens, width), BF)] * 2,
        compiler_params=pltpu.CompilerParams(vmem_limit_bytes=40 * MIB),
        cost_estimate=pl.CostEstimate(
            flops=4 * c2 * width * 4 * wa.shape[4], bytes_accessed=10 * MIB, transcendentals=0
        ),
    )(e, *g_pair, wa, sa, *downs, sd)


def rms(values):
    return lax.rsqrt(jnp.mean(values * values, axis=-1, keepdims=True) + epsilon)


def norm_back(values, inv, gain, upstream):
    weighted = upstream * gain
    inner = jnp.mean(weighted * values, axis=-1, keepdims=True)
    to_input = weighted * inv - values * (inv * inv * inv * inner)
    return to_input, jnp.sum(upstream * values * inv, axis=0)


def half_turn(v):
    lane = lax.broadcasted_iota(jnp.int32, v.shape, 1)
    return jnp.where(
        lane % HD < HD // 2, -jnp.roll(v, -HD // 2, axis=1), jnp.roll(v, HD // 2, axis=1)
    )


def rotary_tables(positions):
    exponent = jnp.arange(HD // 2, dtype=F32) * (2.0 / HD)
    theta = positions.astype(F32)[:, None] * jnp.power(10000.0, -exponent)[None, :]
    theta = jnp.concatenate([theta, theta], axis=-1)
    return jnp.tile(jnp.cos(theta), (1, H)), jnp.tile(jnp.sin(theta), (1, H))


def per_device(
    tokens,
    attn_gain,
    query_weight,
    key_weight,
    value_weight,
    out_weight,
    ffn_gain,
    router_weight,
    shared_gate,
    shared_up,
    shared_down,
    expert_gate,
    expert_up,
    expert_down,
    routes,
    keep_mask,
    cotangent,
):
    e, h = lax.axis_index("ep"), lax.axis_index("hp")
    ep = lax.axis_size("ep")
    stages = ep // 2
    rows, width = tokens.shape
    top = routes.shape[1]
    total = router_weight.shape[1]
    capacity = -(-(5 * rows * top // (4 * total)) // 16) * 16
    e_arr, h_arr = jnp.full((1,), e, jnp.int32), jnp.full((1,), h, jnp.int32)

    far_tokens = swap_y(tokens)
    k_w, v_w = gather_hp(key_weight), gather_hp(value_weight)
    q_w = gather_hp(query_weight)
    o_w = gather_hp(out_weight)
    gates, ups, downs = gather_hp(expert_gate), gather_hp(expert_up), gather_hp(expert_down)
    units = shared_down.shape[0] // ep
    tiny = [attn_gain[:, None], ffn_gain[:, None], router_weight]
    small = jnp.concatenate(tiny + [jnp.zeros((width // 4, LANES - 2 - total), BF)], axis=1)

    def mine(v):
        v = v.reshape(width // 4, 4, -1)
        v = lax.dynamic_slice_in_dim(v, e * units, units, axis=2).reshape(width // 4, 4 * units)
        return jnp.pad(v, ((0, 0), (0, LANES - 4 * units)))

    small = jnp.concatenate([small, mine(shared_gate), mine(shared_up)], axis=1)
    small = jnp.concatenate(gather_hp(small), axis=0)
    gain_one = small[:, 0].astype(F32)[None, :]
    small = relative(small, h, 0)
    gain_two = small[:, 1].astype(F32)[None, :]
    router = small[:, 2 : 2 + total]
    sg, su = small[:, LANES : 2 * LANES], small[:, 2 * LANES :]
    sd = lax.dynamic_slice_in_dim(shared_down, e * units, units, axis=0)
    sd = relative(jnp.concatenate(gather_hp(sd), axis=0), h, 0)
    sd = jnp.pad(sd, ((0, LANES - 4 * units), (0, 0)))

    expert = jnp.arange(total, dtype=jnp.int32)
    hit_each = routes[:, :, None] == expert[None, None, :]
    hit = jnp.any(hit_each, axis=1)
    kept = jnp.sum(jnp.where(hit_each, keep_mask[:, :, None], 0), axis=1)
    below = (jnp.arange(rows)[:, None] > jnp.arange(rows)[None, :]).astype(BF)
    place = jnp.where(hit, dot(below, hit.astype(BF)), -1.0)
    kept = kept.astype(F32)
    g_ext = jnp.concatenate(
        [
            cotangent,
            place.astype(BF),
            jnp.zeros((rows, LANES - total), BF),
        ],
        axis=1,
    )
    g_blocks = gather_ep(g_ext)

    pos = jnp.arange(rows, dtype=jnp.int32)
    pos = jnp.concatenate([h * rows + pos, (h ^ 2) * rows + pos])
    cosine, sine = rotary_tables(pos)
    residual = tokens.astype(F32)
    both = relative(jnp.concatenate([tokens, far_tokens], axis=0), h, 1).astype(F32)
    inv_one = rms(both)
    first_in = (both * inv_one * gain_one).astype(BF)

    def rotate(v, n):
        return v * cosine[:n] + half_turn(v) * sine[:n]

    def rotate_back(v, n):
        return v * cosine[:n] - half_turn(v * sine[:n])

    k_w, v_w = jnp.concatenate(k_w, axis=0), jnp.concatenate(v_w, axis=0)
    q_w, o_w = jnp.concatenate(q_w, axis=0), jnp.concatenate(o_w, axis=0)
    keys = rotate(dot(first_in, k_w), 2 * rows).astype(BF)
    values = dot(first_in, v_w).astype(BF)
    kv_a = jnp.concatenate([keys, values], axis=1)
    kv_b = swap_core(kv_a)
    query = rotate(dot(first_in[:rows], q_w), rows).astype(BF)
    mixed, lse = attend(h_arr, query, kv_a, kv_b)
    mixed_rel = relative(mixed, h, 1)
    middle = residual + dot(mixed_rel, o_w)
    inv_two = rms(middle)
    second_in = (middle * inv_two * gain_two).astype(BF)

    logits = jnp.where(hit, dot(second_in, router), -1e30)
    gates_of = jnp.where(hit, jnp.exp(logits - jnp.max(logits, axis=1, keepdims=True)), 0.0)
    gates_of = gates_of / jnp.sum(gates_of, axis=1, keepdims=True)
    pair_weight = gates_of * kept
    x_ext = jnp.concatenate(
        [second_in, pair_weight.astype(BF), jnp.zeros((rows, LANES - total), BF)], axis=1
    )

    x_blocks = gather_ep(x_ext)
    carry = (jnp.zeros((width, 2 * LANES), F32), jnp.zeros((LANES, width), F32))
    bufs, dx_parts = None, []
    for k in range(stages):
        dx, carry, bufs = expert_stage(
            k,
            stages,
            capacity,
            total,
            e_arr,
            x_blocks[k],
            g_blocks[k],
            gates,
            ups,
            downs,
            sg,
            su,
            sd,
            carry,
            bufs,
        )
        dx_parts.append(dx)
    dx_sum = scatter_ep(dx_parts)
    sa, xr, gr, gi, ui, wa = bufs
    out_parts = [
        expert_out(k, capacity, e_arr, g_blocks[k], wa, sa, downs, sd) for k in range(stages)
    ]
    layer = (middle + scatter_ep(out_parts)).astype(BF)

    flat = (2, stages * 2 * capacity)
    xr, gr = xr.reshape(flat + (width,)), gr.reshape(flat + (width,))
    gi, ui, wa = (v.reshape((4,) + flat + (v.shape[-1],)) for v in (gi, ui, wa))

    def expert_grad(spec, left, right):
        return jnp.einsum(spec, left, right, preferred_element_type=F32)

    gate_grad = scatter_hp([expert_grad("xnd,xnf->xdf", xr, gi[r]) for r in range(4)])
    up_grad = scatter_hp([expert_grad("xnd,xnf->xdf", xr, ui[r]) for r in range(4)])
    down_grad = scatter_hp([expert_grad("xnf,xnd->xfd", wa[r], gr) for r in range(4)])

    sgg, sdg = carry
    sgg = relative(sgg, h, 0)
    sgg = scatter_hp(jnp.split(sgg, 4, axis=0)).astype(BF)
    sdg = scatter_hp(jnp.split(relative(sdg[: 4 * units], h, 0), 4, axis=0)).astype(BF)
    sgg = lax.all_gather(sgg, "ep", axis=0, tiled=False)
    sdg = lax.all_gather(sdg, "ep", axis=0, tiled=True)

    def spread(v):
        v = v[:, :, : 4 * units].reshape(ep, width // 4, 4, units)
        return v.transpose(1, 2, 0, 3).reshape(width // 4, 4 * ep * units).astype(F32)

    sgate_grad, sup_grad = spread(sgg[:, :, :LANES]), spread(sgg[:, :, LANES:])
    sdown_grad = sdg.astype(F32)

    grad_out = cotangent.astype(F32)
    weight_back = dx_sum[:, width : width + total] + dx_sum[:, width + total : width + 2 * total]
    gate_back = weight_back * kept
    chosen_back = gates_of * (gate_back - jnp.sum(gates_of * gate_back, axis=1, keepdims=True))
    logits_back = chosen_back.astype(BF)
    router_part = dot(logits_back, second_in, (0, 0))
    second_back = dx_sum[:, :width] + dot(logits_back, router, (1, 1))
    to_middle, gain_two_part = norm_back(middle, inv_two, gain_two, second_back)
    middle_back = grad_out + to_middle
    attn_back = middle_back.astype(BF)
    counts_part = jnp.sum(kept, axis=0)
    tail = jnp.zeros((1, width - total), F32)
    sums = jnp.concatenate(
        [
            router_part,
            gain_two_part[None, :],
            jnp.concatenate([counts_part[None, :], tail], axis=1),
        ],
        axis=0,
    )
    sums = sum_all_small(sums)

    mixed_back = relative(dot(attn_back, o_w, (1, 1)).astype(BF), h, 1)
    out_part = dot(mixed_rel, attn_back, (0, 0))
    out_grad = sum_ep(scatter_hp(jnp.split(out_part, 4, axis=0)), e)
    dq, dka, dva, dkb, dvb = attend_back(h_arr, query, kv_a, kv_b, mixed_back, lse)
    dk = dka + swap_core(dkb).astype(F32)
    dv = dva + swap_core(dvb).astype(F32)
    query_raw = rotate_back(dq, rows).astype(BF)
    key_raw = rotate_back(dk, 2 * rows).astype(BF)
    value_raw = dv.astype(BF)
    kv_back = dot(key_raw, k_w, (1, 1)) + dot(value_raw, v_w, (1, 1))
    from_far = swap_y(kv_back[rows:].astype(BF))
    q_part = dot(first_in[:rows], query_raw, (0, 0))
    k_part = dot(first_in, key_raw, (0, 0))
    v_part = dot(first_in, value_raw, (0, 0))
    query_grad, key_grad, value_grad = (
        sum_ep(scatter_hp(jnp.split(v, 4, axis=0)), e) for v in (q_part, k_part, v_part)
    )
    first_back = dot(query_raw, q_w, (1, 1)) + kv_back[:rows]
    quarters = jnp.split(from_far.astype(F32), 4, axis=1)
    first_back = first_back + jnp.concatenate([quarters[i ^ 2] for i in range(4)], axis=1)
    to_tokens, gain_one_part = norm_back(both[:rows], inv_one[:rows], gain_one, first_back)
    tokens_grad = middle_back + relative(to_tokens, h, 1)
    gain_one_grad = sum_all_small(relative(gain_one_part[None, :], h, 1))[0]

    def own(v, n):
        return lax.dynamic_slice_in_dim(v, h * n, n, axis=0)

    return (
        layer,
        tokens_grad,
        own(gain_one_grad, width // 4),
        query_grad,
        key_grad,
        value_grad,
        out_grad,
        own(sums[total], width // 4),
        own(sums[:total].T, width // 4),
        sgate_grad,
        sup_grad,
        sdown_grad,
        gate_grad,
        up_grad,
        down_grad,
        own(sums[total + 1], total // 4).astype(jnp.int32),
    )


def solution(mesh):
    row, ep_hp = P("hp", None), P(("ep", "hp"), None)
    return jax.shard_map(
        per_device,
        mesh=mesh,
        in_specs=(
            ep_hp,
            P("hp"),
            row,
            row,
            row,
            row,
            P("hp"),
            row,
            row,
            row,
            row,
            P("ep", None, "hp"),
            P("ep", None, "hp"),
            P("ep", "hp", None),
            ep_hp,
            ep_hp,
            ep_hp,
        ),
        out_specs=(
            ep_hp,
            ep_hp,
            P("hp"),
            row,
            row,
            row,
            row,
            P("hp"),
            row,
            row,
            row,
            row,
            P("ep", None, "hp"),
            P("ep", None, "hp"),
            P("ep", "hp", None),
            P("hp"),
        ),
        check_vma=False,
    )
```

```python
import functools

import jax
import jax.numpy as jnp
from jax import lax
from jax.experimental import pallas as pl
from jax.experimental.pallas import tpu as pltpu
from jax.sharding import PartitionSpec as P

H = 10
HD = 128
LANES = 128
BF = jnp.bfloat16
F32 = jnp.float32
epsilon = 1e-06
MIB = 1 << 20


def dot(left, right, over=(1, 0)):
    return lax.dot_general(
        left, right, (((over[0],), (over[1],)), ((), ())), preferred_element_type=F32
    )


def swap_core(v):
    return lax.ppermute(v, "hp", [(i, i ^ 1) for i in range(4)])


def swap_y(v):
    return lax.ppermute(v, "hp", [(i, i ^ 2) for i in range(4)])


def swap_pair(v):
    n = lax.axis_size("ep")
    return lax.ppermute(v, "ep", [(i, i ^ 1) for i in range(n)])


def ring(v):
    n = lax.axis_size("ep")
    return lax.ppermute(v, "ep", [(i, (i + 2) % n) for i in range(n)])


def shift(v, steps):
    n = lax.axis_size("ep")
    return lax.ppermute(v, "ep", [(i, (i + 2 * steps) % n) for i in range(n)])


def after(v, *others):
    return lax.optimization_barrier((v, others))[0]


def gather_hp(v):
    far = swap_y(v)
    return [v, swap_core(v), far, swap_core(far)]


def scatter_hp(parts):
    near = swap_core(parts[1].astype(BF)).astype(F32) + parts[0].astype(F32)
    over = swap_core(parts[3].astype(BF)).astype(F32) + parts[2].astype(F32)
    return near + swap_y(over.astype(BF)).astype(F32)


def relative(v, h, axis):
    b = jnp.split(v, 4, axis=axis)
    odd = (h & 1) == 1
    c = [jnp.where(odd, b[i ^ 1], b[i]) for i in range(4)]
    high = (h & 2) == 2
    return jnp.concatenate([jnp.where(high, c[i ^ 2], c[i]) for i in range(4)], axis=axis)


def gather_ep(v):
    stages = lax.axis_size("ep") // 2
    own, out = v, []
    for k in range(stages):
        out.append((own, swap_pair(own)))
        if k < stages - 1:
            own = ring(own)
    return out


def scatter_ep(parts):
    stages = len(parts)
    total = None
    for k in list(range(1, stages)) + [0]:
        here = parts[k][0].astype(F32) + swap_pair(parts[k][1]).astype(F32)
        if total is not None:
            here = here + total.astype(F32)
        total = here if k == 0 else ring(here.astype(BF))
    return total


def spread_ep(v, e):
    n = lax.axis_size("ep")
    stages = n // 2
    x, z = e & 1, e >> 1
    column = lax.dynamic_update_index_in_dim(jnp.zeros((stages,) + v.shape, v.dtype), v, z, 0)
    for step in range(1, stages):
        column = lax.dynamic_update_index_in_dim(
            column, shift(v, step), (z + stages - step) % stages, 0
        )
    far = swap_pair(column)
    both = [jnp.where(x == 0, column, far), jnp.where(x == 0, far, column)]
    return jnp.stack(both, axis=1).reshape((n,) + v.shape)


def sum_ep(v, e):
    n = lax.axis_size("ep")
    stages = n // 2
    x, z = e & 1, e >> 1
    halves = v.reshape(2, v.shape[0] // 2, v.shape[1])
    mine = lax.dynamic_index_in_dim(halves, x, 0, False)
    other = lax.dynamic_index_in_dim(halves, 1 - x, 0, False)
    mine = mine + swap_pair(other.astype(BF)).astype(F32)
    chunks = mine.reshape(stages, mine.shape[0] // stages, mine.shape[1])
    low = chunks.astype(BF)
    total = lax.dynamic_index_in_dim(chunks, z, 0, False)
    for step in range(1, stages):
        part = lax.dynamic_index_in_dim(low, (z + step) % stages, 0, False)
        total = total + shift(part, step).astype(F32)
    total = total.astype(BF)
    half = lax.dynamic_update_index_in_dim(jnp.zeros(chunks.shape, BF), total, z, 0)
    for step in range(1, stages):
        half = lax.dynamic_update_index_in_dim(
            half, shift(total, step), (z + stages - step) % stages, 0
        )
    half = half.reshape(mine.shape)
    far = swap_pair(half)
    low = jnp.where(x == 0, half, far)
    high = jnp.where(x == 0, far, half)
    return jnp.concatenate([low, high], axis=0).astype(F32)


def sum_all_small(v):
    v = v + swap_core(v)
    v = v + swap_y(v)
    n = lax.axis_size("ep")
    bit = 1
    while bit < n:
        v = v + lax.ppermute(v, "ep", [(i, i ^ bit) for i in range(n)])
        bit *= 2
    return v


def score_mask(h_ref, rows, cols):
    h = h_ref[0]
    at = lax.broadcasted_iota(jnp.int32, (rows, cols), 0) + h * rows
    key = lax.broadcasted_iota(jnp.int32, (rows, cols), 1)
    block = key // rows
    other = jnp.where(
        block == 0, h, jnp.where(block == 1, h ^ 2, jnp.where(block == 2, h ^ 1, h ^ 3))
    )
    return other * rows + key % rows <= at


def attend_kernel(h_ref, q_ref, ka_ref, kb_ref, va_ref, vb_ref, o_ref, lse_ref):
    rows = q_ref.shape[0]
    half = ka_ref.shape[0]
    q = q_ref[...]
    s = jnp.concatenate([dot(q, ka_ref[...], (1, 1)), dot(q, kb_ref[...], (1, 1))], axis=1)
    s = jnp.where(score_mask(h_ref, rows, 2 * half), s * HD ** (-0.5), -1e30)
    top = jnp.max(s, axis=1, keepdims=True)
    p = jnp.exp(s - top)
    total = jnp.sum(p, axis=1, keepdims=True)
    p = (p * (1.0 / total)).astype(BF)
    o = dot(p[:, :half], va_ref[...]) + dot(p[:, half:], vb_ref[...])
    o_ref[...] = o.astype(BF)
    lse_ref[...] = jnp.broadcast_to(top + jnp.log(total), lse_ref.shape)


def attend_back_kernel(
    h_ref,
    q_ref,
    ka_ref,
    kb_ref,
    va_ref,
    vb_ref,
    d_ref,
    lse_ref,
    dq_ref,
    dka_ref,
    dva_ref,
    dkb_ref,
    dvb_ref,
):
    rows = q_ref.shape[0]
    half = ka_ref.shape[0]
    q, d = q_ref[...], d_ref[...]
    s = jnp.concatenate([dot(q, ka_ref[...], (1, 1)), dot(q, kb_ref[...], (1, 1))], axis=1)
    s = jnp.where(score_mask(h_ref, rows, 2 * half), s * HD ** (-0.5), -1e30)
    p = jnp.exp(s - lse_ref[:, 0:1])
    back = jnp.concatenate([dot(d, va_ref[...], (1, 1)), dot(d, vb_ref[...], (1, 1))], axis=1)
    inner = jnp.sum(p * back, axis=1, keepdims=True)
    sb = (p * (back - inner) * HD ** (-0.5)).astype(BF)
    p = p.astype(BF)
    dq_ref[...] = dot(sb[:, :half], ka_ref[...]) + dot(sb[:, half:], kb_ref[...])
    dk = dot(sb, q, (0, 0))
    dv = dot(p, d, (0, 0))
    dka_ref[...] = dk[:half]
    dkb_ref[...] = dk[half:].astype(BF)
    dva_ref[...] = dv[:half]
    dvb_ref[...] = dv[half:].astype(BF)


def head_spec(rows, skip=0):
    return pl.BlockSpec((rows, HD), lambda i, h: (0, i + skip))


def attend(h, q, kv_a, kv_b):
    rows, width = q.shape
    half = kv_a.shape[0]
    flops = 4 * rows * 2 * half * width
    return pl.pallas_call(
        attend_kernel,
        grid_spec=pltpu.PrefetchScalarGridSpec(
            num_scalar_prefetch=1,
            grid=(H,),
            in_specs=[
                head_spec(rows),
                head_spec(half),
                head_spec(half),
                head_spec(half, H),
                head_spec(half, H),
            ],
            out_specs=[head_spec(rows), head_spec(rows)],
        ),
        out_shape=[
            jax.ShapeDtypeStruct((rows, width), BF),
            jax.ShapeDtypeStruct((rows, width), F32),
        ],
        compiler_params=pltpu.CompilerParams(vmem_limit_bytes=40 * MIB),
        cost_estimate=pl.CostEstimate(
            flops=flops, bytes_accessed=8 * MIB, transcendentals=rows * 2 * half * H
        ),
    )(h, q, kv_a, kv_b, kv_a, kv_b)


def attend_back(h, q, kv_a, kv_b, d, lse):
    rows, width = q.shape
    half = kv_a.shape[0]
    flops = 10 * rows * 2 * half * width
    return pl.pallas_call(
        attend_back_kernel,
        grid_spec=pltpu.PrefetchScalarGridSpec(
            num_scalar_prefetch=1,
            grid=(H,),
            in_specs=[
                head_spec(rows),
                head_spec(half),
                head_spec(half),
                head_spec(half, H),
                head_spec(half, H),
                head_spec(rows),
                head_spec(rows),
            ],
            out_specs=[head_spec(rows)] + [head_spec(half)] * 4,
        ),
        out_shape=[
            jax.ShapeDtypeStruct((rows, width), F32),
            jax.ShapeDtypeStruct((half, width), F32),
            jax.ShapeDtypeStruct((half, width), F32),
            jax.ShapeDtypeStruct((half, width), BF),
            jax.ShapeDtypeStruct((half, width), BF),
        ],
        compiler_params=pltpu.CompilerParams(vmem_limit_bytes=40 * MIB),
        cost_estimate=pl.CostEstimate(
            flops=flops, bytes_accessed=16 * MIB, transcendentals=rows * 2 * half * H
        ),
    )(h, q, kv_a, kv_b, kv_a, kv_b, d, lse)


def pick_matrix(meta, col, capacity):
    lane = lax.broadcasted_iota(jnp.int32, meta.shape, 1)
    code = jnp.sum(jnp.where(lane == col, meta.astype(F32), 0.0), axis=1, keepdims=True)
    place = lax.broadcasted_iota(jnp.int32, (meta.shape[0], capacity), 1).astype(F32)
    return jnp.where(code == place, 1.0, 0.0).astype(BF)


def expert_kernel(capacity, total, olds, e_ref, x0_ref, x1_ref, g0_ref, g1_ref, *refs):
    gates, ups, downs = refs[0:4], refs[4:8], refs[8:12]
    sg_ref, su_ref, sd_ref, sgg_old, sdg_old = refs[12:17]
    (
        dx0_ref,
        dx1_ref,
        sgg_ref,
        sdg_ref,
        sa_ref,
        xr_ref,
        gr_ref,
        gi_ref,
        ui_ref,
        wa_ref,
    ) = refs[17 + olds :]
    xs, gs, dxs = (x0_ref, x1_ref), (g0_ref, g1_ref), (dx0_ref, dx1_ref)
    width = sg_ref.shape[0]
    tokens = x0_ref.shape[0]
    c = capacity
    x2 = jnp.concatenate([r[:, :width] for r in xs], axis=0)
    g2 = jnp.concatenate([r[:, :width] for r in gs], axis=0)
    hg, hu = dot(x2, sg_ref[...]), dot(x2, su_ref[...])
    ab = dot(g2, sd_ref[...], (1, 1))
    s = jax.nn.sigmoid(hg)
    silu = hg * s
    act = (silu * hu).astype(BF)
    gi = (ab * hu * (s * (1.0 + hg * (1.0 - s)))).astype(BF)
    ui = (ab * silu).astype(BF)
    sa_ref[0] = act
    gu = jnp.concatenate([gi, ui], axis=1)
    sgg_ref[...] = sgg_old[...] + dot(x2, gu, (0, 0))
    sdg_ref[...] = sdg_old[...] + dot(act, g2, (0, 0))
    dx = dot(gi, sg_ref[...], (1, 1)) + dot(ui, su_ref[...], (1, 1))
    totals = [dx[:tokens], dx[tokens:]]
    metas = [0.0, 0.0]
    lane = lax.broadcasted_iota(jnp.int32, (2 * c, LANES), 1)
    for x in range(2):
        col = 2 * e_ref[0] + x
        picks, weights = [], []
        for j in range(2):
            pick = pick_matrix(gs[j][:, width:], col, c)
            picks.append(pick)
            rows = dot(pick, xs[j][...], (0, 0))
            xr_ref[x, 0, j * c : (j + 1) * c, :] = rows[:, :width].astype(BF)
            weights.append(rows[:, width:])
            gr_ref[x, 0, j * c : (j + 1) * c, :] = dot(pick, gs[j][:, :width], (0, 0)).astype(BF)
        w = jnp.concatenate(weights, axis=0)
        w = jnp.sum(jnp.where(lane == col, w, 0.0), axis=1, keepdims=True)
        xr, gr = xr_ref[x, 0], gr_ref[x, 0]
        dxr = jnp.zeros((2 * c, width), F32)
        wb = jnp.zeros((2 * c, 1), F32)
        for r in range(4):
            wg, wu, wd = gates[r][x], ups[r][x], downs[r][x]
            hg, hu = dot(xr, wg), dot(xr, wu)
            ab = dot(gr, wd, (1, 1))
            s = jax.nn.sigmoid(hg)
            silu = hg * s
            act = silu * hu
            wb = wb + jnp.sum(act * ab, axis=1, keepdims=True)
            ab = ab * w
            gi = (ab * hu * (s * (1.0 + hg * (1.0 - s)))).astype(BF)
            ui = (ab * silu).astype(BF)
            gi_ref[r, x, 0] = gi
            ui_ref[r, x, 0] = ui
            wa_ref[r, x, 0] = (act * w).astype(BF)
            dxr = dxr + dot(gi, wg, (1, 1)) + dot(ui, wu, (1, 1))
        dxr = dxr.astype(BF)
        high = wb.astype(BF).astype(F32)
        meta = jnp.where(lane == col, high, 0.0) + jnp.where(lane == total + col, wb - high, 0.0)
        meta = meta.astype(BF)
        for j in range(2):
            span = slice(j * c, (j + 1) * c)
            totals[j] = totals[j] + dot(picks[j], dxr[span])
            metas[j] = metas[j] + dot(picks[j], meta[span])
    for j in range(2):
        dxs[j][:, :width] = totals[j].astype(BF)
        dxs[j][:, width:] = metas[j].astype(BF)


def expert_out_kernel(capacity, e_ref, g0_ref, g1_ref, wa_ref, sa_ref, *refs):
    downs, sd_ref, outs = refs[0:4], refs[4], refs[5:7]
    width = sd_ref.shape[1]
    tokens = g0_ref.shape[0]
    c = capacity
    gs = (g0_ref, g1_ref)
    shared = dot(sa_ref[0], sd_ref[...])
    totals = [shared[:tokens], shared[tokens:]]
    for x in range(2):
        rows = jnp.zeros((2 * c, width), F32)
        for r in range(4):
            rows = rows + dot(wa_ref[r, x, 0], downs[r][x])
        rows = rows.astype(BF)
        for j in range(2):
            pick = pick_matrix(gs[j][...], 2 * e_ref[0] + x, c)
            totals[j] = totals[j] + dot(pick, rows[j * c : (j + 1) * c])
    for j in range(2):
        outs[j][...] = totals[j].astype(BF)


def whole(shape):
    return pl.BlockSpec(shape, lambda i, e: (0,) * len(shape), pipeline_mode=pl.Buffered(1))


def expert_stage(
    k, stages, capacity, total, e, x_pair, g_pair, gates, ups, downs, sg, su, sd, carry, bufs
):
    tokens, wide = x_pair[0].shape
    width = sg.shape[0]
    hidden = gates[0].shape[2]
    c2 = 2 * capacity
    shared = sg.shape[1]
    olds = 0 if bufs is None else 6
    shapes = [
        ((stages, 2 * tokens, shared), (1, 2 * tokens, shared), (k, 0, 0)),
        ((2, stages, c2, width), (2, 1, c2, width), (0, k, 0, 0)),
        ((2, stages, c2, width), (2, 1, c2, width), (0, k, 0, 0)),
        ((4, 2, stages, c2, hidden), (4, 2, 1, c2, hidden), (0, 0, k, 0, 0)),
        ((4, 2, stages, c2, hidden), (4, 2, 1, c2, hidden), (0, 0, k, 0, 0)),
        ((4, 2, stages, c2, hidden), (4, 2, 1, c2, hidden), (0, 0, k, 0, 0)),
    ]

    def at(block, where):
        return pl.BlockSpec(block, lambda i, e: where)

    ins = [e, *x_pair, *g_pair, *gates, *ups, *downs, sg, su, sd, *carry]
    in_specs = [whole(v.shape) for v in ins[1:]]
    alias = {}
    if bufs is not None:
        for n, b in enumerate(bufs):
            alias[len(ins)] = 4 + n
            ins.append(b)
            in_specs.append(pl.BlockSpec(memory_space=pl.ANY))
    out_shape = [jax.ShapeDtypeStruct((tokens, wide), BF)] * 2 + [
        jax.ShapeDtypeStruct(v.shape, v.dtype) for v in carry
    ]
    out_specs = [whole((tokens, wide))] * 2 + [whole(v.shape) for v in carry]
    for full, block, where in shapes:
        out_shape.append(jax.ShapeDtypeStruct(full, BF))
        out_specs.append(at(block, where))
    outs = pl.pallas_call(
        functools.partial(expert_kernel, capacity, total, olds),
        grid_spec=pltpu.PrefetchScalarGridSpec(
            num_scalar_prefetch=1, grid=(1,), in_specs=in_specs, out_specs=out_specs
        ),
        out_shape=out_shape,
        input_output_aliases=alias,
        compiler_params=pltpu.CompilerParams(vmem_limit_bytes=60 * MIB),
        cost_estimate=pl.CostEstimate(
            flops=20 * c2 * width * 4 * hidden, bytes_accessed=24 * MIB, transcendentals=c2 * 8 * hidden
        ),
    )(*ins)
    return outs[0:2], outs[2:4], outs[4:]


def expert_out(k, capacity, e, g_pair, wa, sa, downs, sd):
    tokens = g_pair[0].shape[0]
    width = sd.shape[1]
    c2 = wa.shape[3]
    last = g_pair[0].shape[1] // LANES - 1
    meta = pl.BlockSpec((tokens, LANES), lambda i, e: (0, last))
    return pl.pallas_call(
        functools.partial(expert_out_kernel, capacity),
        grid_spec=pltpu.PrefetchScalarGridSpec(
            num_scalar_prefetch=1,
            grid=(1,),
            in_specs=[
                meta,
                meta,
                pl.BlockSpec((4, 2, 1, c2, wa.shape[4]), lambda i, e: (0, 0, k, 0, 0)),
                pl.BlockSpec((1,) + sa.shape[1:], lambda i, e: (k, 0, 0)),
            ]
            + [whole(d.shape) for d in downs]
            + [whole(sd.shape)],
            out_specs=[whole((tokens, width))] * 2,
        ),
        out_shape=[jax.ShapeDtypeStruct((tokens, width), BF)] * 2,
        compiler_params=pltpu.CompilerParams(vmem_limit_bytes=40 * MIB),
        cost_estimate=pl.CostEstimate(
            flops=4 * c2 * width * 4 * wa.shape[4], bytes_accessed=10 * MIB, transcendentals=0
        ),
    )(e, *g_pair, wa, sa, *downs, sd)


def dispatch_kernel(capacity, total, x_ref, g_ref, *refs):
    gates, ups, downs = refs[0:4], refs[4:8], refs[8:12]
    sg_ref, su_ref, sd_ref = refs[12:15]
    dx_ref, out_ref, sgg_ref, sdg_ref, xr_ref, gr_ref, gu_ref, wa_ref = refs[15:23]
    xbuf, sbuf, tbuf, wgu, wd, bounce = refs[23:29]
    rx_s, rx_r, sx_s, sx_r, sr_s, sr_r, rt_s, rt_r, w_sem, d_sem = refs[29:]
    k = pl.program_id(0)
    stages = xbuf.shape[0]
    tokens, width = x_ref.shape[0], sg_ref.shape[0]
    hidden = gates[0].shape[2]
    wide = wd.shape[1] // 4
    c = capacity
    e, h = lax.axis_index("ep"), lax.axis_index("hp")
    n = 2 * stages
    right, left = lax.rem(e + 2, n), lax.rem(e + n - 2, n)
    pair = e + 1 - 2 * lax.rem(e, 2)

    def send(src, dst, s, r, i, where):
        return pltpu.make_async_remote_copy(
            src_ref=src,
            dst_ref=dst,
            send_sem=s.at[i],
            recv_sem=r.at[i],
            device_id=(where, h),
            device_id_type=pl.DeviceIdType.MESH,
        )

    def ring_x(i):
        return send(xbuf.at[i, 0], xbuf.at[i + 1, 0], rx_s, rx_r, i, right)

    def swap_x(i):
        return send(xbuf.at[i, 0], xbuf.at[i, 1], sx_s, sx_r, i, pair)

    def swap_r(i):
        return send(xbuf.at[i, 1], sbuf.at[i], sr_s, sr_r, i, pair)

    def ring_t(i):
        return send(xbuf.at[i, 0], tbuf.at[i], rt_s, rt_r, i, right)

    @pl.when(k == 0)
    def _():
        barrier = pltpu.get_barrier_semaphore()
        for where in (right, left, pair):
            pl.semaphore_signal(
                barrier, inc=1, device_id=(where, h), device_id_type=pl.DeviceIdType.MESH
            )
        xbuf[0, 0] = x_ref[...]
        pl.semaphore_wait(barrier, 3)
        ring_x(0).start()
        swap_x(0).start()
        rest = wide - hidden
        down_copies = []
        for r in range(4):
            for x in range(2):
                copy = pltpu.make_async_copy(
                    downs[r].at[x],
                    wd.at[x, pl.ds(r * wide, hidden), :],
                    d_sem.at[2 * r + x],
                )
                copy.start()
                down_copies.append(copy)
        todo = [
            (v[r], x, 2 * r + i)
            for x in range(2)
            for r in range(4)
            for i, v in enumerate((gates, ups))
        ]
        slots = bounce.shape[0]

        def load(i):
            ref, x, _ = todo[i]
            return pltpu.make_async_copy(ref.at[x], bounce.at[i % slots], w_sem.at[i % slots])

        for i in range(slots):
            load(i).start()
        for i, (_, x, at) in enumerate(todo):
            load(i).wait()
            wgu[x, :, at * wide : (at + 1) * wide] = jnp.concatenate(
                [bounce[i % slots], jnp.zeros((width, rest), BF)], axis=1
            )
            if i + slots < len(todo):
                load(i + slots).start()
        for copy in down_copies:
            copy.wait()
        for r in range(4):
            for x in range(2):
                wd[x, r * wide + hidden : (r + 1) * wide, :] = jnp.zeros((rest, width), BF)
        sgg_ref[...] = jnp.zeros_like(sgg_ref)
        sdg_ref[...] = jnp.zeros_like(sdg_ref)

    @pl.when(k < stages - 1)
    def _():
        ring_x(k).wait_recv()

    @pl.when(k < stages - 2)
    def _():
        ring_x(k + 1).start()

    @pl.when(k < stages - 1)
    def _():
        swap_x(k + 1).start()

    swap_x(k).wait_recv()

    x2 = jnp.concatenate([xbuf[k, j, :, :width] for j in range(2)], axis=0)
    g2 = jnp.concatenate([g_ref[0, j, :, :width] for j in range(2)], axis=0)
    hg, hu = dot(x2, sg_ref[...]), dot(x2, su_ref[...])
    ab = dot(g2, sd_ref[...], (1, 1))
    s = jax.nn.sigmoid(hg)
    silu = hg * s
    act = (silu * hu).astype(BF)
    gi = (ab * hu * (s * (1.0 + hg * (1.0 - s)))).astype(BF)
    ui = (ab * silu).astype(BF)
    sgg_ref[...] += dot(x2, jnp.concatenate([gi, ui], axis=1), (0, 0))
    sdg_ref[...] += dot(act, g2, (0, 0))
    dx = dot(gi, sg_ref[...], (1, 1)) + dot(ui, su_ref[...], (1, 1))
    totals = [dx[:tokens], dx[tokens:]]
    out = dot(act, sd_ref[...])
    outs = [out[:tokens], out[tokens:]]
    metas = [0.0, 0.0]
    lane = lax.broadcasted_iota(jnp.int32, (2 * c, LANES), 1)
    for x in range(2):
        col = 2 * e + x
        picks, weights = [], []
        for j in range(2):
            pick = pick_matrix(g_ref[0, j, :, width:], col, c)
            picks.append(pick)
            rows = dot(pick, xbuf[k, j], (0, 0))
            xr_ref[x, 0, j * c : (j + 1) * c, :] = rows[:, :width].astype(BF)
            weights.append(rows[:, width:])
            gr_ref[x, 0, j * c : (j + 1) * c, :] = dot(
                pick, g_ref[0, j, :, :width], (0, 0)
            ).astype(BF)
        w = jnp.concatenate(weights, axis=0)
        w = jnp.sum(jnp.where(lane == col, w, 0.0), axis=1, keepdims=True)
        xr, gr = xr_ref[x, 0], gr_ref[x, 0]
        wb = jnp.zeros((2 * c, 1), F32)
        for r in range(4):
            hgu = dot(xr, wgu[x, :, 2 * r * wide : 2 * (r + 1) * wide])
            ab = dot(gr, wd[x, r * wide : (r + 1) * wide, :], (1, 1))
            hg, hu = hgu[:, :wide], hgu[:, wide:]
            s = jax.nn.sigmoid(hg)
            silu = hg * s
            act = silu * hu
            wb = wb + jnp.sum(act * ab, axis=1, keepdims=True)
            ab = ab * w
            at = 2 * r * wide
            gu_ref[x, 0, :, at : at + wide] = (ab * hu * (s * (1.0 + hg * (1.0 - s)))).astype(BF)
            gu_ref[x, 0, :, at + wide : at + 2 * wide] = (ab * silu).astype(BF)
            wa_ref[x, 0, :, r * wide : (r + 1) * wide] = (act * w).astype(BF)
        dxr = dot(gu_ref[x, 0], wgu[x], (1, 1)).astype(BF)
        rows = dot(wa_ref[x, 0], wd[x]).astype(BF)
        high = wb.astype(BF).astype(F32)
        meta = jnp.where(lane == col, high, 0.0) + jnp.where(lane == total + col, wb - high, 0.0)
        meta = meta.astype(BF)
        for j in range(2):
            span = slice(j * c, (j + 1) * c)
            totals[j] = totals[j] + dot(picks[j], dxr[span])
            outs[j] = outs[j] + dot(picks[j], rows[span])
            metas[j] = metas[j] + dot(picks[j], meta[span])

    @pl.when(k < stages - 1)
    def _():
        ring_x(k).wait_send()

    swap_x(k).wait_send()
    for j in range(2):
        xbuf[k, j, :, :width] = totals[j].astype(BF)
        xbuf[k, j, :, width:] = metas[j].astype(BF)
        out_ref[0, j] = outs[j].astype(BF)

    @pl.when(k >= 1)
    def _():
        swap_r(k).start()

    def advance(i, first):
        swap_r(i).wait_recv()
        here = xbuf[i, 0].astype(F32) + sbuf[i].astype(F32)
        if not first:
            ring_t(i - 1).wait_recv()
            here = here + tbuf[i - 1].astype(F32)
        xbuf[i, 0] = here.astype(BF)
        ring_t(i).start()

    for i in range(1, stages - 1):

        @pl.when(k == i + 1)
        def _(i=i):
            advance(i, i == 1)

    @pl.when(k == stages - 1)
    def _():
        swap_r(0).start()
        advance(stages - 1, stages == 2)
        swap_r(0).wait_recv()
        ring_t(stages - 1).wait_recv()
        dx_ref[...] = (
            xbuf[0, 0].astype(F32) + sbuf[0].astype(F32) + tbuf[stages - 1].astype(F32)
        )
        for i in range(stages):
            swap_r(i).wait_send()
        for i in range(1, stages):
            ring_t(i).wait_send()


def dispatch(capacity, total, x_ext, g_all, gates, ups, downs, sg, su, sd):
    stages, _, tokens, ext = g_all.shape
    width, shared = sg.shape
    hidden = gates[0].shape[2]
    wide = -(-hidden // LANES) * LANES
    c2 = 2 * capacity
    once = pl.Buffered(1)

    def fixed(shape):
        return pl.BlockSpec(shape, lambda k: (0,) * len(shape), pipeline_mode=once)

    def per_stage(shape):
        return pl.BlockSpec(shape, lambda k: (0, k, 0, 0), pipeline_mode=once)

    anywhere = pl.BlockSpec(memory_space=pl.ANY)
    return pl.pallas_call(
        functools.partial(dispatch_kernel, capacity, total),
        grid=(stages,),
        in_specs=[
            fixed((tokens, ext)),
            pl.BlockSpec((1, 2, tokens, ext), lambda k: (k, 0, 0, 0)),
        ]
        + [anywhere] * 12
        + [fixed(sg.shape), fixed(su.shape), fixed(sd.shape)],
        out_specs=[
            fixed((tokens, ext)),
            pl.BlockSpec((1, 2, tokens, width), lambda k: (k, 0, 0, 0), pipeline_mode=once),
            fixed((width, 2 * shared)),
            fixed((shared, width)),
            per_stage((2, 1, c2, width)),
            per_stage((2, 1, c2, width)),
            per_stage((2, 1, c2, 8 * wide)),
            per_stage((2, 1, c2, 4 * wide)),
        ],
        out_shape=[
            jax.ShapeDtypeStruct((tokens, ext), F32),
            jax.ShapeDtypeStruct((stages, 2, tokens, width), BF),
            jax.ShapeDtypeStruct((width, 2 * shared), F32),
            jax.ShapeDtypeStruct((shared, width), F32),
            jax.ShapeDtypeStruct((2, stages, c2, width), BF),
            jax.ShapeDtypeStruct((2, stages, c2, width), BF),
            jax.ShapeDtypeStruct((2, stages, c2, 8 * wide), BF),
            jax.ShapeDtypeStruct((2, stages, c2, 4 * wide), BF),
        ],
        scratch_shapes=[
            pltpu.VMEM((stages, 2, tokens, ext), BF),
            pltpu.VMEM((stages, tokens, ext), BF),
            pltpu.VMEM((stages, tokens, ext), BF),
            pltpu.VMEM((2, width, 8 * wide), BF),
            pltpu.VMEM((2, 4 * wide, width), BF),
            pltpu.VMEM((2, width, hidden), BF),
        ]
        + [pltpu.SemaphoreType.DMA((stages,))] * 8
        + [pltpu.SemaphoreType.DMA((2,)), pltpu.SemaphoreType.DMA((8,))],
        compiler_params=pltpu.CompilerParams(
            vmem_limit_bytes=63 * MIB, collective_id=0, has_side_effects=True
        ),
        cost_estimate=pl.CostEstimate(
            flops=24 * c2 * stages * width * 4 * hidden,
            bytes_accessed=80 * MIB,
            transcendentals=stages * c2 * 8 * hidden,
        ),
    )(x_ext, g_all, *gates, *ups, *downs, sg, su, sd)


def rms(values):
    return lax.rsqrt(jnp.mean(values * values, axis=-1, keepdims=True) + epsilon)


def norm_back(values, inv, gain, upstream):
    weighted = upstream * gain
    inner = jnp.mean(weighted * values, axis=-1, keepdims=True)
    to_input = weighted * inv - values * (inv * inv * inv * inner)
    return to_input, jnp.sum(upstream * values * inv, axis=0)


def half_turn(v):
    lane = lax.broadcasted_iota(jnp.int32, v.shape, 1)
    return jnp.where(
        lane % HD < HD // 2, -jnp.roll(v, -HD // 2, axis=1), jnp.roll(v, HD // 2, axis=1)
    )


def rotary_tables(positions):
    exponent = jnp.arange(HD // 2, dtype=F32) * (2.0 / HD)
    theta = positions.astype(F32)[:, None] * jnp.power(10000.0, -exponent)[None, :]
    theta = jnp.concatenate([theta, theta], axis=-1)
    return jnp.tile(jnp.cos(theta), (1, H)), jnp.tile(jnp.sin(theta), (1, H))


def per_device(
    tokens,
    attn_gain,
    query_weight,
    key_weight,
    value_weight,
    out_weight,
    ffn_gain,
    router_weight,
    shared_gate,
    shared_up,
    shared_down,
    expert_gate,
    expert_up,
    expert_down,
    routes,
    keep_mask,
    cotangent,
):
    e, h = lax.axis_index("ep"), lax.axis_index("hp")
    ep = lax.axis_size("ep")
    stages = ep // 2
    rows, width = tokens.shape
    top = routes.shape[1]
    total = router_weight.shape[1]
    capacity = -(-(5 * rows * top // (4 * total)) // 16) * 16
    e_arr, h_arr = jnp.full((1,), e, jnp.int32), jnp.full((1,), h, jnp.int32)

    far_tokens = swap_y(tokens)
    k_w, v_w = gather_hp(key_weight), gather_hp(value_weight)
    q_w = gather_hp(query_weight)
    o_w = gather_hp(after(out_weight, q_w[2], k_w[2], v_w[2]))
    gates, ups, downs = (
        gather_hp(after(v, o_w[2])) for v in (expert_gate, expert_up, expert_down)
    )
    units = shared_down.shape[0] // ep
    tiny = [attn_gain[:, None], ffn_gain[:, None], router_weight]
    small = jnp.concatenate(tiny + [jnp.zeros((width // 4, LANES - 2 - total), BF)], axis=1)

    def mine(v):
        v = v.reshape(width // 4, 4, -1)
        v = lax.dynamic_slice_in_dim(v, e * units, units, axis=2).reshape(width // 4, 4 * units)
        return jnp.pad(v, ((0, 0), (0, LANES - 4 * units)))

    small = jnp.concatenate([small, mine(shared_gate), mine(shared_up)], axis=1)
    small = jnp.concatenate(gather_hp(small), axis=0)
    gain_one = small[:, 0].astype(F32)[None, :]
    small = relative(small, h, 0)
    gain_two = small[:, 1].astype(F32)[None, :]
    router = small[:, 2 : 2 + total]
    sg, su = small[:, LANES : 2 * LANES], small[:, 2 * LANES :]
    sd = lax.dynamic_slice_in_dim(shared_down, e * units, units, axis=0)
    sd = relative(jnp.concatenate(gather_hp(sd), axis=0), h, 0)
    sd = jnp.pad(sd, ((0, LANES - 4 * units), (0, 0)))

    expert = jnp.arange(total, dtype=jnp.int32)
    hit_each = routes[:, :, None] == expert[None, None, :]
    hit = jnp.any(hit_each, axis=1)
    kept = jnp.sum(jnp.where(hit_each, keep_mask[:, :, None], 0), axis=1)
    below = (jnp.arange(rows)[:, None] > jnp.arange(rows)[None, :]).astype(BF)
    place = jnp.where(hit, dot(below, hit.astype(BF)), -1.0)
    kept = kept.astype(F32)
    g_ext = jnp.concatenate(
        [
            cotangent,
            place.astype(BF),
            jnp.zeros((rows, LANES - total), BF),
        ],
        axis=1,
    )
    g_blocks = gather_ep(g_ext)

    pos = jnp.arange(rows, dtype=jnp.int32)
    pos = jnp.concatenate([h * rows + pos, (h ^ 2) * rows + pos])
    cosine, sine = rotary_tables(pos)
    residual = tokens.astype(F32)
    both = relative(jnp.concatenate([tokens, far_tokens], axis=0), h, 1).astype(F32)
    inv_one = rms(both)
    first_in = after((both * inv_one * gain_one).astype(BF), g_blocks)

    def rotate(v, n):
        return v * cosine[:n] + half_turn(v) * sine[:n]

    def rotate_back(v, n):
        return v * cosine[:n] - half_turn(v * sine[:n])

    k_w, v_w = jnp.concatenate(k_w, axis=0), jnp.concatenate(v_w, axis=0)
    q_w, o_w = jnp.concatenate(q_w, axis=0), jnp.concatenate(o_w, axis=0)
    keys = rotate(dot(first_in, k_w), 2 * rows).astype(BF)
    values = dot(first_in, v_w).astype(BF)
    kv_a = jnp.concatenate([keys, values], axis=1)
    kv_b = swap_core(kv_a)
    query = rotate(dot(first_in[:rows], q_w), rows).astype(BF)
    mixed, lse = attend(h_arr, query, kv_a, kv_b)
    mixed_rel = relative(mixed, h, 1)
    middle = residual + dot(mixed_rel, o_w)
    inv_two = rms(middle)
    second_in = (middle * inv_two * gain_two).astype(BF)

    logits = jnp.where(hit, dot(second_in, router), -1e30)
    gates_of = jnp.where(hit, jnp.exp(logits - jnp.max(logits, axis=1, keepdims=True)), 0.0)
    gates_of = gates_of / jnp.sum(gates_of, axis=1, keepdims=True)
    pair_weight = gates_of * kept
    x_ext = jnp.concatenate(
        [second_in, pair_weight.astype(BF), jnp.zeros((rows, LANES - total), BF)], axis=1
    )

    flat = (2, ep * capacity)

    def expert_grad(left, right):
        return jnp.einsum("xna,xnb->xab", left, right, preferred_element_type=F32)

    if stages <= 4:
        g_all = jnp.stack([jnp.stack(pair) for pair in g_blocks])
        dx_sum, out_all, sgg, sdg, xr, gr, gu, wa = dispatch(
            capacity, total, x_ext, g_all, gates, ups, downs, sg, su, sd
        )
        out_parts = [(out_all[k, 0], out_all[k, 1]) for k in range(stages)]
        hidden, wide = expert_gate.shape[2], wa.shape[3] // 4
        xr, gr, gu, wa = (v.reshape(flat + (v.shape[-1],)) for v in (xr, gr, gu, wa))
        gu = expert_grad(xr, gu).astype(BF)
        wa = expert_grad(wa, gr).astype(BF)
        gate_parts, up_parts = (
            [gu[:, :, at * wide : at * wide + hidden] for at in range(i, 8, 2)] for i in (0, 1)
        )
        down_parts = [wa[:, r * wide : r * wide + hidden] for r in range(4)]
    else:
        x_blocks = gather_ep(after(x_ext, g_blocks))
        carry = (jnp.zeros((width, 2 * LANES), F32), jnp.zeros((LANES, width), F32))
        bufs, dx_parts = None, []
        for k in range(stages):
            dx, carry, bufs = expert_stage(
                k,
                stages,
                capacity,
                total,
                e_arr,
                x_blocks[k],
                g_blocks[k],
                gates,
                ups,
                downs,
                sg,
                su,
                sd,
                carry,
                bufs,
            )
            dx_parts.append(dx)
        dx_sum = scatter_ep(dx_parts)
        sgg, sdg = carry
        sa, xr, gr, gi, ui, wa = bufs
        out_parts = [
            expert_out(k, capacity, e_arr, g_blocks[k], wa, sa, downs, sd) for k in range(stages)
        ]
        xr, gr = xr.reshape(flat + (width,)), gr.reshape(flat + (width,))
        gi, ui, wa = (v.reshape((4,) + flat + (v.shape[-1],)) for v in (gi, ui, wa))
        gate_parts = [expert_grad(xr, gi[r]) for r in range(4)]
        up_parts = [expert_grad(xr, ui[r]) for r in range(4)]
        down_parts = [expert_grad(wa[r], gr) for r in range(4)]
    layer = (middle + scatter_ep(after(out_parts, dx_sum))).astype(BF)
    gate_grad, up_grad, down_grad = (
        scatter_hp(parts) for parts in (gate_parts, up_parts, down_parts)
    )

    sgg = relative(sgg, h, 0)
    sgg = scatter_hp(jnp.split(sgg, 4, axis=0)).astype(BF)
    sdg = scatter_hp(jnp.split(relative(sdg[: 4 * units], h, 0), 4, axis=0)).astype(BF)
    sgg, sdg = (spread_ep(after(v, dx_sum), e) for v in (sgg, sdg))
    sdg = sdg.reshape(ep * units, width)

    def spread(v):
        v = v[:, :, : 4 * units].reshape(ep, width // 4, 4, units)
        return v.transpose(1, 2, 0, 3).reshape(width // 4, 4 * ep * units).astype(F32)

    sgate_grad, sup_grad = spread(sgg[:, :, :LANES]), spread(sgg[:, :, LANES:])
    sdown_grad = sdg.astype(F32)

    grad_out = cotangent.astype(F32)
    weight_back = dx_sum[:, width : width + total] + dx_sum[:, width + total : width + 2 * total]
    gate_back = weight_back * kept
    chosen_back = gates_of * (gate_back - jnp.sum(gates_of * gate_back, axis=1, keepdims=True))
    logits_back = chosen_back.astype(BF)
    router_part = dot(logits_back, second_in, (0, 0))
    second_back = dx_sum[:, :width] + dot(logits_back, router, (1, 1))
    to_middle, gain_two_part = norm_back(middle, inv_two, gain_two, second_back)
    middle_back = grad_out + to_middle
    attn_back = middle_back.astype(BF)
    counts_part = jnp.sum(kept, axis=0)
    tail = jnp.zeros((1, width - total), F32)
    sums = jnp.concatenate(
        [
            router_part,
            gain_two_part[None, :],
            jnp.concatenate([counts_part[None, :], tail], axis=1),
        ],
        axis=0,
    )
    sums = sum_all_small(sums)

    mixed_back = relative(dot(attn_back, o_w, (1, 1)).astype(BF), h, 1)
    out_part = dot(mixed_rel, attn_back, (0, 0))
    out_grad = sum_ep(scatter_hp(jnp.split(out_part, 4, axis=0)), e)
    dq, dka, dva, dkb, dvb = attend_back(h_arr, query, kv_a, kv_b, mixed_back, lse)
    dk = dka + swap_core(dkb).astype(F32)
    dv = dva + swap_core(dvb).astype(F32)
    query_raw = rotate_back(dq, rows).astype(BF)
    key_raw = rotate_back(dk, 2 * rows).astype(BF)
    value_raw = dv.astype(BF)
    kv_back = dot(key_raw, k_w, (1, 1)) + dot(value_raw, v_w, (1, 1))
    from_far = swap_y(kv_back[rows:].astype(BF))
    q_part = dot(first_in[:rows], query_raw, (0, 0))
    k_part = dot(first_in, key_raw, (0, 0))
    v_part = dot(first_in, value_raw, (0, 0))
    query_grad, key_grad, value_grad = (
        sum_ep(scatter_hp(jnp.split(v, 4, axis=0)), e) for v in (q_part, k_part, v_part)
    )
    first_back = dot(query_raw, q_w, (1, 1)) + kv_back[:rows]
    quarters = jnp.split(from_far.astype(F32), 4, axis=1)
    first_back = first_back + jnp.concatenate([quarters[i ^ 2] for i in range(4)], axis=1)
    to_tokens, gain_one_part = norm_back(both[:rows], inv_one[:rows], gain_one, first_back)
    tokens_grad = middle_back + relative(to_tokens, h, 1)
    gain_one_grad = sum_all_small(relative(gain_one_part[None, :], h, 1))[0]

    def own(v, n):
        return lax.dynamic_slice_in_dim(v, h * n, n, axis=0)

    return (
        layer,
        tokens_grad,
        own(gain_one_grad, width // 4),
        query_grad,
        key_grad,
        value_grad,
        out_grad,
        own(sums[total], width // 4),
        own(sums[:total].T, width // 4),
        sgate_grad,
        sup_grad,
        sdown_grad,
        gate_grad,
        up_grad,
        down_grad,
        own(sums[total + 1], total // 4).astype(jnp.int32),
    )


def solution(mesh):
    row, ep_hp = P("hp", None), P(("ep", "hp"), None)
    return jax.shard_map(
        per_device,
        mesh=mesh,
        in_specs=(
            ep_hp,
            P("hp"),
            row,
            row,
            row,
            row,
            P("hp"),
            row,
            row,
            row,
            row,
            P("ep", None, "hp"),
            P("ep", None, "hp"),
            P("ep", "hp", None),
            ep_hp,
            ep_hp,
            ep_hp,
        ),
        out_specs=(
            ep_hp,
            ep_hp,
            P("hp"),
            row,
            row,
            row,
            row,
            P("hp"),
            row,
            row,
            row,
            row,
            P("ep", None, "hp"),
            P("ep", None, "hp"),
            P("ep", "hp", None),
            P("hp"),
        ),
        check_vma=False,
    )
```

```python
import functools

import jax
import jax.numpy as jnp
from jax import lax
from jax.experimental import pallas as pl
from jax.experimental.pallas import tpu as pltpu
from jax.sharding import PartitionSpec as P

H = 10
HD = 128
LANES = 128
BF = jnp.bfloat16
F32 = jnp.float32
epsilon = 1e-06
MIB = 1 << 20


def dot(left, right, over=(1, 0)):
    return lax.dot_general(
        left, right, (((over[0],), (over[1],)), ((), ())), preferred_element_type=F32
    )


def swap_core(v):
    return lax.ppermute(v, "hp", [(i, i ^ 1) for i in range(4)])


def swap_y(v):
    return lax.ppermute(v, "hp", [(i, i ^ 2) for i in range(4)])


def swap_pair(v):
    n = lax.axis_size("ep")
    return lax.ppermute(v, "ep", [(i, i ^ 1) for i in range(n)])


def ring(v):
    n = lax.axis_size("ep")
    return lax.ppermute(v, "ep", [(i, (i + 2) % n) for i in range(n)])


def shift(v, steps):
    n = lax.axis_size("ep")
    return lax.ppermute(v, "ep", [(i, (i + 2 * steps) % n) for i in range(n)])


def after(v, *others):
    return lax.optimization_barrier((v, others))[0]


def gather_hp(v):
    far = swap_y(v)
    return [v, far, swap_core(v), swap_core(far)]


def scatter_hp(parts):
    near = swap_core(parts[2].astype(BF)).astype(F32) + parts[0].astype(F32)
    over = swap_core(parts[3].astype(BF)).astype(F32) + parts[1].astype(F32)
    return near + swap_y(over.astype(BF)).astype(F32)


def crossed(b, h):
    odd, high = (h & 1) == 1, (h & 2) == 2
    c = [jnp.where(odd, b[i ^ 1], b[i]) for i in range(4)]
    return [jnp.where(high, c[i ^ 2], c[i]) for i in range(4)]


def relative(v, h, axis):
    c = crossed(jnp.split(v, 4, axis=axis), h)
    return jnp.concatenate([c[0], c[2], c[1], c[3]], axis=axis)


def absolute(v, h, axis):
    b = jnp.split(v, 4, axis=axis)
    return jnp.concatenate(crossed([b[0], b[2], b[1], b[3]], h), axis=axis)


def gather_ep(v):
    stages = lax.axis_size("ep") // 2
    own, out = v, []
    for k in range(stages):
        out.append((own, swap_pair(own)))
        if k < stages - 1:
            own = ring(own)
    return out


def scatter_ep(parts):
    stages = len(parts)
    total = None
    for k in list(range(1, stages)) + [0]:
        here = parts[k][0].astype(F32) + swap_pair(parts[k][1]).astype(F32)
        if total is not None:
            here = here + total.astype(F32)
        total = here if k == 0 else ring(here.astype(BF))
    return total


def spread_ep(v, e):
    n = lax.axis_size("ep")
    stages = n // 2
    x, z = e & 1, e >> 1
    column = lax.dynamic_update_index_in_dim(jnp.zeros((stages,) + v.shape, v.dtype), v, z, 0)
    for step in range(1, stages):
        column = lax.dynamic_update_index_in_dim(
            column, shift(v, step), (z + stages - step) % stages, 0
        )
    far = swap_pair(column)
    both = [jnp.where(x == 0, column, far), jnp.where(x == 0, far, column)]
    return jnp.stack(both, axis=1).reshape((n,) + v.shape)


def sum_ep(v, e):
    n = lax.axis_size("ep")
    stages = n // 2
    x, z = e & 1, e >> 1
    halves = v.reshape(2, v.shape[0] // 2, v.shape[1])
    mine = lax.dynamic_index_in_dim(halves, x, 0, False)
    other = lax.dynamic_index_in_dim(halves, 1 - x, 0, False)
    mine = mine + swap_pair(other.astype(BF)).astype(F32)
    chunks = mine.reshape(stages, mine.shape[0] // stages, mine.shape[1])
    low = chunks.astype(BF)
    total = lax.dynamic_index_in_dim(chunks, z, 0, False)
    for step in range(1, stages):
        part = lax.dynamic_index_in_dim(low, (z + step) % stages, 0, False)
        total = total + shift(part, step).astype(F32)
    total = total.astype(BF)
    half = lax.dynamic_update_index_in_dim(jnp.zeros(chunks.shape, BF), total, z, 0)
    for step in range(1, stages):
        half = lax.dynamic_update_index_in_dim(
            half, shift(total, step), (z + stages - step) % stages, 0
        )
    half = half.reshape(mine.shape)
    far = swap_pair(half)
    low = jnp.where(x == 0, half, far)
    high = jnp.where(x == 0, far, half)
    return jnp.concatenate([low, high], axis=0).astype(F32)


def sum_all_small(v):
    v = v + swap_core(v)
    v = v + swap_y(v)
    n = lax.axis_size("ep")
    bit = 1
    while bit < n:
        v = v + lax.ppermute(v, "ep", [(i, i ^ bit) for i in range(n)])
        bit *= 2
    return v


def score_mask(h_ref, rows, cols):
    h = h_ref[0]
    at = lax.broadcasted_iota(jnp.int32, (rows, cols), 0) + h * rows
    key = lax.broadcasted_iota(jnp.int32, (rows, cols), 1)
    block = key // rows
    other = jnp.where(
        block == 0, h, jnp.where(block == 1, h ^ 2, jnp.where(block == 2, h ^ 1, h ^ 3))
    )
    return other * rows + key % rows <= at


def turned(v, cosine, sine):
    return v * cosine + pltpu.roll(v, HD // 2, 1) * sine


def project_kernel(
    t_ref, f_ref, gain_ref, k_ref, v_ref, q_ref, cos_ref, sin_ref, x_ref, kv_ref, query_ref
):
    rows = query_ref.shape[0]

    @pl.when(pl.program_id(0) == 0)
    def _():
        for i, ref in enumerate((t_ref, f_ref)):
            v = ref[...].astype(F32)
            x_ref[i * rows : (i + 1) * rows, :] = (v * rms(v) * gain_ref[...]).astype(BF)

    x = x_ref[...]
    cosine, sine = cos_ref[...], sin_ref[...]
    keys, query = dot(x, k_ref[...]), dot(x[:rows], q_ref[...])
    kv_ref[1] = dot(x, v_ref[...]).astype(BF)
    for i in range(k_ref.shape[1] // HD):
        span = slice(i * HD, (i + 1) * HD)
        kv_ref[0, :, span] = turned(keys[:, span], cosine, sine).astype(BF)
        query_ref[:, span] = turned(query[:, span], cosine[:rows], sine[:rows]).astype(BF)


def project(tokens, far, gain, k_w, v_w, q_w, cosine, sine):
    rows, width = tokens.shape
    two, block = 2 * rows, 2 * HD
    cols = pl.BlockSpec((width, block), lambda i: (0, i))

    def fixed(v):
        return pl.BlockSpec(v.shape, lambda i: (0, 0))

    return pl.pallas_call(
        project_kernel,
        grid=(width // block,),
        in_specs=[fixed(tokens), fixed(far), fixed(gain), cols, cols, cols]
        + [pl.BlockSpec((two, HD), lambda i: (0, 0))] * 2,
        out_specs=[
            pl.BlockSpec((two, width), lambda i: (0, 0)),
            pl.BlockSpec((2, two, block), lambda i: (0, 0, i)),
            pl.BlockSpec((rows, block), lambda i: (0, i)),
        ],
        out_shape=[
            jax.ShapeDtypeStruct((two, width), BF),
            jax.ShapeDtypeStruct((2, two, width), BF),
            jax.ShapeDtypeStruct((rows, width), BF),
        ],
        compiler_params=pltpu.CompilerParams(vmem_limit_bytes=40 * MIB),
        cost_estimate=pl.CostEstimate(
            flops=10 * rows * width * width, bytes_accessed=14 * MIB, transcendentals=0
        ),
    )(tokens, far, gain, k_w, v_w, q_w, cosine, sine)


def attend_kernel(h_ref, q_ref, ka_ref, kb_ref, va_ref, vb_ref, o_ref, lse_ref):
    rows = q_ref.shape[0]
    half = ka_ref.shape[0]
    q = q_ref[...]
    s = jnp.concatenate([dot(q, ka_ref[...], (1, 1)), dot(q, kb_ref[...], (1, 1))], axis=1)
    s = jnp.where(score_mask(h_ref, rows, 2 * half), s * HD ** (-0.5), -1e30)
    top = jnp.max(s, axis=1, keepdims=True)
    p = jnp.exp(s - top)
    total = jnp.sum(p, axis=1, keepdims=True)
    p = (p * (1.0 / total)).astype(BF)
    o = dot(p[:, :half], va_ref[...]) + dot(p[:, half:], vb_ref[...])
    o_ref[...] = o.astype(BF)
    lse_ref[...] = jnp.broadcast_to(top + jnp.log(total), lse_ref.shape)


def attend_back_kernel(
    h_ref,
    q_ref,
    ka_ref,
    kb_ref,
    va_ref,
    vb_ref,
    d_ref,
    lse_ref,
    cos_ref,
    sin_ref,
    dq_ref,
    da_ref,
    db_ref,
):
    rows = q_ref.shape[0]
    half = ka_ref.shape[0]
    q, d = q_ref[...], d_ref[...]
    cosine, sine = cos_ref[...], -sin_ref[...]
    s = jnp.concatenate([dot(q, ka_ref[...], (1, 1)), dot(q, kb_ref[...], (1, 1))], axis=1)
    s = jnp.where(score_mask(h_ref, rows, 2 * half), s * HD ** (-0.5), -1e30)
    p = jnp.exp(s - lse_ref[:, 0:1])
    back = jnp.concatenate([dot(d, va_ref[...], (1, 1)), dot(d, vb_ref[...], (1, 1))], axis=1)
    inner = jnp.sum(p * back, axis=1, keepdims=True)
    sb = (p * (back - inner) * HD ** (-0.5)).astype(BF)
    p = p.astype(BF)
    dq = dot(sb[:, :half], ka_ref[...]) + dot(sb[:, half:], kb_ref[...])
    dq_ref[...] = turned(dq, cosine[:rows], sine[:rows]).astype(BF)
    dk = turned(dot(sb, q, (0, 0)), cosine, sine)
    dv = dot(p, d, (0, 0))
    da_ref[0] = dk[:half]
    da_ref[1] = dv[:half]
    db_ref[0] = dk[half:].astype(BF)
    db_ref[1] = dv[half:].astype(BF)


def head_spec(rows):
    return pl.BlockSpec((rows, HD), lambda i, h: (0, i))


def kv_spec(rows, which):
    return pl.BlockSpec((None, rows, HD), lambda i, h: (which, 0, i))


def attend(h, q, kv_a, kv_b):
    rows, width = q.shape
    half = kv_a.shape[1]
    flops = 4 * rows * 2 * half * width
    return pl.pallas_call(
        attend_kernel,
        grid_spec=pltpu.PrefetchScalarGridSpec(
            num_scalar_prefetch=1,
            grid=(H,),
            in_specs=[
                head_spec(rows),
                kv_spec(half, 0),
                kv_spec(half, 0),
                kv_spec(half, 1),
                kv_spec(half, 1),
            ],
            out_specs=[head_spec(rows), head_spec(rows)],
        ),
        out_shape=[
            jax.ShapeDtypeStruct((rows, width), BF),
            jax.ShapeDtypeStruct((rows, width), F32),
        ],
        compiler_params=pltpu.CompilerParams(vmem_limit_bytes=40 * MIB),
        cost_estimate=pl.CostEstimate(
            flops=flops, bytes_accessed=8 * MIB, transcendentals=rows * 2 * half * H
        ),
    )(h, q, kv_a, kv_b, kv_a, kv_b)


def attend_back(h, q, kv_a, kv_b, d, lse, cosine, sine):
    rows, width = q.shape
    half = kv_a.shape[1]
    flops = 10 * rows * 2 * half * width
    table = pl.BlockSpec((2 * half, HD), lambda i, h: (0, 0))
    both = pl.BlockSpec((2, half, HD), lambda i, h: (0, 0, i))
    return pl.pallas_call(
        attend_back_kernel,
        grid_spec=pltpu.PrefetchScalarGridSpec(
            num_scalar_prefetch=1,
            grid=(H,),
            in_specs=[
                head_spec(rows),
                kv_spec(half, 0),
                kv_spec(half, 0),
                kv_spec(half, 1),
                kv_spec(half, 1),
                head_spec(rows),
                head_spec(rows),
                table,
                table,
            ],
            out_specs=[head_spec(rows), both, both],
        ),
        out_shape=[
            jax.ShapeDtypeStruct((rows, width), BF),
            jax.ShapeDtypeStruct((2, half, width), F32),
            jax.ShapeDtypeStruct((2, half, width), BF),
        ],
        compiler_params=pltpu.CompilerParams(vmem_limit_bytes=40 * MIB),
        cost_estimate=pl.CostEstimate(
            flops=flops, bytes_accessed=16 * MIB, transcendentals=rows * 2 * half * H
        ),
    )(h, q, kv_a, kv_b, kv_a, kv_b, d, lse, cosine, sine)


def pick_matrix(meta, col, capacity):
    lane = lax.broadcasted_iota(jnp.int32, meta.shape, 1)
    code = jnp.sum(jnp.where(lane == col, meta.astype(F32), 0.0), axis=1, keepdims=True)
    place = lax.broadcasted_iota(jnp.int32, (meta.shape[0], capacity), 1).astype(F32)
    return jnp.where(code == place, 1.0, 0.0).astype(BF)


def expert_kernel(capacity, total, olds, e_ref, x0_ref, x1_ref, g0_ref, g1_ref, *refs):
    gates, ups, downs = refs[0:4], refs[4:8], refs[8:12]
    sg_ref, su_ref, sd_ref, sgg_old, sdg_old = refs[12:17]
    (
        dx0_ref,
        dx1_ref,
        sgg_ref,
        sdg_ref,
        sa_ref,
        xr_ref,
        gr_ref,
        gi_ref,
        ui_ref,
        wa_ref,
    ) = refs[17 + olds :]
    xs, gs, dxs = (x0_ref, x1_ref), (g0_ref, g1_ref), (dx0_ref, dx1_ref)
    width = sg_ref.shape[0]
    tokens = x0_ref.shape[0]
    c = capacity
    x2 = jnp.concatenate([r[:, :width] for r in xs], axis=0)
    g2 = jnp.concatenate([r[:, :width] for r in gs], axis=0)
    hg, hu = dot(x2, sg_ref[...]), dot(x2, su_ref[...])
    ab = dot(g2, sd_ref[...], (1, 1))
    s = jax.nn.sigmoid(hg)
    silu = hg * s
    act = (silu * hu).astype(BF)
    gi = (ab * hu * (s * (1.0 + hg * (1.0 - s)))).astype(BF)
    ui = (ab * silu).astype(BF)
    sa_ref[0] = act
    gu = jnp.concatenate([gi, ui], axis=1)
    sgg_ref[...] = sgg_old[...] + dot(x2, gu, (0, 0))
    sdg_ref[...] = sdg_old[...] + dot(act, g2, (0, 0))
    dx = dot(gi, sg_ref[...], (1, 1)) + dot(ui, su_ref[...], (1, 1))
    totals = [dx[:tokens], dx[tokens:]]
    metas = [0.0, 0.0]
    lane = lax.broadcasted_iota(jnp.int32, (2 * c, LANES), 1)
    for x in range(2):
        col = 2 * e_ref[0] + x
        picks, weights = [], []
        for j in range(2):
            pick = pick_matrix(xs[j][:, width:], total + col, c)
            picks.append(pick)
            rows = dot(pick, xs[j][...], (0, 0))
            xr_ref[x, 0, j * c : (j + 1) * c, :] = rows[:, :width].astype(BF)
            weights.append(rows[:, width:])
            gr_ref[x, 0, j * c : (j + 1) * c, :] = dot(pick, gs[j][:, :width], (0, 0)).astype(BF)
        w = jnp.concatenate(weights, axis=0)
        w = jnp.sum(jnp.where(lane == col, w, 0.0), axis=1, keepdims=True)
        xr, gr = xr_ref[x, 0], gr_ref[x, 0]
        dxr = jnp.zeros((2 * c, width), F32)
        wb = jnp.zeros((2 * c, 1), F32)
        for r in range(4):
            wg, wu, wd = gates[r][x], ups[r][x], downs[r][x]
            hg, hu = dot(xr, wg), dot(xr, wu)
            ab = dot(gr, wd, (1, 1))
            s = jax.nn.sigmoid(hg)
            silu = hg * s
            act = silu * hu
            wb = wb + jnp.sum(act * ab, axis=1, keepdims=True)
            ab = ab * w
            gi = (ab * hu * (s * (1.0 + hg * (1.0 - s)))).astype(BF)
            ui = (ab * silu).astype(BF)
            gi_ref[r, x, 0] = gi
            ui_ref[r, x, 0] = ui
            wa_ref[r, x, 0] = (act * w).astype(BF)
            dxr = dxr + dot(gi, wg, (1, 1)) + dot(ui, wu, (1, 1))
        dxr = dxr.astype(BF)
        high = wb.astype(BF).astype(F32)
        meta = jnp.where(lane == col, high, 0.0) + jnp.where(lane == total + col, wb - high, 0.0)
        meta = meta.astype(BF)
        for j in range(2):
            span = slice(j * c, (j + 1) * c)
            totals[j] = totals[j] + dot(picks[j], dxr[span])
            metas[j] = metas[j] + dot(picks[j], meta[span])
    for j in range(2):
        dxs[j][:, :width] = totals[j].astype(BF)
        dxs[j][:, width:] = metas[j].astype(BF)


def expert_out_kernel(capacity, total, e_ref, x0_ref, x1_ref, wa_ref, sa_ref, *refs):
    downs, sd_ref, outs = refs[0:4], refs[4], refs[5:7]
    width = sd_ref.shape[1]
    tokens = x0_ref.shape[0]
    c = capacity
    xs = (x0_ref, x1_ref)
    shared = dot(sa_ref[0], sd_ref[...])
    totals = [shared[:tokens], shared[tokens:]]
    for x in range(2):
        rows = jnp.zeros((2 * c, width), F32)
        for r in range(4):
            rows = rows + dot(wa_ref[r, x, 0], downs[r][x])
        rows = rows.astype(BF)
        for j in range(2):
            pick = pick_matrix(xs[j][...], total + 2 * e_ref[0] + x, c)
            totals[j] = totals[j] + dot(pick, rows[j * c : (j + 1) * c])
    for j in range(2):
        outs[j][...] = totals[j].astype(BF)


def whole(shape):
    return pl.BlockSpec(shape, lambda i, e: (0,) * len(shape), pipeline_mode=pl.Buffered(1))


def expert_stage(
    k, stages, capacity, total, e, x_pair, g_pair, gates, ups, downs, sg, su, sd, carry, bufs
):
    tokens, wide = x_pair[0].shape
    width = sg.shape[0]
    hidden = gates[0].shape[2]
    c2 = 2 * capacity
    shared = sg.shape[1]
    olds = 0 if bufs is None else 6
    shapes = [
        ((stages, 2 * tokens, shared), (1, 2 * tokens, shared), (k, 0, 0)),
        ((2, stages, c2, width), (2, 1, c2, width), (0, k, 0, 0)),
        ((2, stages, c2, width), (2, 1, c2, width), (0, k, 0, 0)),
        ((4, 2, stages, c2, hidden), (4, 2, 1, c2, hidden), (0, 0, k, 0, 0)),
        ((4, 2, stages, c2, hidden), (4, 2, 1, c2, hidden), (0, 0, k, 0, 0)),
        ((4, 2, stages, c2, hidden), (4, 2, 1, c2, hidden), (0, 0, k, 0, 0)),
    ]

    def at(block, where):
        return pl.BlockSpec(block, lambda i, e: where)

    ins = [e, *x_pair, *g_pair, *gates, *ups, *downs, sg, su, sd, *carry]
    in_specs = [whole(v.shape) for v in ins[1:]]
    alias = {}
    if bufs is not None:
        for n, b in enumerate(bufs):
            alias[len(ins)] = 4 + n
            ins.append(b)
            in_specs.append(pl.BlockSpec(memory_space=pl.ANY))
    out_shape = [jax.ShapeDtypeStruct((tokens, wide), BF)] * 2 + [
        jax.ShapeDtypeStruct(v.shape, v.dtype) for v in carry
    ]
    out_specs = [whole((tokens, wide))] * 2 + [whole(v.shape) for v in carry]
    for full, block, where in shapes:
        out_shape.append(jax.ShapeDtypeStruct(full, BF))
        out_specs.append(at(block, where))
    outs = pl.pallas_call(
        functools.partial(expert_kernel, capacity, total, olds),
        grid_spec=pltpu.PrefetchScalarGridSpec(
            num_scalar_prefetch=1, grid=(1,), in_specs=in_specs, out_specs=out_specs
        ),
        out_shape=out_shape,
        input_output_aliases=alias,
        compiler_params=pltpu.CompilerParams(vmem_limit_bytes=60 * MIB),
        cost_estimate=pl.CostEstimate(
            flops=20 * c2 * width * 4 * hidden, bytes_accessed=24 * MIB, transcendentals=c2 * 8 * hidden
        ),
    )(*ins)
    return outs[0:2], outs[2:4], outs[4:]


def expert_out(k, capacity, total, e, x_pair, wa, sa, downs, sd):
    tokens = x_pair[0].shape[0]
    width = sd.shape[1]
    c2 = wa.shape[3]
    last = x_pair[0].shape[1] // LANES - 1
    meta = pl.BlockSpec((tokens, LANES), lambda i, e: (0, last))
    return pl.pallas_call(
        functools.partial(expert_out_kernel, capacity, total),
        grid_spec=pltpu.PrefetchScalarGridSpec(
            num_scalar_prefetch=1,
            grid=(1,),
            in_specs=[
                meta,
                meta,
                pl.BlockSpec((4, 2, 1, c2, wa.shape[4]), lambda i, e: (0, 0, k, 0, 0)),
                pl.BlockSpec((1,) + sa.shape[1:], lambda i, e: (k, 0, 0)),
            ]
            + [whole(d.shape) for d in downs]
            + [whole(sd.shape)],
            out_specs=[whole((tokens, width))] * 2,
        ),
        out_shape=[jax.ShapeDtypeStruct((tokens, width), BF)] * 2,
        compiler_params=pltpu.CompilerParams(vmem_limit_bytes=40 * MIB),
        cost_estimate=pl.CostEstimate(
            flops=4 * c2 * width * 4 * wa.shape[4], bytes_accessed=10 * MIB, transcendentals=0
        ),
    )(e, *x_pair, wa, sa, *downs, sd)


def dispatch_kernel(capacity, total, x_ref, g0_ref, g1_ref, *refs):
    experts = refs[0:4]
    sg_ref, su_ref, sd_ref = refs[4:7]
    dx_ref, near_ref, far_ref, sgg_ref, sdg_ref, xr_ref, gr_ref, gu_ref, wa_ref = refs[7:16]
    xbuf, sbuf, tbuf, wgu, wd = refs[16:21]
    rx_s, rx_r, sx_s, sx_r, sr_s, sr_r, rt_s, rt_r, w_sem = refs[21:]
    k = pl.program_id(0)
    stages = xbuf.shape[0]
    tokens, width = x_ref.shape[0], sg_ref.shape[0]
    hidden = experts[0].shape[1] // 3
    wide = wd.shape[1] // 4
    c = capacity
    e, h = lax.axis_index("ep"), lax.axis_index("hp")
    n = 2 * stages
    right, left = lax.rem(e + 2, n), lax.rem(e + n - 2, n)
    pair = e + 1 - 2 * lax.rem(e, 2)

    def send(src, dst, s, r, i, where):
        return pltpu.make_async_remote_copy(
            src_ref=src,
            dst_ref=dst,
            send_sem=s.at[i],
            recv_sem=r.at[i],
            device_id=(where, h),
            device_id_type=pl.DeviceIdType.MESH,
        )

    def ring_x(i):
        return send(xbuf.at[i, 0], xbuf.at[i + 1, 0], rx_s, rx_r, i, right)

    def swap_x(i):
        return send(xbuf.at[i, 0], xbuf.at[i, 1], sx_s, sx_r, i, pair)

    def swap_r(i):
        return send(xbuf.at[i, 1], sbuf.at[i], sr_s, sr_r, i, pair)

    def ring_t(i):
        return send(xbuf.at[i, 0], tbuf.at[i], rt_s, rt_r, i, right)

    @pl.when(k == 0)
    def _():
        barrier = pltpu.get_barrier_semaphore()
        for where in (right, left, pair):
            pl.semaphore_signal(
                barrier, inc=1, device_id=(where, h), device_id_type=pl.DeviceIdType.MESH
            )
        xbuf[0, 0] = x_ref[...]
        pl.semaphore_wait(barrier, 3)
        ring_x(0).start()
        swap_x(0).start()
        rest = wide - hidden
        copies = []
        for x in range(2):
            for r in range(4):
                for i, (to, at) in enumerate(((wgu, 2 * r), (wgu, 2 * r + 1), (wd, r))):
                    copy = pltpu.make_async_copy(
                        experts[r].at[x, pl.ds(i * hidden, hidden), :],
                        to.at[x, pl.ds(at * wide, hidden), :],
                        w_sem.at[len(copies)],
                    )
                    copy.start()
                    copies.append(copy)
                    to[x, at * wide + hidden : (at + 1) * wide, :] = jnp.zeros((rest, width), BF)
        for copy in copies:
            copy.wait()
        sgg_ref[...] = jnp.zeros_like(sgg_ref)
        sdg_ref[...] = jnp.zeros_like(sdg_ref)

    @pl.when(k < stages - 1)
    def _():
        ring_x(k).wait_recv()

    @pl.when(k < stages - 2)
    def _():
        ring_x(k + 1).start()

    @pl.when(k < stages - 1)
    def _():
        swap_x(k + 1).start()

    swap_x(k).wait_recv()

    x2 = jnp.concatenate([xbuf[k, j, :, :width] for j in range(2)], axis=0)
    gs = (g0_ref, g1_ref)
    g2 = jnp.concatenate([g[0] for g in gs], axis=0)
    hg, hu = dot(x2, sg_ref[...]), dot(x2, su_ref[...])
    ab = dot(g2, sd_ref[...], (1, 1))
    s = jax.nn.sigmoid(hg)
    silu = hg * s
    act = (silu * hu).astype(BF)
    gi = (ab * hu * (s * (1.0 + hg * (1.0 - s)))).astype(BF)
    ui = (ab * silu).astype(BF)
    sgg_ref[...] += dot(x2, jnp.concatenate([gi, ui], axis=1), (0, 0))
    sdg_ref[...] += dot(act, g2, (0, 0))
    dx = dot(gi, sg_ref[...], (1, 1)) + dot(ui, su_ref[...], (1, 1))
    totals = [dx[:tokens], dx[tokens:]]
    out = dot(act, sd_ref[...])
    outs = [out[:tokens], out[tokens:]]
    metas = [0.0, 0.0]
    lane = lax.broadcasted_iota(jnp.int32, (2 * c, LANES), 1)
    for x in range(2):
        col = 2 * e + x
        picks, weights = [], []
        for j in range(2):
            pick = pick_matrix(xbuf[k, j, :, width:], total + col, c)
            picks.append(pick)
            rows = dot(pick, xbuf[k, j], (0, 0))
            xr_ref[x, 0, j * c : (j + 1) * c, :] = rows[:, :width].astype(BF)
            weights.append(rows[:, width:])
            gr_ref[x, 0, j * c : (j + 1) * c, :] = dot(pick, gs[j][0], (0, 0)).astype(BF)
        w = jnp.concatenate(weights, axis=0)
        w = jnp.sum(jnp.where(lane == col, w, 0.0), axis=1, keepdims=True)
        xr, gr = xr_ref[x, 0], gr_ref[x, 0]
        wb = jnp.zeros((2 * c, 1), F32)
        for r in range(4):
            hgu = dot(xr, wgu[x, 2 * r * wide : 2 * (r + 1) * wide, :], (1, 1))
            ab = dot(gr, wd[x, r * wide : (r + 1) * wide, :], (1, 1))
            hg, hu = hgu[:, :wide], hgu[:, wide:]
            s = jax.nn.sigmoid(hg)
            silu = hg * s
            act = silu * hu
            wb = wb + jnp.sum(act * ab, axis=1, keepdims=True)
            ab = ab * w
            at = 2 * r * wide
            gu_ref[x, 0, :, at : at + wide] = (ab * hu * (s * (1.0 + hg * (1.0 - s)))).astype(BF)
            gu_ref[x, 0, :, at + wide : at + 2 * wide] = (ab * silu).astype(BF)
            wa_ref[x, 0, :, r * wide : (r + 1) * wide] = (act * w).astype(BF)
        dxr = dot(gu_ref[x, 0], wgu[x]).astype(BF)
        rows = dot(wa_ref[x, 0], wd[x]).astype(BF)
        high = wb.astype(BF).astype(F32)
        meta = jnp.where(lane == col, high, 0.0) + jnp.where(lane == total + col, wb - high, 0.0)
        meta = meta.astype(BF)
        for j in range(2):
            span = slice(j * c, (j + 1) * c)
            totals[j] = totals[j] + dot(picks[j], dxr[span])
            outs[j] = outs[j] + dot(picks[j], rows[span])
            metas[j] = metas[j] + dot(picks[j], meta[span])

    @pl.when(k < stages - 1)
    def _():
        ring_x(k).wait_send()

    swap_x(k).wait_send()
    for j in range(2):
        xbuf[k, j, :, :width] = totals[j].astype(BF)
        xbuf[k, j, :, width:] = metas[j].astype(BF)
        (near_ref, far_ref)[j][0] = outs[j].astype(BF)

    @pl.when(k >= 1)
    def _():
        swap_r(k).start()

    def advance(i, first):
        swap_r(i).wait_recv()
        here = xbuf[i, 0].astype(F32) + sbuf[i].astype(F32)
        if not first:
            ring_t(i - 1).wait_recv()
            here = here + tbuf[i - 1].astype(F32)
        xbuf[i, 0] = here.astype(BF)
        ring_t(i).start()

    for i in range(1, stages - 1):

        @pl.when(k == i + 1)
        def _(i=i):
            advance(i, i == 1)

    @pl.when(k == stages - 1)
    def _():
        swap_r(0).start()
        advance(stages - 1, stages == 2)
        swap_r(0).wait_recv()
        ring_t(stages - 1).wait_recv()
        dx_ref[...] = (
            xbuf[0, 0].astype(F32) + sbuf[0].astype(F32) + tbuf[stages - 1].astype(F32)
        )
        for i in range(stages):
            swap_r(i).wait_send()
        for i in range(1, stages):
            ring_t(i).wait_send()


def dispatch(capacity, total, x_ext, g_near, g_far, experts, sg, su, sd):
    stages = g_near.shape[0]
    tokens, ext = x_ext.shape
    width, shared = sg.shape
    hidden = experts[0].shape[1] // 3
    wide = -(-hidden // LANES) * LANES
    c2 = 2 * capacity
    once = pl.Buffered(1)

    def fixed(shape):
        return pl.BlockSpec(shape, lambda k: (0,) * len(shape), pipeline_mode=once)

    def per_stage(shape):
        return pl.BlockSpec(shape, lambda k: (0, k, 0, 0), pipeline_mode=once)

    anywhere = pl.BlockSpec(memory_space=pl.ANY)
    return pl.pallas_call(
        functools.partial(dispatch_kernel, capacity, total),
        grid=(stages,),
        in_specs=[
            fixed((tokens, ext)),
            pl.BlockSpec((1, tokens, width), lambda k: (k, 0, 0)),
            pl.BlockSpec((1, tokens, width), lambda k: (k, 0, 0)),
        ]
        + [anywhere] * 4
        + [fixed(sg.shape), fixed(su.shape), fixed(sd.shape)],
        out_specs=[
            fixed((tokens, ext)),
            pl.BlockSpec((1, tokens, width), lambda k: (k, 0, 0), pipeline_mode=once),
            pl.BlockSpec((1, tokens, width), lambda k: (k, 0, 0), pipeline_mode=once),
            fixed((width, 2 * shared)),
            fixed((shared, width)),
            per_stage((2, 1, c2, width)),
            per_stage((2, 1, c2, width)),
            per_stage((2, 1, c2, 8 * wide)),
            per_stage((2, 1, c2, 4 * wide)),
        ],
        out_shape=[
            jax.ShapeDtypeStruct((tokens, ext), F32),
            jax.ShapeDtypeStruct((stages, tokens, width), BF),
            jax.ShapeDtypeStruct((stages, tokens, width), BF),
            jax.ShapeDtypeStruct((width, 2 * shared), F32),
            jax.ShapeDtypeStruct((shared, width), F32),
            jax.ShapeDtypeStruct((2, stages, c2, width), BF),
            jax.ShapeDtypeStruct((2, stages, c2, width), BF),
            jax.ShapeDtypeStruct((2, stages, c2, 8 * wide), BF),
            jax.ShapeDtypeStruct((2, stages, c2, 4 * wide), BF),
        ],
        scratch_shapes=[
            pltpu.VMEM((stages, 2, tokens, ext), BF),
            pltpu.VMEM((stages, tokens, ext), BF),
            pltpu.VMEM((stages, tokens, ext), BF),
            pltpu.VMEM((2, 8 * wide, width), BF),
            pltpu.VMEM((2, 4 * wide, width), BF),
        ]
        + [pltpu.SemaphoreType.DMA((stages,))] * 8
        + [pltpu.SemaphoreType.DMA((24,))],
        compiler_params=pltpu.CompilerParams(
            vmem_limit_bytes=63 * MIB, collective_id=0, has_side_effects=True
        ),
        cost_estimate=pl.CostEstimate(
            flops=24 * c2 * stages * width * 4 * hidden,
            bytes_accessed=80 * MIB,
            transcendentals=stages * c2 * 8 * hidden,
        ),
    )(x_ext, g_near, g_far, *experts, sg, su, sd)


def mesh_copy(src, dst, s, r, i, where):
    return pltpu.make_async_remote_copy(
        src_ref=src,
        dst_ref=dst,
        send_sem=s.at[i],
        recv_sem=r.at[i],
        device_id=where,
        device_id_type=pl.DeviceIdType.MESH,
    )


def greet(peers):
    barrier = pltpu.get_barrier_semaphore()
    for where in peers:
        pl.semaphore_signal(barrier, inc=1, device_id=where, device_id_type=pl.DeviceIdType.MESH)
    pl.semaphore_wait(barrier, len(peers))


def front_kernel(large, count, *refs):
    tok_ref, exp_ref, cot_ref = refs[0:3]
    ins = refs[3 : 3 + count]
    far_ref, expo_ref, g_ref = refs[3 + count : 6 + count]
    outs = refs[6 + count : 6 + 2 * count]
    y_s, y_r, c_s, c_r, f_s, f_r, p_s, p_r, q_s, q_r, l_sem, rg_s, rg_r = refs[6 + 2 * count :]
    stages = g_ref.shape[0]
    n = 2 * stages
    e, h = lax.axis_index("ep"), lax.axis_index("hp")
    x = lax.rem(e, 2)
    h_core, h_far = h + 1 - 2 * lax.rem(h, 2), lax.rem(h + 2, 4)
    core, far = (e, h_core), (e, h_far)
    right, left = (lax.rem(e + 2, n), h), (lax.rem(e + n - 2, n), h)
    pair = (e + 1 - 2 * x, h)
    greet((core, far, right, left, pair))

    def ring_g(k):
        src = cot_ref if k == 0 else g_ref.at[k]
        return mesh_copy(src, g_ref.at[k + 1], rg_s, rg_r, k, right)

    def part(i, other=False):
        rows = ins[i].shape[0] // 2
        return pl.ds((1 - x if other else x) * rows, rows)

    over_y, over_pair, onward, onward_too = [], [], [], []
    for i, v in enumerate(ins):
        o = outs[i]
        if i < large:
            mine, theirs = part(i), part(i, True)
            over_y.append(mesh_copy(v.at[mine], o.at[h, mine], y_s, y_r, i, far))
            got, rest = o.at[h_far, mine], o.at[h_far, theirs]
            over_pair.append(mesh_copy(got, got, p_s, p_r, i, pair))
            onward.append(mesh_copy(got, got, f_s, f_r, i, core))
            onward_too.append(mesh_copy(rest, rest, q_s, q_r, i, core))
        else:
            over_y.append(mesh_copy(v, o.at[h], y_s, y_r, i, far))
            onward.append(mesh_copy(o.at[h_far], o.at[h_far], f_s, f_r, i, core))
    over_y.append(mesh_copy(tok_ref, far_ref, y_s, y_r, count, far))
    over_core = [mesh_copy(v, outs[i].at[h], c_s, c_r, i, core) for i, v in enumerate(ins)]
    over_core.append(mesh_copy(exp_ref, expo_ref, c_s, c_r, count, core))
    local = [pltpu.make_async_copy(v, outs[i].at[h], l_sem.at[i]) for i, v in enumerate(ins)]
    local.append(pltpu.make_async_copy(cot_ref, g_ref.at[0], l_sem.at[count]))
    for copy in over_y:
        copy.start()
    ring_g(0).start()
    for copy in over_core + local:
        copy.start()
    for k in range(max(stages - 1, large)):
        if k < large:
            over_y[k].wait_recv()
            over_pair[k].start()
            onward[k].start()
        if k < stages - 1:
            ring_g(k).wait_recv()
            if k + 1 < stages - 1:
                ring_g(k + 1).start()
    for k in range(large, count):
        over_y[k].wait_recv()
        onward[k].start()
    over_y[count].wait_recv()
    for k in range(large):
        over_pair[k].wait_recv()
        onward_too[k].start()
    for copy in over_y + over_pair + [ring_g(k) for k in range(stages - 1)]:
        copy.wait_send()
    for copy in over_core + onward + onward_too + local:
        copy.wait()


def front(stages, tokens, experts, cotangent, blocks, large):
    count = len(blocks)
    anywhere, vmem = (pl.BlockSpec(memory_space=m) for m in (pl.ANY, pltpu.VMEM))
    dma = pltpu.SemaphoreType.DMA
    return pl.pallas_call(
        functools.partial(front_kernel, large, count),
        in_specs=[anywhere] * 2 + [vmem] * (1 + count),
        out_specs=[anywhere] * (3 + count),
        out_shape=[
            jax.ShapeDtypeStruct(tokens.shape, BF),
            jax.ShapeDtypeStruct(experts.shape, BF),
            jax.ShapeDtypeStruct((stages,) + cotangent.shape, BF),
        ]
        + [jax.ShapeDtypeStruct((4,) + v.shape, BF) for v in blocks],
        scratch_shapes=[dma((count + 1,))] * 4
        + [dma((count,))] * 6
        + [dma((count + 1,))]
        + [dma((stages,))] * 2,
        compiler_params=pltpu.CompilerParams(
            vmem_limit_bytes=32 * MIB, collective_id=1, has_side_effects=True
        ),
        cost_estimate=pl.CostEstimate(flops=0, bytes_accessed=120 * MIB, transcendentals=0),
    )(tokens, experts, cotangent, *blocks)


def tail_kernel(
    m0,
    m1,
    m2,
    m3,
    sg_ref,
    sd_ref,
    sm_ref,
    fb_ref,
    tok_ref,
    gain_ref,
    first_ref,
    mid_ref,
    spread_ref,
    stack_ref,
    out_ref,
    sgout_ref,
    suout_ref,
    sdout_ref,
    smout_ref,
    tokout_ref,
    crecv,
    ysend,
    yrecv,
    acc,
    xrecv,
    zrecv,
    fin,
    sg_c,
    sg_y,
    sg_yr,
    sg_fin,
    sd_c,
    sd_y,
    sd_yr,
    sd_fin,
    g_acc,
    g_recv,
    f_recv,
    c_s,
    c_r,
    y_s,
    y_r,
    x_s,
    x_r,
    z_s,
    z_r,
    za_s,
    za_r,
    xa_s,
    xa_r,
    s_s,
    s_r,
    d_s,
    d_r,
    g_s,
    g_r,
    f_s,
    f_r,
):
    mats = (m0, m1, m2, m3)
    chunks, part = acc.shape[0], acc.shape[3]
    half = m0.shape[3]
    e, h = lax.axis_index("ep"), lax.axis_index("hp")
    x, z = lax.rem(e, 2), e // 2
    c, y = lax.rem(h, 2), h // 2
    core, far = (e, h + 1 - 2 * c), (e, lax.rem(h + 2, 4))
    pair = (e + 1 - 2 * x, h)
    up = [None] + [(2 * lax.rem(z + s, 4) + x, h) for s in range(1, 4)]
    next_z = (2 * (z + 1 - 2 * lax.rem(z, 2)) + x, h)
    greet([core, far, pair] + up[1:])

    def rows(j):
        return pl.ds(j * part, part)

    def over_core(j, m):
        return mesh_copy(
            mats[m].at[:, 1 - c, :, rows(j), :],
            crecv.at[m, :, :, rows(j), :],
            c_s,
            c_r,
            4 * j + m,
            core,
        )

    def over_y(j):
        return mesh_copy(ysend.at[j], yrecv.at[j], y_s, y_r, j, far)

    def over_x(j):
        return mesh_copy(acc.at[j, :, 1 - x], xrecv.at[j], x_s, x_r, j, pair)

    def over_z(j, s):
        return mesh_copy(
            acc.at[j, lax.rem(z + s, 4), x], zrecv.at[j, s - 1], z_s, z_r, 3 * j + s - 1, up[s]
        )

    def back_z(j, s):
        return mesh_copy(fin.at[j, z, x], fin.at[j, z, x], za_s, za_r, 3 * j + s - 1, up[s])

    def back_x(j):
        return mesh_copy(fin.at[j, :, x], fin.at[j, :, x], xa_s, xa_r, j, pair)

    def add_core(j):
        for m in range(4):
            over_core(j, m).wait_recv()
            for at, to in ((y, acc), (1 - y, ysend)):
                total = mats[m][at, c, :, rows(j), :].astype(F32)
                to[j, m] = (total + crecv[m, at, :, rows(j), :].astype(F32)).astype(BF)
        over_y(j).start()

    def add_y(j):
        over_y(j).wait_recv()
        acc[j] = (acc[j].astype(F32) + yrecv[j].astype(F32)).astype(BF)
        over_x(j).start()

    def add_x(j):
        over_x(j).wait_recv()
        acc[j, :, x] = (acc[j, :, x].astype(F32) + xrecv[j].astype(F32)).astype(BF)
        for s in range(1, 4):
            over_z(j, s).start()

    def add_z(j):
        total = acc[j, z, x].astype(F32)
        for s in range(1, 4):
            over_z(j, s).wait_recv()
            total = total + zrecv[j, s - 1].astype(F32)
        fin[j, z, x] = total.astype(BF)
        for s in range(1, 4):
            back_z(j, s).start()

    def end_z(j):
        for s in range(1, 4):
            back_z(j, s).wait_recv()
        back_x(j).start()

    def end_x(j):
        back_x(j).wait_recv()
        for m in range(4):
            for i in range(2):
                out_ref[m, i * half + j * part : i * half + (j + 1) * part, :] = fin[j, m, i]

    class Flow:
        def __init__(self, ref, got, to_far, from_far, fin, s, r):
            self.ref, self.got, self.to_far, self.from_far, self.fin = ref, got, to_far, from_far, fin
            self.core = mesh_copy(ref.at[:, 1 - c], got, s, r, 0, core)
            self.far = mesh_copy(to_far, from_far, s, r, 1, far)
            self.up = [
                mesh_copy(fin.at[x, z], fin.at[x, z], s, r, 1 + k, up[k]) for k in range(1, 4)
            ]
            self.pair = mesh_copy(fin.at[x], fin.at[x], s, r, 5, pair)
            self.all = [self.core, self.far, self.pair] + self.up

        def step(self, t):
            if t == 0:
                self.core.wait_recv()
                total = self.ref[1 - y, c].astype(F32) + self.got[1 - y].astype(F32)
                self.to_far[...] = total.astype(BF)
                self.far.start()
            if t == 2:
                self.far.wait_recv()
                total = self.ref[y, c].astype(F32) + self.got[y].astype(F32)
                self.fin[x, z] = (total + self.from_far[...].astype(F32)).astype(BF)
                for copy in self.up:
                    copy.start()
            if t == 4:
                for copy in self.up:
                    copy.wait_recv()
                self.pair.start()

    flows = [
        Flow(sg_ref, sg_c, sg_y, sg_yr, sg_fin, s_s, s_r),
        Flow(sd_ref, sd_c, sd_y, sd_yr, sd_fin, d_s, d_r),
    ]
    route = (core, far, pair, next_z, up[2])
    small = [
        mesh_copy(g_acc.at[i], g_recv.at[i], g_s, g_r, i, route[i]) for i in range(len(route))
    ]
    back = mesh_copy(fb_ref, f_recv, f_s, f_r, 0, far)

    def side(t):
        for flow in flows:
            flow.step(t)
        if t < len(small):
            small[t].wait_recv()
            g_acc[t + 1] = g_acc[t] + g_recv[t]
            if t + 1 < len(small):
                small[t + 1].start()
        if t == 6:
            back.wait_recv()
            first_back = first_ref[...] + f_recv[...].astype(F32)
            values = tok_ref[...].astype(F32)
            to_tokens = norm_back(values, rms(values), gain_ref[...], first_back)
            tokout_ref[...] = mid_ref[...] + to_tokens
        if t == 8:
            for flow in flows:
                flow.pair.wait_recv()
            lanes = sg_fin.shape[3] // 2
            gate = up_ = down = 0.0
            for k in range(8):
                block = sg_fin[k % 2, k // 2]
                gate = gate + dot(block[:, :lanes], spread_ref[k])
                up_ = up_ + dot(block[:, lanes:], spread_ref[k])
                down = down + dot(stack_ref[k], sd_fin[k % 2, k // 2])
            sgout_ref[...] = gate
            suout_ref[...] = up_
            sdout_ref[...] = down

    g_acc[0] = sm_ref[...]
    for m in range(4):
        over_core(0, m).start()
    back.start()
    for flow in flows:
        flow.core.start()
    small[0].start()
    for j in range(1, chunks):
        for m in range(4):
            over_core(j, m).start()
    steps = (add_core, add_y, add_x, add_z, end_z, end_x)
    for t in range(chunks + len(steps) - 1):
        for p in reversed(range(len(steps))):
            if 0 <= t - p < chunks:
                steps[p](t - p)
        side(t)
    smout_ref[...] = g_acc[len(small)]
    back.wait_send()
    for copy in flows[0].all + flows[1].all + small:
        copy.wait_send()
    for j in range(chunks):
        for m in range(4):
            over_core(j, m).wait_send()
        for copy in (over_y(j), over_x(j), back_x(j)):
            copy.wait_send()
        for s in range(1, 4):
            over_z(j, s).wait_send()
            back_z(j, s).wait_send()


def tail(mats, sgg, sdg, small, share, tokens, gain, first_back, middle_back, spread, stack):
    width = mats[0].shape[1]
    half = width // 8
    part = 16
    chunks = half // part
    dma = pltpu.SemaphoreType.DMA
    vmem = pl.BlockSpec(memory_space=pltpu.VMEM)

    def buffers(shape):
        return [
            pltpu.VMEM((2,) + shape, BF),
            pltpu.VMEM(shape, BF),
            pltpu.VMEM(shape, BF),
            pltpu.VMEM((2, 4) + shape, BF),
        ]

    return pl.pallas_call(
        tail_kernel,
        in_specs=[vmem] * 14,
        out_specs=[vmem] * 6,
        out_shape=[
            jax.ShapeDtypeStruct((4, 2 * half, width), BF),
            jax.ShapeDtypeStruct((2 * half, spread.shape[2]), F32),
            jax.ShapeDtypeStruct((2 * half, spread.shape[2]), F32),
            jax.ShapeDtypeStruct((stack.shape[1], width), F32),
            jax.ShapeDtypeStruct(small.shape, F32),
            jax.ShapeDtypeStruct(tokens.shape, F32),
        ],
        scratch_shapes=[
            pltpu.VMEM((4, 2, 2, half, width), BF),
            pltpu.VMEM((chunks, 4, 2, part, width), BF),
            pltpu.VMEM((chunks, 4, 2, part, width), BF),
            pltpu.VMEM((chunks, 4, 2, part, width), BF),
            pltpu.VMEM((chunks, 4, part, width), BF),
            pltpu.VMEM((chunks, 3, part, width), BF),
            pltpu.VMEM((chunks, 4, 2, part, width), BF),
        ]
        + buffers(sgg.shape[2:])
        + buffers(sdg.shape[2:])
        + [
            pltpu.VMEM((6,) + small.shape, F32),
            pltpu.VMEM((5,) + small.shape, F32),
            pltpu.VMEM(share.shape, BF),
        ]
        + [dma((4 * chunks,))] * 2
        + [dma((chunks,))] * 4
        + [dma((3 * chunks,))] * 4
        + [dma((chunks,))] * 2
        + [dma((6,))] * 4
        + [dma((5,))] * 2
        + [dma((1,))] * 2,
        compiler_params=pltpu.CompilerParams(
            vmem_limit_bytes=62 * MIB, collective_id=2, has_side_effects=True
        ),
        cost_estimate=pl.CostEstimate(flops=0, bytes_accessed=300 * MIB, transcendentals=0),
    )(
        *[m.reshape(2, 2, 2, half, width) for m in mats],
        sgg,
        sdg,
        small,
        share,
        tokens,
        gain,
        first_back,
        middle_back,
        spread,
        stack,
    )


def rms(values):
    return lax.rsqrt(jnp.mean(values * values, axis=-1, keepdims=True) + epsilon)


def norm_back(values, inv, gain, upstream):
    weighted = upstream * gain
    inner = jnp.mean(weighted * values, axis=-1, keepdims=True)
    return weighted * inv - values * (inv * inv * inv * inner)


def rotary_tables(positions):
    exponent = jnp.arange(HD // 2, dtype=F32) * (2.0 / HD)
    theta = positions.astype(F32)[:, None] * jnp.power(10000.0, -exponent)[None, :]
    cosine, sine = jnp.cos(theta), jnp.sin(theta)
    return jnp.concatenate([cosine, cosine], axis=1), jnp.concatenate([-sine, sine], axis=1)


def per_device(
    tokens,
    attn_gain,
    query_weight,
    key_weight,
    value_weight,
    out_weight,
    ffn_gain,
    router_weight,
    shared_gate,
    shared_up,
    shared_down,
    expert_gate,
    expert_up,
    expert_down,
    routes,
    keep_mask,
    cotangent,
):
    e, h = lax.axis_index("ep"), lax.axis_index("hp")
    ep = lax.axis_size("ep")
    stages = ep // 2
    rows, width = tokens.shape
    top = routes.shape[1]
    total = router_weight.shape[1]
    capacity = -(-(5 * rows * top // (4 * total)) // 16) * 16
    e_arr, h_arr = jnp.full((1,), e, jnp.int32), jnp.full((1,), h, jnp.int32)

    units = shared_down.shape[0] // ep
    pad = -(-units // 16) * 16
    tiny = [attn_gain[:, None], ffn_gain[:, None], router_weight]
    small = jnp.concatenate(tiny + [jnp.zeros((width // 4, LANES - 2 - total), BF)], axis=1)

    def mine(v):
        v = v.reshape(width // 4, 4, -1)
        v = lax.dynamic_slice_in_dim(v, e * units, units, axis=2).reshape(width // 4, 4 * units)
        return jnp.pad(v, ((0, 0), (0, LANES - 4 * units)))

    small = jnp.concatenate([small, mine(shared_gate), mine(shared_up)], axis=1)
    sd = lax.dynamic_slice_in_dim(shared_down, e * units, units, axis=0)
    sd = jnp.pad(sd, ((0, pad - units), (0, 0)))
    blocks = [key_weight, value_weight, query_weight, out_weight, small, sd]
    experts = jnp.concatenate(
        [jnp.swapaxes(expert_gate, 1, 2), jnp.swapaxes(expert_up, 1, 2), expert_down], axis=1
    )
    fused = stages == 4
    if fused:
        far_tokens, experts_core, g_near, *blocks = front(
            stages, tokens, experts, cotangent, blocks, 4
        )
        experts_far = swap_y(after(experts, blocks[0]))
        g_far = swap_pair(g_near)
    else:
        far_tokens = swap_y(tokens)
        blocks = [absolute(jnp.stack(gather_hp(v)), h, 0) for v in blocks]
        g_blocks = gather_ep(cotangent)
        experts = gather_hp(experts)
    k_w, v_w, q_w, o_w, small = (v.reshape(width, v.shape[2]) for v in blocks[:5])
    gain_one = small[:, 0].astype(F32)[None, :]
    gain_two = small[:, 1].astype(F32)[None, :]
    router = small[:, 2 : 2 + total]
    sg, su = small[:, LANES : 2 * LANES], small[:, 2 * LANES :]
    sd = blocks[5][:, :units].reshape(4 * units, width)
    sd = jnp.pad(sd, ((0, LANES - 4 * units), (0, 0)))

    expert = jnp.arange(total, dtype=jnp.int32)
    hit_each = routes[:, :, None] == expert[None, None, :]
    hit = jnp.any(hit_each, axis=1)
    kept = jnp.sum(jnp.where(hit_each, keep_mask[:, :, None], 0), axis=1)
    below = (jnp.arange(rows)[:, None] > jnp.arange(rows)[None, :]).astype(BF)
    place = jnp.where(hit, dot(below, hit.astype(BF)), -1.0)
    kept = kept.astype(F32)

    pos = jnp.arange(rows, dtype=jnp.int32)
    pos = jnp.concatenate([(h ^ i) * rows + pos for i in (0, 2, 1, 3)])
    cosine, sine = rotary_tables(pos)
    residual = tokens.astype(F32)
    table = cosine[: 2 * rows], sine[: 2 * rows]
    first_in, kv_a, query = project(tokens, far_tokens, gain_one, k_w, v_w, q_w, *table)
    kv_b = swap_core(kv_a)
    mixed, lse = attend(h_arr, query, kv_a, kv_b)
    middle = residual + dot(mixed, o_w)
    inv_two = rms(middle)
    second_in = (middle * inv_two * gain_two).astype(BF)

    logits = jnp.where(hit, dot(second_in, router), -1e30)
    gates_of = jnp.where(hit, jnp.exp(logits - jnp.max(logits, axis=1, keepdims=True)), 0.0)
    gates_of = gates_of / jnp.sum(gates_of, axis=1, keepdims=True)
    pair_weight = gates_of * kept
    x_ext = jnp.concatenate(
        [
            second_in,
            pair_weight.astype(BF),
            place.astype(BF),
            jnp.zeros((rows, LANES - 2 * total), BF),
        ],
        axis=1,
    )

    flat = (2, ep * capacity)

    hidden = expert_down.shape[1]

    def expert_grad(left, right):
        return jnp.einsum("xna,xnb->xab", left, right, preferred_element_type=F32)

    if fused:
        experts = [
            experts,
            experts_far,
            experts_core,
            swap_core(after(experts_far, mixed)),
        ]
        dx_sum, near, far, sgg, sdg, xr, gr, gu, wa = dispatch(
            capacity, total, x_ext, g_near, g_far, experts, sg, su, sd
        )
        far = swap_pair(far)
        wide = wa.shape[3] // 4
        xr, gr, gu, wa = (v.reshape(flat + (v.shape[-1],)) for v in (xr, gr, gu, wa))
        gu = expert_grad(gu, xr).astype(BF)
        wa = expert_grad(wa, gr).astype(BF)
        dx_sum = after(dx_sum, gu, wa)

        def piece(r):
            starts = ((gu, 2 * r * wide), (gu, (2 * r + 1) * wide), (wa, r * wide))
            return jnp.concatenate([v[:, a : a + hidden] for v, a in starts], axis=1)

        piece_near = [piece(r) for r in (0, 1)]
        piece_core = swap_core(jnp.stack([piece(r) for r in (2, 3)]))
        piece_sum = (piece_near[1].astype(F32) + piece_core[1].astype(F32)).astype(BF)
        piece_far = swap_y(piece_sum)
    else:
        x_blocks = gather_ep(after(x_ext, g_blocks))
        carry = (jnp.zeros((width, 2 * LANES), F32), jnp.zeros((LANES, width), F32))
        bufs, dx_parts = None, []
        gates, ups = (
            [jnp.swapaxes(v[:, i * hidden : (i + 1) * hidden], 1, 2) for v in experts]
            for i in (0, 1)
        )
        downs = [v[:, 2 * hidden :] for v in experts]
        for k in range(stages):
            dx, carry, bufs = expert_stage(
                k,
                stages,
                capacity,
                total,
                e_arr,
                x_blocks[k],
                g_blocks[k],
                gates,
                ups,
                downs,
                sg,
                su,
                sd,
                carry,
                bufs,
            )
            dx_parts.append(dx)
        dx_sum = scatter_ep(dx_parts)
        sgg, sdg = carry
        sa, xr, gr, gi, ui, wa = bufs
        out_parts = [
            expert_out(k, capacity, total, e_arr, x_blocks[k], wa, sa, downs, sd)
            for k in range(stages)
        ]
        xr, gr = xr.reshape(flat + (width,)), gr.reshape(flat + (width,))
        gi, ui, wa = (v.reshape((4,) + flat + (v.shape[-1],)) for v in (gi, ui, wa))
        routed = scatter_ep(after(out_parts, dx_sum))
        expert_sum = scatter_hp(
            [
                jnp.concatenate(
                    [
                        expert_grad(gi[r], xr),
                        expert_grad(ui[r], xr),
                        expert_grad(wa[r], gr),
                    ],
                    axis=1,
                )
                for r in range(4)
            ]
        )

    grad_out = cotangent.astype(F32)
    weight_back = dx_sum[:, width : width + total] + dx_sum[:, width + total : width + 2 * total]
    gate_back = weight_back * kept
    chosen_back = gates_of * (gate_back - jnp.sum(gates_of * gate_back, axis=1, keepdims=True))
    logits_back = chosen_back.astype(BF)
    router_part = dot(logits_back, second_in, (0, 0))
    second_back = dx_sum[:, :width] + dot(logits_back, router, (1, 1))
    gain_two_part = jnp.sum(second_back * middle * inv_two, axis=0)
    middle_back = grad_out + norm_back(middle, inv_two, gain_two, second_back)
    attn_back = middle_back.astype(BF)
    counts_part = jnp.pad(jnp.sum(kept, axis=0), (0, width - total))

    mixed_back = dot(attn_back, o_w, (1, 1)).astype(BF)
    if fused:
        mixed_back = after(mixed_back, piece_sum)
    out_part = dot(mixed, attn_back, (0, 0))
    query_raw, near_back, far_back = attend_back(
        h_arr, query, kv_a, kv_b, mixed_back, lse, cosine, sine
    )
    kv_raw = (near_back + swap_core(far_back).astype(F32)).astype(BF)
    key_raw, value_raw = kv_raw[0], kv_raw[1]
    if fused:
        both_out = near.astype(F32) + after(far, query_raw).astype(F32)
        low_out = both_out.astype(BF)
        routed = [shift(low_out[k], stages - k) for k in range(1, stages)]
    kv_back = dot(key_raw, k_w, (1, 1)) + dot(value_raw, v_w, (1, 1))
    q_back = dot(query_raw, q_w, (1, 1))
    share = kv_back[rows:].astype(BF)
    q_part = dot(first_in[:rows], query_raw, (0, 0))
    k_part = dot(first_in, key_raw, (0, 0))
    v_part = dot(first_in, value_raw, (0, 0))
    first_back = kv_back[:rows] + q_back
    gain_one_part = jnp.zeros((1, width), F32)
    for values, upstream in ((tokens, first_back), (far_tokens, kv_back[rows:])):
        values = values.astype(F32)
        gain_one_part += jnp.sum(upstream * values * rms(values), axis=0, keepdims=True)
    sums = [router_part, gain_two_part[None, :], counts_part[None, :], gain_one_part]
    sums = jnp.concatenate(sums + [jnp.zeros((-(total + 3) % 8, width), F32)], axis=0)
    parts = [q_part, k_part, v_part, out_part]

    sgg = sgg.reshape(4, width // 4, 2 * LANES)
    sdg = sdg[: 4 * units].reshape(4, units, width)
    unit = jnp.arange(LANES)
    to = (unit // units) * (ep * units) + unit % units
    to = jnp.where(unit < 4 * units, to, -ep * units)[None, :, None]
    block = jnp.arange(ep)[:, None, None] * units
    spread = (to + block == jnp.arange(4 * ep * units)[None, None, :]).astype(BF)
    if fused:
        sdg = jnp.pad(sdg, ((0, 0), (0, pad - units), (0, 0))).astype(BF)
        at = jnp.where(jnp.arange(pad) < units, jnp.arange(pad), -ep * units)[None, None, :]
        stack = (at + block == jnp.arange(ep * units)[None, :, None]).astype(BF)
        out, sgate_grad, sup_grad, sdown_grad, sums, tokens_grad = tail(
            [v.astype(BF) for v in parts],
            sgg.astype(BF).reshape(2, 2, width // 4, 2 * LANES),
            sdg.reshape(2, 2, pad, width),
            after(sums, piece_far),
            share,
            tokens,
            gain_one,
            first_back,
            middle_back,
            spread,
            stack,
        )
        grads = [out[i].astype(F32) for i in range(4)]
        routed = after(routed, sums)
        routed = both_out[0] + sum(v.astype(F32) for v in routed)
        piece_far = after(piece_far, sums)
        expert_sum = sum(v.astype(F32) for v in (piece_near[0], piece_core[0], piece_far))
    else:

        def over_hp(v):
            return scatter_hp(jnp.split(relative(v, h, 0), 4, axis=0))

        grads = [sum_ep(over_hp(v), e) for v in parts]
        sums = sum_all_small(sums)
        first_back = first_back + swap_y(share).astype(F32)
        tokens_grad = middle_back + norm_back(residual, rms(residual), gain_one, first_back)
        sgg, sdg = (
            spread_ep(over_hp(v)[0].astype(BF), e) for v in (sgg, sdg)
        )
        sgate_grad, sup_grad = (
            jnp.einsum("kra,kan->rn", v, spread, preferred_element_type=F32)
            for v in (sgg[:, :, :LANES], sgg[:, :, LANES:])
        )
        sdown_grad = sdg.reshape(ep * units, width).astype(F32)
    layer = (middle + routed).astype(BF)
    gate_grad, up_grad = (
        jnp.swapaxes(expert_sum[:, i * hidden : (i + 1) * hidden], 1, 2) for i in (0, 1)
    )
    down_grad = expert_sum[:, 2 * hidden :]

    def own(v, n):
        return lax.dynamic_slice_in_dim(v, h * n, n, axis=0)

    return (
        layer,
        tokens_grad,
        own(sums[total + 2], width // 4),
        *grads,
        own(sums[total], width // 4),
        own(sums[:total].T, width // 4),
        sgate_grad,
        sup_grad,
        sdown_grad,
        gate_grad,
        up_grad,
        down_grad,
        own(sums[total + 1], total // 4).astype(jnp.int32),
    )


def solution(mesh):
    row, ep_hp = P("hp", None), P(("ep", "hp"), None)
    return jax.shard_map(
        per_device,
        mesh=mesh,
        in_specs=(
            ep_hp,
            P("hp"),
            row,
            row,
            row,
            row,
            P("hp"),
            row,
            row,
            row,
            row,
            P("ep", None, "hp"),
            P("ep", None, "hp"),
            P("ep", "hp", None),
            ep_hp,
            ep_hp,
            ep_hp,
        ),
        out_specs=(
            ep_hp,
            ep_hp,
            P("hp"),
            row,
            row,
            row,
            row,
            P("hp"),
            row,
            row,
            row,
            row,
            P("ep", None, "hp"),
            P("ep", None, "hp"),
            P("ep", "hp", None),
            P("hp"),
        ),
        check_vma=False,
    )
```

```python
import functools

import jax
import jax.numpy as jnp
from jax import lax
from jax.experimental import pallas as pl
from jax.experimental.pallas import tpu as pltpu
from jax.sharding import PartitionSpec as P

H = 10
HD = 128
LANES = 128
BF = jnp.bfloat16
F32 = jnp.float32
epsilon = 1e-06
MIB = 1 << 20


def dot(left, right, over=(1, 0)):
    return lax.dot_general(
        left, right, (((over[0],), (over[1],)), ((), ())), preferred_element_type=F32
    )


def swap_core(v):
    return lax.ppermute(v, "hp", [(i, i ^ 1) for i in range(4)])


def swap_y(v):
    return lax.ppermute(v, "hp", [(i, i ^ 2) for i in range(4)])


def swap_pair(v):
    n = lax.axis_size("ep")
    return lax.ppermute(v, "ep", [(i, i ^ 1) for i in range(n)])


def ring(v):
    n = lax.axis_size("ep")
    return lax.ppermute(v, "ep", [(i, (i + 2) % n) for i in range(n)])


def shift(v, steps):
    n = lax.axis_size("ep")
    return lax.ppermute(v, "ep", [(i, (i + 2 * steps) % n) for i in range(n)])


def after(v, *others):
    return lax.optimization_barrier((v, others))[0]


def gather_hp(v):
    far = swap_y(v)
    return [v, far, swap_core(v), swap_core(far)]


def scatter_hp(parts):
    near = swap_core(parts[2].astype(BF)).astype(F32) + parts[0].astype(F32)
    over = swap_core(parts[3].astype(BF)).astype(F32) + parts[1].astype(F32)
    return near + swap_y(over.astype(BF)).astype(F32)


def crossed(b, h):
    odd, high = (h & 1) == 1, (h & 2) == 2
    c = [jnp.where(odd, b[i ^ 1], b[i]) for i in range(4)]
    return [jnp.where(high, c[i ^ 2], c[i]) for i in range(4)]


def relative(v, h, axis):
    c = crossed(jnp.split(v, 4, axis=axis), h)
    return jnp.concatenate([c[0], c[2], c[1], c[3]], axis=axis)


def absolute(v, h, axis):
    b = jnp.split(v, 4, axis=axis)
    return jnp.concatenate(crossed([b[0], b[2], b[1], b[3]], h), axis=axis)


def gather_ep(v):
    stages = lax.axis_size("ep") // 2
    own, out = v, []
    for k in range(stages):
        out.append((own, swap_pair(own)))
        if k < stages - 1:
            own = ring(own)
    return out


def scatter_ep(parts):
    stages = len(parts)
    total = None
    for k in list(range(1, stages)) + [0]:
        here = parts[k][0].astype(F32) + swap_pair(parts[k][1]).astype(F32)
        if total is not None:
            here = here + total.astype(F32)
        total = here if k == 0 else ring(here.astype(BF))
    return total


def spread_ep(v, e):
    n = lax.axis_size("ep")
    stages = n // 2
    x, z = e & 1, e >> 1
    column = lax.dynamic_update_index_in_dim(jnp.zeros((stages,) + v.shape, v.dtype), v, z, 0)
    for step in range(1, stages):
        column = lax.dynamic_update_index_in_dim(
            column, shift(v, step), (z + stages - step) % stages, 0
        )
    far = swap_pair(column)
    both = [jnp.where(x == 0, column, far), jnp.where(x == 0, far, column)]
    return jnp.stack(both, axis=1).reshape((n,) + v.shape)


def sum_ep(v, e):
    n = lax.axis_size("ep")
    stages = n // 2
    x, z = e & 1, e >> 1
    halves = v.reshape(2, v.shape[0] // 2, v.shape[1])
    mine = lax.dynamic_index_in_dim(halves, x, 0, False)
    other = lax.dynamic_index_in_dim(halves, 1 - x, 0, False)
    mine = mine + swap_pair(other.astype(BF)).astype(F32)
    chunks = mine.reshape(stages, mine.shape[0] // stages, mine.shape[1])
    low = chunks.astype(BF)
    total = lax.dynamic_index_in_dim(chunks, z, 0, False)
    for step in range(1, stages):
        part = lax.dynamic_index_in_dim(low, (z + step) % stages, 0, False)
        total = total + shift(part, step).astype(F32)
    total = total.astype(BF)
    half = lax.dynamic_update_index_in_dim(jnp.zeros(chunks.shape, BF), total, z, 0)
    for step in range(1, stages):
        half = lax.dynamic_update_index_in_dim(
            half, shift(total, step), (z + stages - step) % stages, 0
        )
    half = half.reshape(mine.shape)
    far = swap_pair(half)
    low = jnp.where(x == 0, half, far)
    high = jnp.where(x == 0, far, half)
    return jnp.concatenate([low, high], axis=0).astype(F32)


def sum_all_small(v):
    v = v + swap_core(v)
    v = v + swap_y(v)
    n = lax.axis_size("ep")
    bit = 1
    while bit < n:
        v = v + lax.ppermute(v, "ep", [(i, i ^ bit) for i in range(n)])
        bit *= 2
    return v


def score_mask(h, rows, cols):
    at = lax.broadcasted_iota(jnp.int32, (rows, cols), 0) + h * rows
    key = lax.broadcasted_iota(jnp.int32, (rows, cols), 1)
    block = key // rows
    other = jnp.where(
        block == 0, h, jnp.where(block == 1, h ^ 2, jnp.where(block == 2, h ^ 1, h ^ 3))
    )
    return other * rows + key % rows <= at


def turned(v, cosine, sine):
    return v * cosine + pltpu.roll(v, HD // 2, 1) * sine


def project_kernel(
    t_ref, f_ref, gain_ref, k_ref, v_ref, q_ref, cos_ref, sin_ref, x_ref, kv_ref, query_ref
):
    rows = query_ref.shape[0]

    @pl.when(pl.program_id(0) == 0)
    def _():
        for i, ref in enumerate((t_ref, f_ref)):
            v = ref[...].astype(F32)
            x_ref[i * rows : (i + 1) * rows, :] = (v * rms(v) * gain_ref[...]).astype(BF)

    x = x_ref[...]
    cosine, sine = cos_ref[...], sin_ref[...]
    keys, query = dot(x, k_ref[...]), dot(x[:rows], q_ref[...])
    kv_ref[1] = dot(x, v_ref[...]).astype(BF)
    for i in range(k_ref.shape[1] // HD):
        span = slice(i * HD, (i + 1) * HD)
        kv_ref[0, :, span] = turned(keys[:, span], cosine, sine).astype(BF)
        query_ref[:, span] = turned(query[:, span], cosine[:rows], sine[:rows]).astype(BF)


def project(tokens, far, gain, k_w, v_w, q_w, cosine, sine):
    rows, width = tokens.shape
    two, block = 2 * rows, 2 * HD
    cols = pl.BlockSpec((width, block), lambda i: (0, i))

    def fixed(v):
        return pl.BlockSpec(v.shape, lambda i: (0, 0))

    return pl.pallas_call(
        project_kernel,
        grid=(width // block,),
        in_specs=[fixed(tokens), fixed(far), fixed(gain), cols, cols, cols]
        + [pl.BlockSpec((two, HD), lambda i: (0, 0))] * 2,
        out_specs=[
            pl.BlockSpec((two, width), lambda i: (0, 0)),
            pl.BlockSpec((2, two, block), lambda i: (0, 0, i)),
            pl.BlockSpec((rows, block), lambda i: (0, i)),
        ],
        out_shape=[
            jax.ShapeDtypeStruct((two, width), BF),
            jax.ShapeDtypeStruct((2, two, width), BF),
            jax.ShapeDtypeStruct((rows, width), BF),
        ],
        compiler_params=pltpu.CompilerParams(vmem_limit_bytes=40 * MIB),
        cost_estimate=pl.CostEstimate(flops=0, bytes_accessed=0, transcendentals=0),
    )(tokens, far, gain, k_w, v_w, q_w, cosine, sine)


def attend_kernel(h_ref, q_ref, ka_ref, kb_ref, va_ref, vb_ref, o_ref, lse_ref):
    rows = q_ref.shape[0]
    half = ka_ref.shape[0]
    q = q_ref[...]
    s = jnp.concatenate([dot(q, ka_ref[...], (1, 1)), dot(q, kb_ref[...], (1, 1))], axis=1)
    s = jnp.where(score_mask(h_ref[0], rows, 2 * half), s * HD ** (-0.5), -1e30)
    top = jnp.max(s, axis=1, keepdims=True)
    p = jnp.exp(s - top)
    total = jnp.sum(p, axis=1, keepdims=True)
    p = (p * (1.0 / total)).astype(BF)
    o = dot(p[:, :half], va_ref[...]) + dot(p[:, half:], vb_ref[...])
    o_ref[...] = o.astype(BF)
    lse_ref[...] = jnp.broadcast_to(top + jnp.log(total), lse_ref.shape)


def attend_back_kernel(
    h_ref,
    q_ref,
    ka_ref,
    kb_ref,
    va_ref,
    vb_ref,
    d_ref,
    lse_ref,
    cos_ref,
    sin_ref,
    dq_ref,
    da_ref,
    db_ref,
):
    rows = q_ref.shape[0]
    half = ka_ref.shape[0]
    q, d = q_ref[...], d_ref[...]
    cosine, sine = cos_ref[...], -sin_ref[...]
    s = jnp.concatenate([dot(q, ka_ref[...], (1, 1)), dot(q, kb_ref[...], (1, 1))], axis=1)
    s = jnp.where(score_mask(h_ref[0], rows, 2 * half), s * HD ** (-0.5), -1e30)
    p = jnp.exp(s - lse_ref[:, 0:1])
    back = jnp.concatenate([dot(d, va_ref[...], (1, 1)), dot(d, vb_ref[...], (1, 1))], axis=1)
    inner = jnp.sum(p * back, axis=1, keepdims=True)
    sb = (p * (back - inner) * HD ** (-0.5)).astype(BF)
    p = p.astype(BF)
    dq = dot(sb[:, :half], ka_ref[...]) + dot(sb[:, half:], kb_ref[...])
    dq_ref[...] = turned(dq, cosine[:rows], sine[:rows]).astype(BF)
    dk = turned(dot(sb, q, (0, 0)), cosine, sine)
    dv = dot(p, d, (0, 0))
    da_ref[0] = dk[:half]
    da_ref[1] = dv[:half]
    db_ref[0] = dk[half:].astype(BF)
    db_ref[1] = dv[half:].astype(BF)


def head_spec(rows):
    return pl.BlockSpec((rows, HD), lambda i, h: (0, i))


def kv_spec(rows, which):
    return pl.BlockSpec((None, rows, HD), lambda i, h: (which, 0, i))


def attend(h, q, kv_a, kv_b):
    rows, width = q.shape
    half = kv_a.shape[1]
    return pl.pallas_call(
        attend_kernel,
        grid_spec=pltpu.PrefetchScalarGridSpec(
            num_scalar_prefetch=1,
            grid=(H,),
            in_specs=[
                head_spec(rows),
                kv_spec(half, 0),
                kv_spec(half, 0),
                kv_spec(half, 1),
                kv_spec(half, 1),
            ],
            out_specs=[head_spec(rows), head_spec(rows)],
        ),
        out_shape=[
            jax.ShapeDtypeStruct((rows, width), BF),
            jax.ShapeDtypeStruct((rows, width), F32),
        ],
        compiler_params=pltpu.CompilerParams(vmem_limit_bytes=40 * MIB),
        cost_estimate=pl.CostEstimate(flops=0, bytes_accessed=0, transcendentals=0),
    )(h, q, kv_a, kv_b, kv_a, kv_b)


def attend_back(h, q, kv_a, kv_b, d, lse, cosine, sine):
    rows, width = q.shape
    half = kv_a.shape[1]
    flops = 10 * rows * 2 * half * width
    table = pl.BlockSpec((2 * half, HD), lambda i, h: (0, 0))
    both = pl.BlockSpec((2, half, HD), lambda i, h: (0, 0, i))
    return pl.pallas_call(
        attend_back_kernel,
        grid_spec=pltpu.PrefetchScalarGridSpec(
            num_scalar_prefetch=1,
            grid=(H,),
            in_specs=[
                head_spec(rows),
                kv_spec(half, 0),
                kv_spec(half, 0),
                kv_spec(half, 1),
                kv_spec(half, 1),
                head_spec(rows),
                head_spec(rows),
                table,
                table,
            ],
            out_specs=[head_spec(rows), both, both],
        ),
        out_shape=[
            jax.ShapeDtypeStruct((rows, width), BF),
            jax.ShapeDtypeStruct((2, half, width), F32),
            jax.ShapeDtypeStruct((2, half, width), BF),
        ],
        compiler_params=pltpu.CompilerParams(vmem_limit_bytes=40 * MIB),
        cost_estimate=pl.CostEstimate(
            flops=flops, bytes_accessed=16 * MIB, transcendentals=rows * 2 * half * H
        ),
    )(h, q, kv_a, kv_b, kv_a, kv_b, d, lse, cosine, sine)


def pick_matrix(meta, col, capacity):
    lane = lax.broadcasted_iota(jnp.int32, meta.shape, 1)
    code = jnp.sum(jnp.where(lane == col, meta.astype(F32), 0.0), axis=1, keepdims=True)
    place = lax.broadcasted_iota(jnp.int32, (meta.shape[0], capacity), 1).astype(F32)
    return jnp.where(code == place, 1.0, 0.0).astype(BF)


def expert_kernel(capacity, total, olds, e_ref, x0_ref, x1_ref, g0_ref, g1_ref, *refs):
    gates, ups, downs = refs[0:4], refs[4:8], refs[8:12]
    sg_ref, su_ref, sd_ref, sgg_old, sdg_old = refs[12:17]
    (
        dx0_ref,
        dx1_ref,
        sgg_ref,
        sdg_ref,
        sa_ref,
        xr_ref,
        gr_ref,
        gi_ref,
        ui_ref,
        wa_ref,
    ) = refs[17 + olds :]
    xs, gs, dxs = (x0_ref, x1_ref), (g0_ref, g1_ref), (dx0_ref, dx1_ref)
    width = sg_ref.shape[0]
    tokens = x0_ref.shape[0]
    c = capacity
    x2 = jnp.concatenate([r[:, :width] for r in xs], axis=0)
    g2 = jnp.concatenate([r[:, :width] for r in gs], axis=0)
    hg, hu = dot(x2, sg_ref[...]), dot(x2, su_ref[...])
    ab = dot(g2, sd_ref[...], (1, 1))
    s = jax.nn.sigmoid(hg)
    silu = hg * s
    act = (silu * hu).astype(BF)
    gi = (ab * hu * (s * (1.0 + hg * (1.0 - s)))).astype(BF)
    ui = (ab * silu).astype(BF)
    sa_ref[0] = act
    gu = jnp.concatenate([gi, ui], axis=1)
    sgg_ref[...] = sgg_old[...] + dot(x2, gu, (0, 0))
    sdg_ref[...] = sdg_old[...] + dot(act, g2, (0, 0))
    dx = dot(gi, sg_ref[...], (1, 1)) + dot(ui, su_ref[...], (1, 1))
    totals = [dx[:tokens], dx[tokens:]]
    metas = [0.0, 0.0]
    lane = lax.broadcasted_iota(jnp.int32, (2 * c, LANES), 1)
    for x in range(2):
        col = 2 * e_ref[0] + x
        picks, weights = [], []
        for j in range(2):
            pick = pick_matrix(xs[j][:, width:], total + col, c)
            picks.append(pick)
            rows = dot(pick, xs[j][...], (0, 0))
            xr_ref[x, 0, j * c : (j + 1) * c, :] = rows[:, :width].astype(BF)
            weights.append(rows[:, width:])
            gr_ref[x, 0, j * c : (j + 1) * c, :] = dot(pick, gs[j][:, :width], (0, 0)).astype(BF)
        w = jnp.concatenate(weights, axis=0)
        w = jnp.sum(jnp.where(lane == col, w, 0.0), axis=1, keepdims=True)
        xr, gr = xr_ref[x, 0], gr_ref[x, 0]
        dxr = jnp.zeros((2 * c, width), F32)
        wb = jnp.zeros((2 * c, 1), F32)
        for r in range(4):
            wg, wu, wd = gates[r][x], ups[r][x], downs[r][x]
            hg, hu = dot(xr, wg), dot(xr, wu)
            ab = dot(gr, wd, (1, 1))
            s = jax.nn.sigmoid(hg)
            silu = hg * s
            act = silu * hu
            wb = wb + jnp.sum(act * ab, axis=1, keepdims=True)
            ab = ab * w
            gi = (ab * hu * (s * (1.0 + hg * (1.0 - s)))).astype(BF)
            ui = (ab * silu).astype(BF)
            gi_ref[r, x, 0] = gi
            ui_ref[r, x, 0] = ui
            wa_ref[r, x, 0] = (act * w).astype(BF)
            dxr = dxr + dot(gi, wg, (1, 1)) + dot(ui, wu, (1, 1))
        dxr = dxr.astype(BF)
        high = wb.astype(BF).astype(F32)
        meta = jnp.where(lane == col, high, 0.0) + jnp.where(lane == total + col, wb - high, 0.0)
        meta = meta.astype(BF)
        for j in range(2):
            span = slice(j * c, (j + 1) * c)
            totals[j] = totals[j] + dot(picks[j], dxr[span])
            metas[j] = metas[j] + dot(picks[j], meta[span])
    for j in range(2):
        dxs[j][:, :width] = totals[j].astype(BF)
        dxs[j][:, width:] = metas[j].astype(BF)


def expert_out_kernel(capacity, total, e_ref, x0_ref, x1_ref, wa_ref, sa_ref, *refs):
    downs, sd_ref, outs = refs[0:4], refs[4], refs[5:7]
    width = sd_ref.shape[1]
    tokens = x0_ref.shape[0]
    c = capacity
    xs = (x0_ref, x1_ref)
    shared = dot(sa_ref[0], sd_ref[...])
    totals = [shared[:tokens], shared[tokens:]]
    for x in range(2):
        rows = jnp.zeros((2 * c, width), F32)
        for r in range(4):
            rows = rows + dot(wa_ref[r, x, 0], downs[r][x])
        rows = rows.astype(BF)
        for j in range(2):
            pick = pick_matrix(xs[j][...], total + 2 * e_ref[0] + x, c)
            totals[j] = totals[j] + dot(pick, rows[j * c : (j + 1) * c])
    for j in range(2):
        outs[j][...] = totals[j].astype(BF)


def whole(shape):
    return pl.BlockSpec(shape, lambda i, e: (0,) * len(shape), pipeline_mode=pl.Buffered(1))


def expert_stage(
    k, stages, capacity, total, e, x_pair, g_pair, gates, ups, downs, sg, su, sd, carry, bufs
):
    tokens, wide = x_pair[0].shape
    width = sg.shape[0]
    hidden = gates[0].shape[2]
    c2 = 2 * capacity
    shared = sg.shape[1]
    olds = 0 if bufs is None else 6
    shapes = [
        ((stages, 2 * tokens, shared), (1, 2 * tokens, shared), (k, 0, 0)),
        ((2, stages, c2, width), (2, 1, c2, width), (0, k, 0, 0)),
        ((2, stages, c2, width), (2, 1, c2, width), (0, k, 0, 0)),
        ((4, 2, stages, c2, hidden), (4, 2, 1, c2, hidden), (0, 0, k, 0, 0)),
        ((4, 2, stages, c2, hidden), (4, 2, 1, c2, hidden), (0, 0, k, 0, 0)),
        ((4, 2, stages, c2, hidden), (4, 2, 1, c2, hidden), (0, 0, k, 0, 0)),
    ]

    def at(block, where):
        return pl.BlockSpec(block, lambda i, e: where)

    ins = [e, *x_pair, *g_pair, *gates, *ups, *downs, sg, su, sd, *carry]
    in_specs = [whole(v.shape) for v in ins[1:]]
    alias = {}
    if bufs is not None:
        for n, b in enumerate(bufs):
            alias[len(ins)] = 4 + n
            ins.append(b)
            in_specs.append(pl.BlockSpec(memory_space=pl.ANY))
    out_shape = [jax.ShapeDtypeStruct((tokens, wide), BF)] * 2 + [
        jax.ShapeDtypeStruct(v.shape, v.dtype) for v in carry
    ]
    out_specs = [whole((tokens, wide))] * 2 + [whole(v.shape) for v in carry]
    for full, block, where in shapes:
        out_shape.append(jax.ShapeDtypeStruct(full, BF))
        out_specs.append(at(block, where))
    outs = pl.pallas_call(
        functools.partial(expert_kernel, capacity, total, olds),
        grid_spec=pltpu.PrefetchScalarGridSpec(
            num_scalar_prefetch=1, grid=(1,), in_specs=in_specs, out_specs=out_specs
        ),
        out_shape=out_shape,
        input_output_aliases=alias,
        compiler_params=pltpu.CompilerParams(vmem_limit_bytes=60 * MIB),
        cost_estimate=pl.CostEstimate(
            flops=20 * c2 * width * 4 * hidden, bytes_accessed=24 * MIB, transcendentals=c2 * 8 * hidden
        ),
    )(*ins)
    return outs[0:2], outs[2:4], outs[4:]


def expert_out(k, capacity, total, e, x_pair, wa, sa, downs, sd):
    tokens = x_pair[0].shape[0]
    width = sd.shape[1]
    c2 = wa.shape[3]
    last = x_pair[0].shape[1] // LANES - 1
    meta = pl.BlockSpec((tokens, LANES), lambda i, e: (0, last))
    return pl.pallas_call(
        functools.partial(expert_out_kernel, capacity, total),
        grid_spec=pltpu.PrefetchScalarGridSpec(
            num_scalar_prefetch=1,
            grid=(1,),
            in_specs=[
                meta,
                meta,
                pl.BlockSpec((4, 2, 1, c2, wa.shape[4]), lambda i, e: (0, 0, k, 0, 0)),
                pl.BlockSpec((1,) + sa.shape[1:], lambda i, e: (k, 0, 0)),
            ]
            + [whole(d.shape) for d in downs]
            + [whole(sd.shape)],
            out_specs=[whole((tokens, width))] * 2,
        ),
        out_shape=[jax.ShapeDtypeStruct((tokens, width), BF)] * 2,
        compiler_params=pltpu.CompilerParams(vmem_limit_bytes=40 * MIB),
        cost_estimate=pl.CostEstimate(
            flops=4 * c2 * width * 4 * wa.shape[4], bytes_accessed=10 * MIB, transcendentals=0
        ),
    )(e, *x_pair, wa, sa, *downs, sd)


def dispatch_kernel(capacity, total, x_ref, m_ref, g0_ref, g1_ref, *refs):
    experts = refs[0:3]
    sg_ref, su_ref, sd_ref = refs[3:6]
    dx_ref, wb_ref, near_ref, far_ref, sgg_ref, sdg_ref = refs[6:12]
    xr_ref, gr_ref, gu_ref, wa_ref, last_ref = refs[12:17]
    xbuf, sbuf, tbuf, mbuf, nbuf, bbuf, sbbuf, tbbuf, wgu, wd = refs[17:27]
    (
        rx_s,
        rx_r,
        sx_s,
        sx_r,
        sr_s,
        sr_r,
        rt_s,
        rt_r,
        rm_s,
        rm_r,
        sm_s,
        sm_r,
        sb_s,
        sb_r,
        rb_s,
        rb_r,
        w_sem,
        l_s,
        l_r,
    ) = refs[27:]
    experts = experts + (last_ref,)
    k = pl.program_id(0)
    stages = xbuf.shape[0]
    tokens, width = x_ref.shape[0], sg_ref.shape[0]
    hidden = experts[0].shape[1] // 3
    wide = wd.shape[1] // 4
    c = capacity
    last = stages - 1
    e, h = lax.axis_index("ep"), lax.axis_index("hp")
    n = 2 * stages
    right, left = (lax.rem(e + 2, n), h), (lax.rem(e + n - 2, n), h)
    pair = (e + 1 - 2 * lax.rem(e, 2), h)
    core = (e, h + 1 - 2 * lax.rem(h, 2))

    def ring_x(i):
        return mesh_copy(xbuf.at[i, 0], xbuf.at[i + 1, 0], rx_s, rx_r, i, right)

    def ring_last():
        return mesh_copy(xbuf.at[last - 1, 1], xbuf.at[last, 1], rx_s, rx_r, last, right)

    def swap_x(i):
        return mesh_copy(xbuf.at[i, 0], xbuf.at[i, 1], sx_s, sx_r, i, pair)

    def ring_m(i):
        return mesh_copy(mbuf.at[i], mbuf.at[i + 1], rm_s, rm_r, i, right)

    def swap_m(i):
        return mesh_copy(mbuf.at[i], nbuf.at[i], sm_s, sm_r, i, pair)

    def swap_r(i):
        return mesh_copy(xbuf.at[i, 1], sbuf.at[i], sr_s, sr_r, i, pair)

    def ring_t(i):
        return mesh_copy(xbuf.at[i, 0], tbuf.at[i], rt_s, rt_r, i, right)

    def swap_b(i):
        return mesh_copy(bbuf.at[i, 1], sbbuf.at[i], sb_s, sb_r, i, pair)

    def ring_b(i):
        return mesh_copy(bbuf.at[i, 0], tbbuf.at[i], rb_s, rb_r, i, right)

    to_core = mesh_copy(experts[1], last_ref, l_s, l_r, 0, core)

    def weight_copies(r):
        copies = []
        for x in range(2):
            for i, (to, at) in enumerate(((wgu, 2 * r), (wgu, 2 * r + 1), (wd, r))):
                copies.append(
                    pltpu.make_async_copy(
                        experts[r].at[x, pl.ds(i * hidden, hidden), :],
                        to.at[x, pl.ds(at * wide, hidden), :],
                        w_sem.at[6 * r + 3 * x + i],
                    )
                )
        return copies

    @pl.when(k == 0)
    def _():
        xbuf[0, 0] = x_ref[...]
        mbuf[0] = m_ref[...]
        greet((right, left, pair, core))
        ring_m(0).start()
        swap_m(0).start()
        ring_x(0).start()
        swap_x(0).start()
        to_core.start()
        rest = wide - hidden
        for r in range(3):
            for copy in weight_copies(r):
                copy.start()
        for x in range(2):
            for to, count in ((wgu, 8), (wd, 4)):
                for at in range(count):
                    to[x, at * wide + hidden : (at + 1) * wide, :] = jnp.zeros((rest, width), BF)
        sgg_ref[...] = jnp.zeros_like(sgg_ref)
        sdg_ref[...] = jnp.zeros_like(sdg_ref)
        to_core.wait()
        for copy in weight_copies(3):
            copy.start()

    @pl.when(k < last)
    def _():
        ring_m(k).wait_recv()
        swap_m(k + 1).start()
        ring_x(k).wait_recv()

    @pl.when(k < last - 1)
    def _():
        ring_m(k + 1).start()
        ring_x(k + 1).start()
        swap_x(k + 1).start()

    @pl.when(k < last)
    def _():
        swap_x(k).wait_recv()

    @pl.when(k == last - 1)
    def _():
        ring_last().start()

    @pl.when(k == last)
    def _():
        ring_last().wait_recv()

    swap_m(k).wait_recv()

    @pl.when(k == 0)
    def _():
        for r in range(4):
            for copy in weight_copies(r):
                copy.wait()

    gs = (g0_ref, g1_ref)
    x2 = jnp.concatenate([xbuf[k, j] for j in range(2)], axis=0)
    g2 = jnp.concatenate([g[0] for g in gs], axis=0)
    hg, hu = dot(x2, sg_ref[...]), dot(x2, su_ref[...])
    ab = dot(g2, sd_ref[...], (1, 1))
    s = jax.nn.sigmoid(hg)
    silu = hg * s
    act = (silu * hu).astype(BF)
    gi = (ab * hu * (s * (1.0 + hg * (1.0 - s)))).astype(BF)
    ui = (ab * silu).astype(BF)
    sgg_ref[...] += dot(x2, jnp.concatenate([gi, ui], axis=1), (0, 0))
    sdg_ref[...] += dot(act, g2, (0, 0))
    dx = dot(gi, sg_ref[...], (1, 1)) + dot(ui, su_ref[...], (1, 1))
    totals = [dx[:tokens], dx[tokens:]]
    out = dot(act, sd_ref[...])
    outs = [out[:tokens], out[tokens:]]
    backs = [0.0, 0.0]
    metas = [mbuf[k], nbuf[k]]
    line = lax.broadcasted_iota(jnp.int32, metas[0].shape, 0)
    short = lax.broadcasted_iota(jnp.int32, (total, tokens), 0)
    place = lax.broadcasted_iota(jnp.int32, (c, tokens), 0).astype(F32)
    for x in range(2):
        col = 2 * e + x
        picks, weights, found = [], [], []
        for j in range(2):
            code = jnp.sum(jnp.where(line == total + col, metas[j], 0.0), axis=0, keepdims=True)
            weight = jnp.sum(jnp.where(line == col, metas[j], 0.0), axis=0, keepdims=True)
            hit = code == place
            pick = jnp.where(hit, 1.0, 0.0).astype(BF)
            found.append(hit)
            picks.append(pick)
            weights.append(jnp.sum(jnp.where(hit, weight, 0.0), axis=1, keepdims=True))
            xr_ref[x, 0, j * c : (j + 1) * c, :] = dot(pick, xbuf[k, j]).astype(BF)
            gr_ref[x, 0, j * c : (j + 1) * c, :] = dot(pick, gs[j][0]).astype(BF)
        w = jnp.concatenate(weights, axis=0)
        xr, gr = xr_ref[x, 0], gr_ref[x, 0]
        wb = jnp.zeros((2 * c, 1), F32)
        for r in range(4):
            hgu = dot(xr, wgu[x, 2 * r * wide : 2 * (r + 1) * wide, :], (1, 1))
            ab = dot(gr, wd[x, r * wide : (r + 1) * wide, :], (1, 1))
            hg, hu = hgu[:, :wide], hgu[:, wide:]
            s = jax.nn.sigmoid(hg)
            silu = hg * s
            act = silu * hu
            wb = wb + jnp.sum(act * ab, axis=1, keepdims=True)
            ab = ab * w
            at = 2 * r * wide
            gu_ref[x, 0, :, at : at + wide] = (ab * hu * (s * (1.0 + hg * (1.0 - s)))).astype(BF)
            gu_ref[x, 0, :, at + wide : at + 2 * wide] = (ab * silu).astype(BF)
            wa_ref[x, 0, :, r * wide : (r + 1) * wide] = (act * w).astype(BF)
        dxr = dot(gu_ref[x, 0], wgu[x]).astype(BF)
        rows = dot(wa_ref[x, 0], wd[x]).astype(BF)
        for j in range(2):
            span = slice(j * c, (j + 1) * c)
            totals[j] = totals[j] + dot(picks[j], dxr[span], (0, 0))
            outs[j] = outs[j] + dot(picks[j], rows[span], (0, 0))
            row = jnp.sum(jnp.where(found[j], wb[span], 0.0), axis=0, keepdims=True)
            backs[j] = backs[j] + jnp.where(short == col, row, 0.0)

    @pl.when(k < last)
    def _():
        ring_x(k).wait_send()
        swap_x(k).wait_send()

    @pl.when(k == last - 1)
    def _():
        ring_last().wait_send()

    for j in range(2):
        xbuf[k, j] = totals[j].astype(BF)
        bbuf[k, j] = backs[j]
        (near_ref, far_ref)[j][0] = outs[j].astype(BF)

    @pl.when(k >= 1)
    def _():
        swap_b(k).start()
        swap_r(k).start()

    def advance(i, first):
        swap_b(i).wait_recv()
        swap_r(i).wait_recv()
        here = xbuf[i, 0].astype(F32) + sbuf[i].astype(F32)
        small = bbuf[i, 0] + sbbuf[i]
        if not first:
            ring_b(i - 1).wait_recv()
            ring_t(i - 1).wait_recv()
            here = here + tbuf[i - 1].astype(F32)
            small = small + tbbuf[i - 1]
        xbuf[i, 0] = here.astype(BF)
        bbuf[i, 0] = small
        ring_b(i).start()
        ring_t(i).start()

    for i in range(1, last):

        @pl.when(k == i + 1)
        def _(i=i):
            advance(i, i == 1)

    @pl.when(k == last)
    def _():
        swap_b(0).start()
        swap_r(0).start()
        advance(last, last == 1)
        swap_b(0).wait_recv()
        swap_r(0).wait_recv()
        ring_b(last).wait_recv()
        ring_t(last).wait_recv()
        dx_ref[...] = xbuf[0, 0].astype(F32) + sbuf[0].astype(F32) + tbuf[last].astype(F32)
        wb_ref[...] = bbuf[0, 0] + sbbuf[0] + tbbuf[last]
        for i in range(stages):
            swap_r(i).wait_send()
            swap_b(i).wait_send()
            swap_m(i).wait_send()
        for i in range(1, stages):
            ring_t(i).wait_send()
            ring_b(i).wait_send()
            ring_m(i - 1).wait_send()


def dispatch(capacity, total, x, meta, g_near, g_far, experts, sg, su, sd):
    stages = g_near.shape[0]
    tokens, width = x.shape
    lines = meta.shape[0]
    shared = sg.shape[1]
    hidden = experts[0].shape[1] // 3
    wide = -(-hidden // LANES) * LANES
    c2 = 2 * capacity
    once = pl.Buffered(1)
    dma = pltpu.SemaphoreType.DMA

    def fixed(shape):
        return pl.BlockSpec(shape, lambda k: (0,) * len(shape), pipeline_mode=once)

    def per_stage(shape):
        return pl.BlockSpec(shape, lambda k: (0, k, 0, 0), pipeline_mode=once)

    anywhere = pl.BlockSpec(memory_space=pl.ANY)
    return pl.pallas_call(
        functools.partial(dispatch_kernel, capacity, total),
        grid=(stages,),
        in_specs=[
            fixed((tokens, width)),
            fixed(meta.shape),
            pl.BlockSpec((1, tokens, width), lambda k: (k, 0, 0)),
            pl.BlockSpec((1, tokens, width), lambda k: (k, 0, 0)),
        ]
        + [anywhere] * 3
        + [fixed(sg.shape), fixed(su.shape), fixed(sd.shape)],
        out_specs=[
            fixed((tokens, width)),
            fixed((total, tokens)),
            pl.BlockSpec((1, tokens, width), lambda k: (k, 0, 0), pipeline_mode=once),
            pl.BlockSpec((1, tokens, width), lambda k: (k, 0, 0), pipeline_mode=once),
            fixed((width, 2 * shared)),
            fixed((shared, width)),
            per_stage((2, 1, c2, width)),
            per_stage((2, 1, c2, width)),
            per_stage((2, 1, c2, 8 * wide)),
            per_stage((2, 1, c2, 4 * wide)),
            anywhere,
        ],
        out_shape=[
            jax.ShapeDtypeStruct((tokens, width), F32),
            jax.ShapeDtypeStruct((total, tokens), F32),
            jax.ShapeDtypeStruct((stages, tokens, width), BF),
            jax.ShapeDtypeStruct((stages, tokens, width), BF),
            jax.ShapeDtypeStruct((width, 2 * shared), F32),
            jax.ShapeDtypeStruct((shared, width), F32),
            jax.ShapeDtypeStruct((2, stages, c2, width), BF),
            jax.ShapeDtypeStruct((2, stages, c2, width), BF),
            jax.ShapeDtypeStruct((2, stages, c2, 8 * wide), BF),
            jax.ShapeDtypeStruct((2, stages, c2, 4 * wide), BF),
            jax.ShapeDtypeStruct(experts[0].shape, BF),
        ],
        scratch_shapes=[
            pltpu.VMEM((stages, 2, tokens, width), BF),
            pltpu.VMEM((stages, tokens, width), BF),
            pltpu.VMEM((stages, tokens, width), BF),
            pltpu.VMEM((stages, lines, tokens), F32),
            pltpu.VMEM((stages, lines, tokens), F32),
            pltpu.VMEM((stages, 2, total, tokens), F32),
            pltpu.VMEM((stages, total, tokens), F32),
            pltpu.VMEM((stages, total, tokens), F32),
            pltpu.VMEM((2, 8 * wide, width), BF),
            pltpu.VMEM((2, 4 * wide, width), BF),
        ]
        + [dma((stages,))] * 16
        + [dma((24,))]
        + [dma((1,))] * 2,
        compiler_params=pltpu.CompilerParams(
            vmem_limit_bytes=63 * MIB, collective_id=0, has_side_effects=True
        ),
        cost_estimate=pl.CostEstimate(
            flops=24 * c2 * stages * width * 4 * hidden,
            bytes_accessed=80 * MIB,
            transcendentals=stages * c2 * 8 * hidden,
        ),
    )(x, meta, g_near, g_far, *experts, sg, su, sd)[:10]


def mesh_copy(src, dst, s, r, i, where):
    return pltpu.make_async_remote_copy(
        src_ref=src,
        dst_ref=dst,
        send_sem=s.at[i],
        recv_sem=r.at[i],
        device_id=where,
        device_id_type=pl.DeviceIdType.MESH,
    )


def greet(peers):
    barrier = pltpu.get_barrier_semaphore()
    for where in peers:
        pl.semaphore_signal(barrier, inc=1, device_id=where, device_id_type=pl.DeviceIdType.MESH)
    pl.semaphore_wait(barrier, len(peers))


def front_kernel(large, count, *refs):
    tok_ref, exp_ref, cot_ref = refs[0:3]
    ins = refs[3 : 3 + count]
    far_ref, expo_ref, g_ref = refs[3 + count : 6 + count]
    outs = refs[6 + count : 6 + 2 * count]
    y_s, y_r, c_s, c_r, f_s, f_r, p_s, p_r, q_s, q_r, l_sem, rg_s, rg_r = refs[6 + 2 * count :]
    stages = g_ref.shape[0]
    n = 2 * stages
    e, h = lax.axis_index("ep"), lax.axis_index("hp")
    x = lax.rem(e, 2)
    h_core, h_far = h + 1 - 2 * lax.rem(h, 2), lax.rem(h + 2, 4)
    core, far = (e, h_core), (e, h_far)
    right, left = (lax.rem(e + 2, n), h), (lax.rem(e + n - 2, n), h)
    pair = (e + 1 - 2 * x, h)
    greet((core, far, right, left, pair))

    def ring_g(k):
        src = cot_ref if k == 0 else g_ref.at[k]
        return mesh_copy(src, g_ref.at[k + 1], rg_s, rg_r, k, right)

    def part(i, other=False):
        rows = ins[i].shape[0] // 2
        return pl.ds((1 - x if other else x) * rows, rows)

    over_y, over_pair, onward, onward_too = [], [], [], []
    for i, v in enumerate(ins):
        o = outs[i]
        if i < large:
            mine, theirs = part(i), part(i, True)
            over_y.append(mesh_copy(v.at[mine], o.at[h, mine], y_s, y_r, i, far))
            got, rest = o.at[h_far, mine], o.at[h_far, theirs]
            over_pair.append(mesh_copy(got, got, p_s, p_r, i, pair))
            onward.append(mesh_copy(got, got, f_s, f_r, i, core))
            onward_too.append(mesh_copy(rest, rest, q_s, q_r, i, core))
        else:
            over_y.append(mesh_copy(v, o.at[h], y_s, y_r, i, far))
            onward.append(mesh_copy(o.at[h_far], o.at[h_far], f_s, f_r, i, core))
    over_y.append(mesh_copy(tok_ref, far_ref, y_s, y_r, count, far))
    over_core = [mesh_copy(v, outs[i].at[h], c_s, c_r, i, core) for i, v in enumerate(ins)]
    over_core.append(mesh_copy(exp_ref, expo_ref, c_s, c_r, count, core))
    local = [pltpu.make_async_copy(v, outs[i].at[h], l_sem.at[i]) for i, v in enumerate(ins)]
    local.append(pltpu.make_async_copy(cot_ref, g_ref.at[0], l_sem.at[count]))
    for copy in over_y:
        copy.start()
    ring_g(0).start()
    for copy in over_core + local:
        copy.start()
    for k in range(max(stages - 1, large)):
        if k < large:
            over_y[k].wait_recv()
            over_pair[k].start()
            onward[k].start()
        if k < stages - 1:
            ring_g(k).wait_recv()
            if k + 1 < stages - 1:
                ring_g(k + 1).start()
    for k in range(large, count):
        over_y[k].wait_recv()
        onward[k].start()
    over_y[count].wait_recv()
    for k in range(large):
        over_pair[k].wait_recv()
        onward_too[k].start()
    for copy in over_y + over_pair + [ring_g(k) for k in range(stages - 1)]:
        copy.wait_send()
    for copy in over_core + onward + onward_too + local:
        copy.wait()


def front(stages, tokens, experts, cotangent, blocks, large):
    count = len(blocks)
    anywhere, vmem = (pl.BlockSpec(memory_space=m) for m in (pl.ANY, pltpu.VMEM))
    dma = pltpu.SemaphoreType.DMA
    return pl.pallas_call(
        functools.partial(front_kernel, large, count),
        in_specs=[anywhere] * 2 + [vmem] * (1 + count),
        out_specs=[anywhere] * (3 + count),
        out_shape=[
            jax.ShapeDtypeStruct(tokens.shape, BF),
            jax.ShapeDtypeStruct(experts.shape, BF),
            jax.ShapeDtypeStruct((stages,) + cotangent.shape, BF),
        ]
        + [jax.ShapeDtypeStruct((4,) + v.shape, BF) for v in blocks],
        scratch_shapes=[dma((count + 1,))] * 4
        + [dma((count,))] * 6
        + [dma((count + 1,))]
        + [dma((stages,))] * 2,
        compiler_params=pltpu.CompilerParams(
            vmem_limit_bytes=32 * MIB, collective_id=1, has_side_effects=True
        ),
        cost_estimate=pl.CostEstimate(flops=0, bytes_accessed=120 * MIB, transcendentals=0),
    )(tokens, experts, cotangent, *blocks)


class SharedSum:
    def __init__(self, at, peers, ref, got, to_far, from_far, fin, s, r):
        c, y, x, z = at
        core, far, pair, up = peers
        self.at, self.fin = at, fin
        self.ref, self.got, self.to_far, self.from_far = ref, got, to_far, from_far
        self.core = mesh_copy(ref.at[:, 1 - c], got, s, r, 0, core)
        self.far = mesh_copy(to_far, from_far, s, r, 1, far)
        own = fin.at[x, z]
        self.up = [mesh_copy(own, own, s, r, 1 + k, up[k]) for k in range(1, 4)]
        self.pair = mesh_copy(fin.at[x], fin.at[x], s, r, 5, pair)
        self.all = [self.core, self.far, self.pair] + self.up

    def over_y(self):
        c, y, _, _ = self.at
        self.core.wait_recv()
        total = self.ref[1 - y, c].astype(F32) + self.got[1 - y].astype(F32)
        self.to_far[...] = total.astype(BF)
        self.far.start()

    def over_z(self):
        c, y, x, z = self.at
        self.far.wait_recv()
        total = self.ref[y, c].astype(F32) + self.got[y].astype(F32)
        self.fin[x, z] = (total + self.from_far[...].astype(F32)).astype(BF)
        for copy in self.up:
            copy.start()

    def over_x(self):
        for copy in self.up:
            copy.wait_recv()
        self.pair.start()


def back_kernel(
    q_ref,
    ka_ref,
    kb_ref,
    va_ref,
    vb_ref,
    d_ref,
    lse_ref,
    wq_ref,
    wk_ref,
    wv_ref,
    cos_ref,
    sin_ref,
    x_ref,
    tok_ref,
    ftok_ref,
    sg_ref,
    sd_ref,
    spread_ref,
    stack_ref,
    near_ref,
    mid_ref,
    away_ref,
    piece_ref,
    qp_ref,
    kp_ref,
    vp_ref,
    first_ref,
    share_ref,
    gain_ref,
    sgout_ref,
    suout_ref,
    sdout_ref,
    layer_ref,
    piece_far,
    sendb,
    recvb,
    nearb,
    kvacc,
    qacc,
    sg_c,
    sg_y,
    sg_yr,
    sg_fin,
    sd_c,
    sd_y,
    sd_yr,
    sd_fin,
    xgot,
    zsend,
    zgot,
    k_s,
    k_r,
    s_s,
    s_r,
    d_s,
    d_r,
    x_s,
    x_r,
    z_s,
    z_r,
    p_s,
    p_r,
):
    i = pl.program_id(0)
    heads = sendb.shape[0]
    rows, half = q_ref.shape[0], ka_ref.shape[0]
    e, h = lax.axis_index("ep"), lax.axis_index("hp")
    x, z = lax.rem(e, 2), e // 2
    c, y = lax.rem(h, 2), h // 2
    core, far = (e, h + 1 - 2 * c), (e, lax.rem(h + 2, 4))
    pair = (e + 1 - 2 * x, h)
    up = [None] + [(2 * lax.rem(z + s, 4) + x, h) for s in range(1, 4)]

    def over_core(n):
        return mesh_copy(sendb.at[n], recvb.at[n], k_s, k_r, n, core)

    def over_x(n):
        return mesh_copy(away_ref.at[n], xgot.at[n], x_s, x_r, n, pair)

    def home(n):
        return mesh_copy(zsend.at[n - 1], zgot.at[n - 1], z_s, z_r, n - 1, up[4 - n])

    hidden = piece_ref.shape[1] // 3
    pieces = []
    for n in range(6):
        place = (n // 3, pl.ds(n % 3 * hidden, hidden))
        pieces.append(mesh_copy(piece_ref.at[place], piece_far.at[place], p_s, p_r, n, far))
    at, peers = (c, y, x, z), (core, far, pair, up)
    sums = [
        SharedSum(at, peers, sg_ref, sg_c, sg_y, sg_yr, sg_fin, s_s, s_r),
        SharedSum(at, peers, sd_ref, sd_c, sd_y, sd_yr, sd_fin, d_s, d_r),
    ]

    def send_home(n):
        over_x(n).wait_recv()
        zsend[n - 1] = (near_ref[n].astype(F32) + xgot[n].astype(F32)).astype(BF)
        home(n).start()

    @pl.when(i == 0)
    def _():
        greet([core, far, pair] + up[1:])
        for n in (1, 2, 3, 0):
            over_x(n).start()
        for flow in sums:
            flow.core.start()
        pieces[0].start()
        kvacc[...] = jnp.zeros_like(kvacc)
        qacc[...] = jnp.zeros_like(qacc)

    @pl.when(i < heads)
    def _():
        q, d = q_ref[...], d_ref[...]
        cosine, sine = cos_ref[...], -sin_ref[...]
        s = jnp.concatenate([dot(q, ka_ref[...], (1, 1)), dot(q, kb_ref[...], (1, 1))], axis=1)
        s = jnp.where(score_mask(h, rows, 2 * half), s * HD ** (-0.5), -1e30)
        p = jnp.exp(s - lse_ref[:, 0:1])
        back = [dot(d, va_ref[...], (1, 1)), dot(d, vb_ref[...], (1, 1))]
        back = jnp.concatenate(back, axis=1)
        inner = jnp.sum(p * back, axis=1, keepdims=True)
        sb = (p * (back - inner) * HD ** (-0.5)).astype(BF)
        p = p.astype(BF)
        dq = dot(sb[:, :half], ka_ref[...]) + dot(sb[:, half:], kb_ref[...])
        dk = turned(dot(sb, q, (0, 0)), cosine, sine)
        dv = dot(p, d, (0, 0))
        nearb[lax.rem(i, 2), 0] = dk[:half]
        nearb[lax.rem(i, 2), 1] = dv[:half]
        sendb[i, 0] = dk[half:].astype(BF)
        sendb[i, 1] = dv[half:].astype(BF)
        over_core(i).start()
        raw = turned(dq, cosine[:rows], sine[:rows]).astype(BF)
        qp_ref[...] = dot(x_ref[:rows, :], raw, (0, 0)).astype(BF)
        qacc[...] += dot(raw, wq_ref[...], (1, 1))

    @pl.when(i > 0)
    def _():
        n = i - 1
        over_core(n).wait_recv()
        kept = lax.rem(n, 2)
        key = (nearb[kept, 0] + recvb[n, 0].astype(F32)).astype(BF)
        value = (nearb[kept, 1] + recvb[n, 1].astype(F32)).astype(BF)
        kp_ref[...] = dot(x_ref[...], key, (0, 0)).astype(BF)
        vp_ref[...] = dot(x_ref[...], value, (0, 0)).astype(BF)
        kvacc[...] += dot(key, wk_ref[...], (1, 1)) + dot(value, wv_ref[...], (1, 1))

    @pl.when(i == 1)
    def _():
        for flow in sums:
            flow.over_y()
        for copy in pieces[1:]:
            copy.start()

    @pl.when(i == 4)
    def _():
        send_home(1)

    @pl.when(i == 5)
    def _():
        for flow in sums:
            flow.over_z()

    @pl.when(i == 7)
    def _():
        send_home(2)

    @pl.when(i == heads - 1)
    def _():
        for flow in sums:
            flow.over_x()

    @pl.when(i == heads)
    def _():
        first_ref[...] = qacc[...] + kvacc[:rows, :]
        share_ref[...] = kvacc[rows:, :].astype(BF)
        gain = jnp.zeros((1, kvacc.shape[1]), F32)
        for ref, upstream in ((tok_ref, first_ref[...]), (ftok_ref, kvacc[rows:, :])):
            v = ref[...].astype(F32)
            gain = gain + jnp.sum(upstream * v * rms(v), axis=0, keepdims=True)
        gain_ref[...] = gain
        send_home(3)
        over_x(0).wait_recv()
        total = mid_ref[...] + near_ref[0].astype(F32) + xgot[0].astype(F32)
        for n in (1, 2, 3):
            home(n).wait_recv()
            total = total + zgot[n - 1].astype(F32)
        layer_ref[...] = total.astype(BF)
        for flow in sums:
            flow.pair.wait_recv()
        lanes = sg_fin.shape[3] // 2
        gate = more = down = 0.0
        for k in range(8):
            block = sg_fin[k % 2, k // 2]
            gate = gate + dot(block[:, :lanes], spread_ref[k])
            more = more + dot(block[:, lanes:], spread_ref[k])
            down = down + dot(stack_ref[k], sd_fin[k % 2, k // 2])
        sgout_ref[...] = gate
        suout_ref[...] = more
        sdout_ref[...] = down
        for copy in pieces:
            copy.wait()
        for flow in sums:
            for copy in flow.all:
                copy.wait_send()
        for n in range(4):
            over_x(n).wait_send()
        for n in (1, 2, 3):
            home(n).wait_send()
        for n in range(heads):
            over_core(n).wait_send()


def attend_back_and_sums(
    q, kv_a, kv_b, d, lse, weights, tables, first_in, pairs, sgg, sdg, spread, stack, near, middle, away, piece
):
    rows, width = q.shape
    half = kv_a.shape[1]
    stages = near.shape[0]
    dma = pltpu.SemaphoreType.DMA
    once = pl.Buffered(1)
    anywhere = pl.BlockSpec(memory_space=pl.ANY)

    def fixed(v):
        return pl.BlockSpec(v.shape, lambda i: (0,) * v.ndim, pipeline_mode=once)

    def now(i):
        return i - i // H

    def before(i):
        return i - 1 + (H - i) // H

    def head(rows_of, at=now):
        return pl.BlockSpec((rows_of, HD), lambda i: (0, at(i)))

    def kv(which):
        return pl.BlockSpec((None, half, HD), lambda i: (which, 0, now(i)))

    def shape(dims, dtype):
        return jax.ShapeDtypeStruct(dims, dtype)

    def buffers(dims):
        return [
            pltpu.VMEM((2,) + dims, BF),
            pltpu.VMEM(dims, BF),
            pltpu.VMEM(dims, BF),
            pltpu.VMEM((2, 4) + dims, BF),
        ]

    kept = [*tables, first_in, *pairs, sgg, sdg, spread, stack, near, middle]
    ends = [
        shape((rows, width), F32),
        shape((rows, width), BF),
        shape((1, width), F32),
        shape((width // 4, spread.shape[2]), F32),
        shape((width // 4, spread.shape[2]), F32),
        shape((stack.shape[1], width), F32),
        shape((rows, width), BF),
    ]
    return pl.pallas_call(
        back_kernel,
        grid=(H + 1,),
        in_specs=[head(rows), kv(0), kv(0), kv(1), kv(1), head(rows), head(rows)]
        + [head(width), head(width, before), head(width, before)]
        + [fixed(v) for v in kept]
        + [anywhere] * 2,
        out_specs=[head(width), head(width, before), head(width, before)]
        + [fixed(v) for v in ends]
        + [anywhere],
        out_shape=[shape((width, width), BF)] * 3 + ends + [shape(piece.shape, BF)],
        scratch_shapes=[
            pltpu.VMEM((H, 2, half, HD), BF),
            pltpu.VMEM((H, 2, half, HD), BF),
            pltpu.VMEM((2, 2, half, HD), F32),
            pltpu.VMEM((half, width), F32),
            pltpu.VMEM((rows, width), F32),
        ]
        + buffers(sgg.shape[2:])
        + buffers(sdg.shape[2:])
        + [
            pltpu.VMEM((stages, rows, width), BF),
            pltpu.VMEM((stages - 1, rows, width), BF),
            pltpu.VMEM((stages - 1, rows, width), BF),
        ]
        + [dma((H,))] * 2
        + [dma((6,))] * 4
        + [dma((stages,))] * 4
        + [dma((6,))] * 2,
        compiler_params=pltpu.CompilerParams(
            vmem_limit_bytes=60 * MIB, collective_id=3, has_side_effects=True
        ),
        cost_estimate=pl.CostEstimate(
            flops=22 * rows * width * width,
            bytes_accessed=60 * MIB,
            transcendentals=rows * 2 * half * H,
        ),
    )(q, kv_a, kv_b, kv_a, kv_b, d, lse, *weights, *kept, away, piece)


def tail_kernel(
    m0,
    m1,
    m2,
    m3,
    sm_ref,
    fb_ref,
    tok_ref,
    gain_ref,
    first_ref,
    mid_ref,
    out_ref,
    smout_ref,
    tokout_ref,
    crecv,
    ysend,
    yrecv,
    acc,
    xrecv,
    zrecv,
    fin,
    g_acc,
    g_recv,
    f_recv,
    c_s,
    c_r,
    y_s,
    y_r,
    x_s,
    x_r,
    z_s,
    z_r,
    za_s,
    za_r,
    xa_s,
    xa_r,
    g_s,
    g_r,
    f_s,
    f_r,
):
    mats = (m0, m1, m2, m3)
    chunks, part = acc.shape[0], acc.shape[3]
    half = m0.shape[3]
    e, h = lax.axis_index("ep"), lax.axis_index("hp")
    x, z = lax.rem(e, 2), e // 2
    c, y = lax.rem(h, 2), h // 2
    core, far = (e, h + 1 - 2 * c), (e, lax.rem(h + 2, 4))
    pair = (e + 1 - 2 * x, h)
    up = [None] + [(2 * lax.rem(z + s, 4) + x, h) for s in range(1, 4)]
    next_z = (2 * (z + 1 - 2 * lax.rem(z, 2)) + x, h)
    greet([core, far, pair] + up[1:])

    def rows(j):
        return pl.ds(j * part, part)

    def over_core(j, m):
        return mesh_copy(
            mats[m].at[:, 1 - c, :, rows(j), :],
            crecv.at[m, :, :, rows(j), :],
            c_s,
            c_r,
            4 * j + m,
            core,
        )

    def over_y(j):
        return mesh_copy(ysend.at[j], yrecv.at[j], y_s, y_r, j, far)

    def over_x(j):
        return mesh_copy(acc.at[j, :, 1 - x], xrecv.at[j], x_s, x_r, j, pair)

    def over_z(j, s):
        return mesh_copy(
            acc.at[j, lax.rem(z + s, 4), x], zrecv.at[j, s - 1], z_s, z_r, 3 * j + s - 1, up[s]
        )

    def back_z(j, s):
        return mesh_copy(fin.at[j, z, x], fin.at[j, z, x], za_s, za_r, 3 * j + s - 1, up[s])

    def back_x(j):
        return mesh_copy(fin.at[j, :, x], fin.at[j, :, x], xa_s, xa_r, j, pair)

    def add_core(j):
        for m in range(4):
            over_core(j, m).wait_recv()
            for at, to in ((y, acc), (1 - y, ysend)):
                total = mats[m][at, c, :, rows(j), :].astype(F32)
                to[j, m] = (total + crecv[m, at, :, rows(j), :].astype(F32)).astype(BF)
        over_y(j).start()

    def add_y(j):
        over_y(j).wait_recv()
        acc[j] = (acc[j].astype(F32) + yrecv[j].astype(F32)).astype(BF)
        over_x(j).start()

    def add_x(j):
        over_x(j).wait_recv()
        acc[j, :, x] = (acc[j, :, x].astype(F32) + xrecv[j].astype(F32)).astype(BF)
        for s in range(1, 4):
            over_z(j, s).start()

    def add_z(j):
        total = acc[j, z, x].astype(F32)
        for s in range(1, 4):
            over_z(j, s).wait_recv()
            total = total + zrecv[j, s - 1].astype(F32)
        fin[j, z, x] = total.astype(BF)
        for s in range(1, 4):
            back_z(j, s).start()

    def end_z(j):
        for s in range(1, 4):
            back_z(j, s).wait_recv()
        back_x(j).start()

    def end_x(j):
        back_x(j).wait_recv()
        for m in range(4):
            for i in range(2):
                out_ref[m, i * half + j * part : i * half + (j + 1) * part, :] = fin[j, m, i]

    route = (core, far, pair, next_z, up[2])
    small = [
        mesh_copy(g_acc.at[i], g_recv.at[i], g_s, g_r, i, route[i]) for i in range(len(route))
    ]

    back = mesh_copy(fb_ref, f_recv, f_s, f_r, 0, far)

    def side(t):
        if t == chunks - lead:
            back.start()
        if t % 2 == 1 and t // 2 < len(small):
            i = t // 2
            small[i].wait_recv()
            g_acc[i + 1] = g_acc[i] + g_recv[i]
            if i + 1 < len(small):
                small[i + 1].start()
        if t == chunks + 3:
            back.wait()
            first_back = first_ref[...] + f_recv[...].astype(F32)
            values = tok_ref[...].astype(F32)
            to_tokens = norm_back(values, rms(values), gain_ref[...], first_back)
            tokout_ref[...] = mid_ref[...] + to_tokens

    lead = 3
    g_acc[0] = sm_ref[...]
    for m in range(4):
        over_core(0, m).start()
    small[0].start()
    for j in range(1, chunks):
        for m in range(4):
            over_core(j, m).start()
    for j in range(lead):
        add_core(j)
    steps = (add_y, add_x, add_z, end_z, end_x)
    for t in range(chunks + len(steps) - 1):
        if t + lead < chunks:
            add_core(t + lead)
        for p in reversed(range(len(steps))):
            if 0 <= t - p < chunks:
                steps[p](t - p)
        side(t)
    smout_ref[...] = g_acc[len(small)]
    for copy in small:
        copy.wait_send()
    for j in range(chunks):
        for m in range(4):
            over_core(j, m).wait_send()
        for copy in (over_y(j), over_x(j), back_x(j)):
            copy.wait_send()
        for s in range(1, 4):
            over_z(j, s).wait_send()
            back_z(j, s).wait_send()


def tail(mats, small, share, tokens, gain, first_back, middle_back):
    width = mats[0].shape[1]
    half = width // 8
    part = 16
    chunks = half // part
    dma = pltpu.SemaphoreType.DMA
    vmem = pl.BlockSpec(memory_space=pltpu.VMEM)
    return pl.pallas_call(
        tail_kernel,
        in_specs=[vmem] * 10,
        out_specs=[vmem] * 3,
        out_shape=[
            jax.ShapeDtypeStruct((4, 2 * half, width), BF),
            jax.ShapeDtypeStruct(small.shape, F32),
            jax.ShapeDtypeStruct(tokens.shape, F32),
        ],
        scratch_shapes=[
            pltpu.VMEM((4, 2, 2, half, width), BF),
            pltpu.VMEM((chunks, 4, 2, part, width), BF),
            pltpu.VMEM((chunks, 4, 2, part, width), BF),
            pltpu.VMEM((chunks, 4, 2, part, width), BF),
            pltpu.VMEM((chunks, 4, part, width), BF),
            pltpu.VMEM((chunks, 3, part, width), BF),
            pltpu.VMEM((chunks, 4, 2, part, width), BF),
            pltpu.VMEM((6,) + small.shape, F32),
            pltpu.VMEM((5,) + small.shape, F32),
            pltpu.VMEM(share.shape, BF),
        ]
        + [dma((4 * chunks,))] * 2
        + [dma((chunks,))] * 4
        + [dma((3 * chunks,))] * 4
        + [dma((chunks,))] * 2
        + [dma((5,))] * 2
        + [dma((1,))] * 2,
        compiler_params=pltpu.CompilerParams(
            vmem_limit_bytes=60 * MIB, collective_id=2, has_side_effects=True
        ),
        cost_estimate=pl.CostEstimate(flops=0, bytes_accessed=300 * MIB, transcendentals=0),
    )(
        *[m.reshape(2, 2, 2, half, width) for m in mats],
        small,
        share,
        tokens,
        gain,
        first_back,
        middle_back,
    )


def rms(values):
    return lax.rsqrt(jnp.mean(values * values, axis=-1, keepdims=True) + epsilon)


def norm_back(values, inv, gain, upstream):
    weighted = upstream * gain
    inner = jnp.mean(weighted * values, axis=-1, keepdims=True)
    return weighted * inv - values * (inv * inv * inv * inner)


def rotary_tables(positions):
    exponent = jnp.arange(HD // 2, dtype=F32) * (2.0 / HD)
    theta = positions.astype(F32)[:, None] * jnp.power(10000.0, -exponent)[None, :]
    cosine, sine = jnp.cos(theta), jnp.sin(theta)
    return jnp.concatenate([cosine, cosine], axis=1), jnp.concatenate([-sine, sine], axis=1)


def per_device(
    tokens,
    attn_gain,
    query_weight,
    key_weight,
    value_weight,
    out_weight,
    ffn_gain,
    router_weight,
    shared_gate,
    shared_up,
    shared_down,
    expert_gate,
    expert_up,
    expert_down,
    routes,
    keep_mask,
    cotangent,
):
    e, h = lax.axis_index("ep"), lax.axis_index("hp")
    ep = lax.axis_size("ep")
    stages = ep // 2
    rows, width = tokens.shape
    top = routes.shape[1]
    total = router_weight.shape[1]
    capacity = -(-(5 * rows * top // (4 * total)) // 16) * 16
    e_arr, h_arr = jnp.full((1,), e, jnp.int32), jnp.full((1,), h, jnp.int32)

    units = shared_down.shape[0] // ep
    pad = -(-units // 16) * 16
    tiny = [attn_gain[:, None], ffn_gain[:, None], router_weight]
    small = jnp.concatenate(tiny + [jnp.zeros((width // 4, LANES - 2 - total), BF)], axis=1)

    unit = jnp.arange(LANES)
    to = (unit // pad) * (ep * units) + unit % pad
    to = jnp.where((unit < 4 * pad) & (unit % pad < units), to, -ep * units)
    column = jnp.arange(4 * ep * units)
    mine = (column[:, None] == (to + e * units)[None, :]).astype(BF)
    small = [small, dot(shared_gate, mine).astype(BF), dot(shared_up, mine).astype(BF)]
    small = jnp.concatenate(small, axis=1)
    sd = lax.dynamic_slice_in_dim(shared_down, e * units, units, axis=0)
    sd = jnp.pad(sd, ((0, pad - units), (0, 0)))
    blocks = [key_weight, value_weight, query_weight, out_weight, small, sd]
    experts = jnp.concatenate(
        [jnp.swapaxes(expert_gate, 1, 2), jnp.swapaxes(expert_up, 1, 2), expert_down], axis=1
    )
    fused = stages == 4
    if fused:
        far_tokens, experts_core, g_near, *blocks = front(
            stages, tokens, experts, cotangent, blocks, 4
        )
        experts_far = swap_y(after(experts, blocks[0]))
        g_far = swap_pair(g_near)
    else:
        far_tokens = swap_y(tokens)
        blocks = [absolute(jnp.stack(gather_hp(v)), h, 0) for v in blocks]
        g_blocks = gather_ep(cotangent)
        experts = gather_hp(experts)
    k_w, v_w, q_w, o_w, small = (v.reshape(width, v.shape[2]) for v in blocks[:5])
    gain_one = small[:, 0].astype(F32)[None, :]
    gain_two = small[:, 1].astype(F32)[None, :]
    router = small[:, 2 : 2 + total]
    sg, su = small[:, LANES : 2 * LANES], small[:, 2 * LANES :]
    sd = blocks[5].reshape(4 * pad, width)
    if 4 * pad < LANES:
        sd = jnp.pad(sd, ((0, LANES - 4 * pad), (0, 0)))

    pos = jnp.arange(rows, dtype=jnp.int32)
    pos = jnp.concatenate([(h ^ i) * rows + pos for i in (0, 2, 1, 3)])
    cosine, sine = rotary_tables(pos)
    residual = tokens.astype(F32)
    table = cosine[: 2 * rows], sine[: 2 * rows]
    first_in, kv_a, query = project(tokens, far_tokens, gain_one, k_w, v_w, q_w, *table)
    kv_b = swap_core(kv_a)
    mixed, lse = attend(h_arr, query, kv_a, kv_b)
    routes, keep_mask, late = after((routes, keep_mask, jnp.arange(ep)), query)
    if fused:
        mixed = after(mixed, g_far)
    middle = residual + dot(mixed, o_w)
    inv_two = rms(middle)
    second_in = (middle * inv_two * gain_two).astype(BF)

    expert = jnp.arange(total, dtype=jnp.int32)
    hit_each = routes[:, :, None] == expert[None, None, :]
    hit = jnp.any(hit_each, axis=1)
    kept = jnp.sum(jnp.where(hit_each, keep_mask[:, :, None], 0), axis=1)
    below = (jnp.arange(rows)[:, None] > jnp.arange(rows)[None, :]).astype(BF)
    place = jnp.where(hit, dot(below, hit.astype(BF)), -1.0)
    kept = kept.astype(F32)

    logits = jnp.where(hit, dot(second_in, router), -1e30)
    gates_of = jnp.where(hit, jnp.exp(logits - jnp.max(logits, axis=1, keepdims=True)), 0.0)
    gates_of = gates_of / jnp.sum(gates_of, axis=1, keepdims=True)
    pair_weight = gates_of * kept
    flat = (2, ep * capacity)

    hidden = expert_down.shape[1]

    def expert_grad(left, right):
        return jnp.einsum("xna,xnb->xab", left, right, preferred_element_type=F32)

    if fused:
        meta = jnp.concatenate([pair_weight.T, place.T], axis=0)
        experts = [experts, experts_far, experts_core]
        dx_sum, weight_back, near, far, sgg, sdg, xr, gr, gu, wa = dispatch(
            capacity, total, second_in, meta, g_near, g_far, experts, sg, su, sd
        )
        weight_back = weight_back.T
        wide = wa.shape[3] // 4
        xr, gr, gu, wa = (v.reshape(flat + (v.shape[-1],)) for v in (xr, gr, gu, wa))
        gu = expert_grad(gu, xr).astype(BF)
        wa = expert_grad(wa, gr).astype(BF)
        dx_sum = after(dx_sum, gu, wa)

        def piece(r):
            starts = ((gu, 2 * r * wide), (gu, (2 * r + 1) * wide), (wa, r * wide))
            return jnp.concatenate([v[:, a : a + hidden] for v, a in starts], axis=1)

        piece_near = [piece(r) for r in (0, 1)]
        piece_core = swap_core(jnp.stack([piece(r) for r in (2, 3)]))
        piece_sum = (piece_near[1].astype(F32) + piece_core[1].astype(F32)).astype(BF)
    else:
        x_ext = jnp.concatenate(
            [
                second_in,
                pair_weight.astype(BF),
                place.astype(BF),
                jnp.zeros((rows, LANES - 2 * total), BF),
            ],
            axis=1,
        )
        x_blocks = gather_ep(after(x_ext, g_blocks))
        carry = (jnp.zeros((width, 2 * LANES), F32), jnp.zeros((LANES, width), F32))
        bufs, dx_parts = None, []
        gates, ups = (
            [jnp.swapaxes(v[:, i * hidden : (i + 1) * hidden], 1, 2) for v in experts]
            for i in (0, 1)
        )
        downs = [v[:, 2 * hidden :] for v in experts]
        for k in range(stages):
            dx, carry, bufs = expert_stage(
                k,
                stages,
                capacity,
                total,
                e_arr,
                x_blocks[k],
                g_blocks[k],
                gates,
                ups,
                downs,
                sg,
                su,
                sd,
                carry,
                bufs,
            )
            dx_parts.append(dx)
        dx_sum = scatter_ep(dx_parts)
        weight_back = (
            dx_sum[:, width : width + total] + dx_sum[:, width + total : width + 2 * total]
        )
        dx_sum = dx_sum[:, :width]
        sgg, sdg = carry
        sa, xr, gr, gi, ui, wa = bufs
        out_parts = [
            expert_out(k, capacity, total, e_arr, x_blocks[k], wa, sa, downs, sd)
            for k in range(stages)
        ]
        xr, gr = xr.reshape(flat + (width,)), gr.reshape(flat + (width,))
        gi, ui, wa = (v.reshape((4,) + flat + (v.shape[-1],)) for v in (gi, ui, wa))
        routed = scatter_ep(after(out_parts, dx_sum))
        expert_sum = scatter_hp(
            [
                jnp.concatenate(
                    [
                        expert_grad(gi[r], xr),
                        expert_grad(ui[r], xr),
                        expert_grad(wa[r], gr),
                    ],
                    axis=1,
                )
                for r in range(4)
            ]
        )

    grad_out = cotangent.astype(F32)
    gate_back = weight_back * kept
    chosen_back = gates_of * (gate_back - jnp.sum(gates_of * gate_back, axis=1, keepdims=True))
    logits_back = chosen_back.astype(BF)
    router_part = dot(logits_back, second_in, (0, 0))
    second_back = dx_sum + dot(logits_back, router, (1, 1))
    gain_two_part = jnp.sum(second_back * middle * inv_two, axis=0)
    middle_back = grad_out + norm_back(middle, inv_two, gain_two, second_back)
    attn_back = middle_back.astype(BF)
    counts_part = jnp.pad(jnp.sum(kept, axis=0), (0, width - total))

    mixed_back = dot(attn_back, o_w, (1, 1)).astype(BF)
    if fused:
        mixed_back = after(mixed_back, piece_sum)
    out_part = dot(mixed, attn_back, (0, 0))
    sgg = sgg.reshape(4, width // 4, 2 * LANES)
    sdg = sdg[: 4 * pad].reshape(4, pad, width)
    block = late[:, None, None] * units
    spread = (to[None, :, None] + block == column[None, None, :]).astype(BF)

    def small_sums(gain_one_part):
        lines = [router_part, gain_two_part[None, :], counts_part[None, :], gain_one_part]
        return jnp.concatenate(lines + [jnp.zeros((-(total + 3) % 8, width), F32)], axis=0)

    if fused:
        sdg = sdg.astype(BF)
        at = jnp.where(jnp.arange(pad) < units, jnp.arange(pad), -ep * units)[None, None, :]
        stack = (at + block == jnp.arange(ep * units)[None, :, None]).astype(BF)
        (
            q_part,
            k_part,
            v_part,
            first_back,
            share,
            gain_one_part,
            sgate_grad,
            sup_grad,
            sdown_grad,
            layer,
            piece_far,
        ) = attend_back_and_sums(
            query,
            kv_a,
            kv_b,
            mixed_back,
            lse,
            (q_w, k_w, v_w),
            (cosine, sine),
            first_in,
            (tokens, far_tokens),
            sgg.astype(BF).reshape(2, 2, width // 4, 2 * LANES),
            sdg.reshape(2, 2, pad, width),
            spread,
            stack,
            near,
            middle,
            far,
            piece_sum,
        )
        out, sums, tokens_grad = tail(
            [q_part, k_part, v_part, out_part.astype(BF)],
            small_sums(gain_one_part),
            share,
            tokens,
            gain_one,
            first_back,
            middle_back,
        )
        grads = [out[i].astype(F32) for i in range(4)]
        expert_sum = sum(v.astype(F32) for v in (piece_near[0], piece_core[0], piece_far))
    else:
        query_raw, near_back, far_back = attend_back(
            h_arr, query, kv_a, kv_b, mixed_back, lse, cosine, sine
        )
        kv_raw = (near_back + swap_core(far_back).astype(F32)).astype(BF)
        key_raw, value_raw = kv_raw[0], kv_raw[1]
        kv_back = dot(key_raw, k_w, (1, 1)) + dot(value_raw, v_w, (1, 1))
        q_part = dot(first_in[:rows], query_raw, (0, 0))
        k_part = dot(first_in, key_raw, (0, 0))
        v_part = dot(first_in, value_raw, (0, 0))
        first_back = kv_back[:rows] + dot(query_raw, q_w, (1, 1))
        gain_one_part = jnp.zeros((1, width), F32)
        for values, upstream in ((tokens, first_back), (far_tokens, kv_back[rows:])):
            values = values.astype(F32)
            gain_one_part += jnp.sum(upstream * values * rms(values), axis=0, keepdims=True)

        def over_hp(v):
            return scatter_hp(jnp.split(relative(v, h, 0), 4, axis=0))

        grads = [sum_ep(over_hp(v), e) for v in (q_part, k_part, v_part, out_part)]
        sums = sum_all_small(small_sums(gain_one_part))
        first_back = first_back + swap_y(kv_back[rows:].astype(BF)).astype(F32)
        tokens_grad = middle_back + norm_back(residual, rms(residual), gain_one, first_back)
        sgg, sdg = (spread_ep(over_hp(v)[0].astype(BF), e) for v in (sgg, sdg))
        sgate_grad, sup_grad = (
            jnp.einsum("kra,kan->rn", v, spread, preferred_element_type=F32)
            for v in (sgg[:, :, :LANES], sgg[:, :, LANES:])
        )
        sdown_grad = sdg[:, :units].reshape(ep * units, width).astype(F32)
        layer = (middle + routed).astype(BF)
    gate_grad, up_grad = (
        jnp.swapaxes(expert_sum[:, i * hidden : (i + 1) * hidden], 1, 2) for i in (0, 1)
    )
    down_grad = expert_sum[:, 2 * hidden :]

    def own(v, n):
        return lax.dynamic_slice_in_dim(v, h * n, n, axis=0)

    return (
        layer,
        tokens_grad,
        own(sums[total + 2], width // 4),
        *grads,
        own(sums[total], width // 4),
        own(sums[:total].T, width // 4),
        sgate_grad,
        sup_grad,
        sdown_grad,
        gate_grad,
        up_grad,
        down_grad,
        own(sums[total + 1], total // 4).astype(jnp.int32),
    )


def solution(mesh):
    row, ep_hp = P("hp", None), P(("ep", "hp"), None)
    return jax.shard_map(
        per_device,
        mesh=mesh,
        in_specs=(
            ep_hp,
            P("hp"),
            row,
            row,
            row,
            row,
            P("hp"),
            row,
            row,
            row,
            row,
            P("ep", None, "hp"),
            P("ep", None, "hp"),
            P("ep", "hp", None),
            ep_hp,
            ep_hp,
            ep_hp,
        ),
        out_specs=(
            ep_hp,
            ep_hp,
            P("hp"),
            row,
            row,
            row,
            row,
            P("hp"),
            row,
            row,
            row,
            row,
            P("ep", None, "hp"),
            P("ep", None, "hp"),
            P("ep", "hp", None),
            P("hp"),
        ),
        check_vma=False,
    )
```

```python
import functools

import jax
import jax.numpy as jnp
from jax import lax
from jax.experimental import pallas as pl
from jax.experimental.pallas import tpu as pltpu
from jax.sharding import PartitionSpec as P

H = 10
HD = 128
LANES = 128
BF = jnp.bfloat16
F32 = jnp.float32
epsilon = 1e-06
MIB = 1 << 20


def dot(left, right, over=(1, 0)):
    return lax.dot_general(
        left, right, (((over[0],), (over[1],)), ((), ())), preferred_element_type=F32
    )


def swap_core(v):
    return lax.ppermute(v, "hp", [(i, i ^ 1) for i in range(4)])


def swap_y(v):
    return lax.ppermute(v, "hp", [(i, i ^ 2) for i in range(4)])


def swap_pair(v):
    n = lax.axis_size("ep")
    return lax.ppermute(v, "ep", [(i, i ^ 1) for i in range(n)])


def ring(v):
    n = lax.axis_size("ep")
    return lax.ppermute(v, "ep", [(i, (i + 2) % n) for i in range(n)])


def shift(v, steps):
    n = lax.axis_size("ep")
    return lax.ppermute(v, "ep", [(i, (i + 2 * steps) % n) for i in range(n)])


def after(v, *others):
    return lax.optimization_barrier((v, others))[0]


def gather_hp(v):
    far = swap_y(v)
    return [v, far, swap_core(v), swap_core(far)]


def scatter_hp(parts):
    near = swap_core(parts[2].astype(BF)).astype(F32) + parts[0].astype(F32)
    over = swap_core(parts[3].astype(BF)).astype(F32) + parts[1].astype(F32)
    return near + swap_y(over.astype(BF)).astype(F32)


def crossed(b, h):
    odd, high = (h & 1) == 1, (h & 2) == 2
    c = [jnp.where(odd, b[i ^ 1], b[i]) for i in range(4)]
    return [jnp.where(high, c[i ^ 2], c[i]) for i in range(4)]


def relative(v, h, axis):
    c = crossed(jnp.split(v, 4, axis=axis), h)
    return jnp.concatenate([c[0], c[2], c[1], c[3]], axis=axis)


def absolute(v, h, axis):
    b = jnp.split(v, 4, axis=axis)
    return jnp.concatenate(crossed([b[0], b[2], b[1], b[3]], h), axis=axis)


def gather_ep(v):
    stages = lax.axis_size("ep") // 2
    own, out = v, []
    for k in range(stages):
        out.append((own, swap_pair(own)))
        if k < stages - 1:
            own = ring(own)
    return out


def scatter_ep(parts):
    stages = len(parts)
    total = None
    for k in list(range(1, stages)) + [0]:
        here = parts[k][0].astype(F32) + swap_pair(parts[k][1]).astype(F32)
        if total is not None:
            here = here + total.astype(F32)
        total = here if k == 0 else ring(here.astype(BF))
    return total


def spread_ep(v, e):
    n = lax.axis_size("ep")
    stages = n // 2
    x, z = e & 1, e >> 1
    column = lax.dynamic_update_index_in_dim(jnp.zeros((stages,) + v.shape, v.dtype), v, z, 0)
    for step in range(1, stages):
        column = lax.dynamic_update_index_in_dim(
            column, shift(v, step), (z + stages - step) % stages, 0
        )
    far = swap_pair(column)
    both = [jnp.where(x == 0, column, far), jnp.where(x == 0, far, column)]
    return jnp.stack(both, axis=1).reshape((n,) + v.shape)


def sum_ep(v, e):
    n = lax.axis_size("ep")
    stages = n // 2
    x, z = e & 1, e >> 1
    halves = v.reshape(2, v.shape[0] // 2, v.shape[1])
    mine = lax.dynamic_index_in_dim(halves, x, 0, False)
    other = lax.dynamic_index_in_dim(halves, 1 - x, 0, False)
    mine = mine + swap_pair(other.astype(BF)).astype(F32)
    chunks = mine.reshape(stages, mine.shape[0] // stages, mine.shape[1])
    low = chunks.astype(BF)
    total = lax.dynamic_index_in_dim(chunks, z, 0, False)
    for step in range(1, stages):
        part = lax.dynamic_index_in_dim(low, (z + step) % stages, 0, False)
        total = total + shift(part, step).astype(F32)
    total = total.astype(BF)
    half = lax.dynamic_update_index_in_dim(jnp.zeros(chunks.shape, BF), total, z, 0)
    for step in range(1, stages):
        half = lax.dynamic_update_index_in_dim(
            half, shift(total, step), (z + stages - step) % stages, 0
        )
    half = half.reshape(mine.shape)
    far = swap_pair(half)
    low = jnp.where(x == 0, half, far)
    high = jnp.where(x == 0, far, half)
    return jnp.concatenate([low, high], axis=0).astype(F32)


def sum_all_small(v):
    v = v + swap_core(v)
    v = v + swap_y(v)
    n = lax.axis_size("ep")
    bit = 1
    while bit < n:
        v = v + lax.ppermute(v, "ep", [(i, i ^ bit) for i in range(n)])
        bit *= 2
    return v


def score_mask(h, rows, cols):
    at = lax.broadcasted_iota(jnp.int32, (rows, cols), 0) + h * rows
    key = lax.broadcasted_iota(jnp.int32, (rows, cols), 1)
    block = key // rows
    other = jnp.where(
        block == 0, h, jnp.where(block == 1, h ^ 2, jnp.where(block == 2, h ^ 1, h ^ 3))
    )
    return other * rows + key % rows <= at


def turned(v, cosine, sine):
    return v * cosine + pltpu.roll(v, HD // 2, 1) * sine


def project_kernel(
    t_ref, f_ref, gain_ref, k_ref, v_ref, q_ref, cos_ref, sin_ref, x_ref, kv_ref, query_ref
):
    rows = query_ref.shape[0]

    @pl.when(pl.program_id(0) == 0)
    def _():
        for i, ref in enumerate((t_ref, f_ref)):
            v = ref[...].astype(F32)
            x_ref[i * rows : (i + 1) * rows, :] = (v * rms(v) * gain_ref[...]).astype(BF)

    x = x_ref[...]
    cosine, sine = cos_ref[...], sin_ref[...]
    keys, query = dot(x, k_ref[...]), dot(x[:rows], q_ref[...])
    kv_ref[1] = dot(x, v_ref[...]).astype(BF)
    for i in range(k_ref.shape[1] // HD):
        span = slice(i * HD, (i + 1) * HD)
        kv_ref[0, :, span] = turned(keys[:, span], cosine, sine).astype(BF)
        query_ref[:, span] = turned(query[:, span], cosine[:rows], sine[:rows]).astype(BF)


def project(tokens, far, gain, k_w, v_w, q_w, cosine, sine):
    rows, width = tokens.shape
    two, block = 2 * rows, 2 * HD
    cols = pl.BlockSpec((width, block), lambda i: (0, i))

    def fixed(v):
        return pl.BlockSpec(v.shape, lambda i: (0, 0))

    return pl.pallas_call(
        project_kernel,
        grid=(width // block,),
        in_specs=[fixed(tokens), fixed(far), fixed(gain), cols, cols, cols]
        + [pl.BlockSpec((two, HD), lambda i: (0, 0))] * 2,
        out_specs=[
            pl.BlockSpec((two, width), lambda i: (0, 0)),
            pl.BlockSpec((2, two, block), lambda i: (0, 0, i)),
            pl.BlockSpec((rows, block), lambda i: (0, i)),
        ],
        out_shape=[
            jax.ShapeDtypeStruct((two, width), BF),
            jax.ShapeDtypeStruct((2, two, width), BF),
            jax.ShapeDtypeStruct((rows, width), BF),
        ],
        compiler_params=pltpu.CompilerParams(vmem_limit_bytes=40 * MIB),
        cost_estimate=pl.CostEstimate(flops=0, bytes_accessed=0, transcendentals=0),
    )(tokens, far, gain, k_w, v_w, q_w, cosine, sine)


def attend_kernel(h_ref, q_ref, ka_ref, kb_ref, va_ref, vb_ref, o_ref, lse_ref):
    rows = q_ref.shape[0]
    half = ka_ref.shape[0]
    q = q_ref[...]
    s = jnp.concatenate([dot(q, ka_ref[...], (1, 1)), dot(q, kb_ref[...], (1, 1))], axis=1)
    s = jnp.where(score_mask(h_ref[0], rows, 2 * half), s * HD ** (-0.5), -1e30)
    top = jnp.max(s, axis=1, keepdims=True)
    p = jnp.exp(s - top)
    total = jnp.sum(p, axis=1, keepdims=True)
    p = (p * (1.0 / total)).astype(BF)
    o = dot(p[:, :half], va_ref[...]) + dot(p[:, half:], vb_ref[...])
    o_ref[...] = o.astype(BF)
    lse_ref[...] = jnp.broadcast_to(top + jnp.log(total), lse_ref.shape)


def attend_back_kernel(
    h_ref,
    q_ref,
    ka_ref,
    kb_ref,
    va_ref,
    vb_ref,
    d_ref,
    lse_ref,
    cos_ref,
    sin_ref,
    dq_ref,
    da_ref,
    db_ref,
):
    rows = q_ref.shape[0]
    half = ka_ref.shape[0]
    q, d = q_ref[...], d_ref[...]
    cosine, sine = cos_ref[...], -sin_ref[...]
    s = jnp.concatenate([dot(q, ka_ref[...], (1, 1)), dot(q, kb_ref[...], (1, 1))], axis=1)
    s = jnp.where(score_mask(h_ref[0], rows, 2 * half), s * HD ** (-0.5), -1e30)
    p = jnp.exp(s - lse_ref[:, 0:1])
    back = jnp.concatenate([dot(d, va_ref[...], (1, 1)), dot(d, vb_ref[...], (1, 1))], axis=1)
    inner = jnp.sum(p * back, axis=1, keepdims=True)
    sb = (p * (back - inner) * HD ** (-0.5)).astype(BF)
    p = p.astype(BF)
    dq = dot(sb[:, :half], ka_ref[...]) + dot(sb[:, half:], kb_ref[...])
    dq_ref[...] = turned(dq, cosine[:rows], sine[:rows]).astype(BF)
    dk = turned(dot(sb, q, (0, 0)), cosine, sine)
    dv = dot(p, d, (0, 0))
    da_ref[0] = dk[:half]
    da_ref[1] = dv[:half]
    db_ref[0] = dk[half:].astype(BF)
    db_ref[1] = dv[half:].astype(BF)


def head_spec(rows):
    return pl.BlockSpec((rows, HD), lambda i, h: (0, i))


def kv_spec(rows, which):
    return pl.BlockSpec((None, rows, HD), lambda i, h: (which, 0, i))


def attend(h, q, kv_a, kv_b):
    rows, width = q.shape
    half = kv_a.shape[1]
    return pl.pallas_call(
        attend_kernel,
        grid_spec=pltpu.PrefetchScalarGridSpec(
            num_scalar_prefetch=1,
            grid=(H,),
            in_specs=[
                head_spec(rows),
                kv_spec(half, 0),
                kv_spec(half, 0),
                kv_spec(half, 1),
                kv_spec(half, 1),
            ],
            out_specs=[head_spec(rows), head_spec(rows)],
        ),
        out_shape=[
            jax.ShapeDtypeStruct((rows, width), BF),
            jax.ShapeDtypeStruct((rows, width), F32),
        ],
        compiler_params=pltpu.CompilerParams(vmem_limit_bytes=40 * MIB),
        cost_estimate=pl.CostEstimate(flops=0, bytes_accessed=0, transcendentals=0),
    )(h, q, kv_a, kv_b, kv_a, kv_b)


def attend_back(h, q, kv_a, kv_b, d, lse, cosine, sine):
    rows, width = q.shape
    half = kv_a.shape[1]
    flops = 10 * rows * 2 * half * width
    table = pl.BlockSpec((2 * half, HD), lambda i, h: (0, 0))
    both = pl.BlockSpec((2, half, HD), lambda i, h: (0, 0, i))
    return pl.pallas_call(
        attend_back_kernel,
        grid_spec=pltpu.PrefetchScalarGridSpec(
            num_scalar_prefetch=1,
            grid=(H,),
            in_specs=[
                head_spec(rows),
                kv_spec(half, 0),
                kv_spec(half, 0),
                kv_spec(half, 1),
                kv_spec(half, 1),
                head_spec(rows),
                head_spec(rows),
                table,
                table,
            ],
            out_specs=[head_spec(rows), both, both],
        ),
        out_shape=[
            jax.ShapeDtypeStruct((rows, width), BF),
            jax.ShapeDtypeStruct((2, half, width), F32),
            jax.ShapeDtypeStruct((2, half, width), BF),
        ],
        compiler_params=pltpu.CompilerParams(vmem_limit_bytes=40 * MIB),
        cost_estimate=pl.CostEstimate(
            flops=flops, bytes_accessed=16 * MIB, transcendentals=rows * 2 * half * H
        ),
    )(h, q, kv_a, kv_b, kv_a, kv_b, d, lse, cosine, sine)


def pick_matrix(meta, col, capacity):
    lane = lax.broadcasted_iota(jnp.int32, meta.shape, 1)
    code = jnp.sum(jnp.where(lane == col, meta.astype(F32), 0.0), axis=1, keepdims=True)
    place = lax.broadcasted_iota(jnp.int32, (meta.shape[0], capacity), 1).astype(F32)
    return jnp.where(code == place, 1.0, 0.0).astype(BF)


def expert_kernel(capacity, total, olds, e_ref, x0_ref, x1_ref, g0_ref, g1_ref, *refs):
    gates, ups, downs = refs[0:4], refs[4:8], refs[8:12]
    sg_ref, su_ref, sd_ref, sgg_old, sdg_old = refs[12:17]
    (
        dx0_ref,
        dx1_ref,
        sgg_ref,
        sdg_ref,
        sa_ref,
        xr_ref,
        gr_ref,
        gi_ref,
        ui_ref,
        wa_ref,
    ) = refs[17 + olds :]
    xs, gs, dxs = (x0_ref, x1_ref), (g0_ref, g1_ref), (dx0_ref, dx1_ref)
    width = sg_ref.shape[0]
    tokens = x0_ref.shape[0]
    c = capacity
    x2 = jnp.concatenate([r[:, :width] for r in xs], axis=0)
    g2 = jnp.concatenate([r[:, :width] for r in gs], axis=0)
    hg, hu = dot(x2, sg_ref[...]), dot(x2, su_ref[...])
    ab = dot(g2, sd_ref[...], (1, 1))
    s = jax.nn.sigmoid(hg)
    silu = hg * s
    act = (silu * hu).astype(BF)
    gi = (ab * hu * (s * (1.0 + hg * (1.0 - s)))).astype(BF)
    ui = (ab * silu).astype(BF)
    sa_ref[0] = act
    gu = jnp.concatenate([gi, ui], axis=1)
    sgg_ref[...] = sgg_old[...] + dot(x2, gu, (0, 0))
    sdg_ref[...] = sdg_old[...] + dot(act, g2, (0, 0))
    dx = dot(gi, sg_ref[...], (1, 1)) + dot(ui, su_ref[...], (1, 1))
    totals = [dx[:tokens], dx[tokens:]]
    metas = [0.0, 0.0]
    lane = lax.broadcasted_iota(jnp.int32, (2 * c, LANES), 1)
    for x in range(2):
        col = 2 * e_ref[0] + x
        picks, weights = [], []
        for j in range(2):
            pick = pick_matrix(xs[j][:, width:], total + col, c)
            picks.append(pick)
            rows = dot(pick, xs[j][...], (0, 0))
            xr_ref[x, 0, j * c : (j + 1) * c, :] = rows[:, :width].astype(BF)
            weights.append(rows[:, width:])
            gr_ref[x, 0, j * c : (j + 1) * c, :] = dot(pick, gs[j][:, :width], (0, 0)).astype(BF)
        w = jnp.concatenate(weights, axis=0)
        w = jnp.sum(jnp.where(lane == col, w, 0.0), axis=1, keepdims=True)
        xr, gr = xr_ref[x, 0], gr_ref[x, 0]
        dxr = jnp.zeros((2 * c, width), F32)
        wb = jnp.zeros((2 * c, 1), F32)
        for r in range(4):
            wg, wu, wd = gates[r][x], ups[r][x], downs[r][x]
            hg, hu = dot(xr, wg), dot(xr, wu)
            ab = dot(gr, wd, (1, 1))
            s = jax.nn.sigmoid(hg)
            silu = hg * s
            act = silu * hu
            wb = wb + jnp.sum(act * ab, axis=1, keepdims=True)
            ab = ab * w
            gi = (ab * hu * (s * (1.0 + hg * (1.0 - s)))).astype(BF)
            ui = (ab * silu).astype(BF)
            gi_ref[r, x, 0] = gi
            ui_ref[r, x, 0] = ui
            wa_ref[r, x, 0] = (act * w).astype(BF)
            dxr = dxr + dot(gi, wg, (1, 1)) + dot(ui, wu, (1, 1))
        dxr = dxr.astype(BF)
        high = wb.astype(BF).astype(F32)
        meta = jnp.where(lane == col, high, 0.0) + jnp.where(lane == total + col, wb - high, 0.0)
        meta = meta.astype(BF)
        for j in range(2):
            span = slice(j * c, (j + 1) * c)
            totals[j] = totals[j] + dot(picks[j], dxr[span])
            metas[j] = metas[j] + dot(picks[j], meta[span])
    for j in range(2):
        dxs[j][:, :width] = totals[j].astype(BF)
        dxs[j][:, width:] = metas[j].astype(BF)


def expert_out_kernel(capacity, total, e_ref, x0_ref, x1_ref, wa_ref, sa_ref, *refs):
    downs, sd_ref, outs = refs[0:4], refs[4], refs[5:7]
    width = sd_ref.shape[1]
    tokens = x0_ref.shape[0]
    c = capacity
    xs = (x0_ref, x1_ref)
    shared = dot(sa_ref[0], sd_ref[...])
    totals = [shared[:tokens], shared[tokens:]]
    for x in range(2):
        rows = jnp.zeros((2 * c, width), F32)
        for r in range(4):
            rows = rows + dot(wa_ref[r, x, 0], downs[r][x])
        rows = rows.astype(BF)
        for j in range(2):
            pick = pick_matrix(xs[j][...], total + 2 * e_ref[0] + x, c)
            totals[j] = totals[j] + dot(pick, rows[j * c : (j + 1) * c])
    for j in range(2):
        outs[j][...] = totals[j].astype(BF)


def whole(shape):
    return pl.BlockSpec(shape, lambda i, e: (0,) * len(shape), pipeline_mode=pl.Buffered(1))


def expert_stage(
    k, stages, capacity, total, e, x_pair, g_pair, gates, ups, downs, sg, su, sd, carry, bufs
):
    tokens, wide = x_pair[0].shape
    width = sg.shape[0]
    hidden = gates[0].shape[2]
    c2 = 2 * capacity
    shared = sg.shape[1]
    olds = 0 if bufs is None else 6
    shapes = [
        ((stages, 2 * tokens, shared), (1, 2 * tokens, shared), (k, 0, 0)),
        ((2, stages, c2, width), (2, 1, c2, width), (0, k, 0, 0)),
        ((2, stages, c2, width), (2, 1, c2, width), (0, k, 0, 0)),
        ((4, 2, stages, c2, hidden), (4, 2, 1, c2, hidden), (0, 0, k, 0, 0)),
        ((4, 2, stages, c2, hidden), (4, 2, 1, c2, hidden), (0, 0, k, 0, 0)),
        ((4, 2, stages, c2, hidden), (4, 2, 1, c2, hidden), (0, 0, k, 0, 0)),
    ]

    def at(block, where):
        return pl.BlockSpec(block, lambda i, e: where)

    ins = [e, *x_pair, *g_pair, *gates, *ups, *downs, sg, su, sd, *carry]
    in_specs = [whole(v.shape) for v in ins[1:]]
    alias = {}
    if bufs is not None:
        for n, b in enumerate(bufs):
            alias[len(ins)] = 4 + n
            ins.append(b)
            in_specs.append(pl.BlockSpec(memory_space=pl.ANY))
    out_shape = [jax.ShapeDtypeStruct((tokens, wide), BF)] * 2 + [
        jax.ShapeDtypeStruct(v.shape, v.dtype) for v in carry
    ]
    out_specs = [whole((tokens, wide))] * 2 + [whole(v.shape) for v in carry]
    for full, block, where in shapes:
        out_shape.append(jax.ShapeDtypeStruct(full, BF))
        out_specs.append(at(block, where))
    outs = pl.pallas_call(
        functools.partial(expert_kernel, capacity, total, olds),
        grid_spec=pltpu.PrefetchScalarGridSpec(
            num_scalar_prefetch=1, grid=(1,), in_specs=in_specs, out_specs=out_specs
        ),
        out_shape=out_shape,
        input_output_aliases=alias,
        compiler_params=pltpu.CompilerParams(vmem_limit_bytes=60 * MIB),
        cost_estimate=pl.CostEstimate(
            flops=20 * c2 * width * 4 * hidden, bytes_accessed=24 * MIB, transcendentals=c2 * 8 * hidden
        ),
    )(*ins)
    return outs[0:2], outs[2:4], outs[4:]


def expert_out(k, capacity, total, e, x_pair, wa, sa, downs, sd):
    tokens = x_pair[0].shape[0]
    width = sd.shape[1]
    c2 = wa.shape[3]
    last = x_pair[0].shape[1] // LANES - 1
    meta = pl.BlockSpec((tokens, LANES), lambda i, e: (0, last))
    return pl.pallas_call(
        functools.partial(expert_out_kernel, capacity, total),
        grid_spec=pltpu.PrefetchScalarGridSpec(
            num_scalar_prefetch=1,
            grid=(1,),
            in_specs=[
                meta,
                meta,
                pl.BlockSpec((4, 2, 1, c2, wa.shape[4]), lambda i, e: (0, 0, k, 0, 0)),
                pl.BlockSpec((1,) + sa.shape[1:], lambda i, e: (k, 0, 0)),
            ]
            + [whole(d.shape) for d in downs]
            + [whole(sd.shape)],
            out_specs=[whole((tokens, width))] * 2,
        ),
        out_shape=[jax.ShapeDtypeStruct((tokens, width), BF)] * 2,
        compiler_params=pltpu.CompilerParams(vmem_limit_bytes=40 * MIB),
        cost_estimate=pl.CostEstimate(
            flops=4 * c2 * width * 4 * wa.shape[4], bytes_accessed=10 * MIB, transcendentals=0
        ),
    )(e, *x_pair, wa, sa, *downs, sd)


def dispatch_kernel(capacity, total, x_ref, m_ref, g0_ref, g1_ref, g_all, *refs):
    experts = refs[0:3]
    sg_ref, su_ref, sd_ref = refs[3:6]
    dx_ref, wb_ref, near_ref, far_ref, sgg_ref, sdg_ref = refs[6:12]
    xr_ref, gr_ref, gu_ref, wa_ref, last_ref, down_far, down_last = refs[12:19]
    xbuf, sbuf, tbuf, mbuf, nbuf, bbuf, sbbuf, tbbuf, wgu, wd, gbuf, gown, acts, wacts = refs[19:33]
    (
        rx_s,
        rx_r,
        sx_s,
        sx_r,
        sr_s,
        sr_r,
        rt_s,
        rt_r,
        rm_s,
        rm_r,
        sm_s,
        sm_r,
        sb_s,
        sb_r,
        rb_s,
        rb_r,
        w_sem,
        l_s,
        l_r,
    ) = refs[33:]
    experts = experts + (last_ref,)
    k = pl.program_id(0)
    stages = xbuf.shape[0]
    tokens, width = x_ref.shape[0], sg_ref.shape[0]
    hidden = experts[0].shape[1] // 3
    inner = 4 * hidden
    c = capacity
    last = stages - 1
    e, h = lax.axis_index("ep"), lax.axis_index("hp")
    n = 2 * stages
    right, left = (lax.rem(e + 2, n), h), (lax.rem(e + n - 2, n), h)
    pair = (e + 1 - 2 * lax.rem(e, 2), h)
    core = (e, h + 1 - 2 * lax.rem(h, 2))
    y_far = (e, lax.rem(h + 2, 4))

    def ring_x(i):
        return mesh_copy(xbuf.at[i, 0], xbuf.at[i + 1, 0], rx_s, rx_r, i, right)

    def ring_last():
        return mesh_copy(xbuf.at[last - 1, 1], xbuf.at[last, 1], rx_s, rx_r, last, right)

    def swap_x(i):
        return mesh_copy(xbuf.at[i, 0], xbuf.at[i, 1], sx_s, sx_r, i, pair)

    def ring_m(i):
        return mesh_copy(mbuf.at[i], mbuf.at[i + 1], rm_s, rm_r, i, right)

    def swap_m(i):
        return mesh_copy(mbuf.at[i], nbuf.at[i], sm_s, sm_r, i, pair)

    def swap_r(i):
        return mesh_copy(xbuf.at[i, 1], sbuf.at[i], sr_s, sr_r, i, pair)

    def ring_t(i):
        return mesh_copy(xbuf.at[i, 0], tbuf.at[i], rt_s, rt_r, i, right)

    def swap_b(i):
        return mesh_copy(bbuf.at[i, 1], sbbuf.at[i], sb_s, sb_r, i, pair)

    def ring_b(i):
        return mesh_copy(bbuf.at[i, 0], tbbuf.at[i], rb_s, rb_r, i, right)

    to_core = mesh_copy(experts[1], last_ref, l_s, l_r, 0, core)
    down_over = mesh_copy(
        experts[0].at[:, pl.ds(2 * hidden, hidden), :], down_far, l_s, l_r, 1, y_far
    )
    down_on = mesh_copy(down_far, down_last, l_s, l_r, 2, core)
    last_g = mesh_copy(g_all.at[last], gbuf, l_s, l_r, 3, pair)

    def weight_copies(r):
        copies = []
        for x in range(2):
            for i, (to, at) in enumerate(((wgu, 0), (wgu, inner), (wd, 0))):
                if i == 2 and r % 2 == 1:
                    src = (down_far if r == 1 else down_last).at[x]
                else:
                    src = experts[r].at[x, pl.ds(i * hidden, hidden), :]
                copies.append(
                    pltpu.make_async_copy(
                        src,
                        to.at[x, pl.ds(at + r * hidden, hidden), :],
                        w_sem.at[6 * r + 3 * x + i],
                    )
                )
        return copies

    @pl.when(k == 0)
    def _():
        xbuf[0, 0] = x_ref[...]
        mbuf[0] = m_ref[...]
        greet((right, left, pair, core, y_far))
        down_over.start()
        ring_m(0).start()
        swap_m(0).start()
        ring_x(0).start()
        swap_x(0).start()
        to_core.start()
        for r in (0, 2):
            for copy in weight_copies(r):
                copy.start()
        sgg_ref[...] = jnp.zeros_like(sgg_ref)
        sdg_ref[...] = jnp.zeros_like(sdg_ref)

    @pl.when(k < last)
    def _():
        ring_m(k).wait_recv()
        swap_m(k + 1).start()
        ring_x(k).wait_recv()

    @pl.when(k < last - 1)
    def _():
        ring_m(k + 1).start()
        ring_x(k + 1).start()
        swap_x(k + 1).start()

    @pl.when(k < last)
    def _():
        swap_x(k).wait_recv()

    @pl.when(k == last - 2)
    def _():
        last_g.start()

    @pl.when(k == last - 1)
    def _():
        ring_last().start()

    @pl.when(k < last)
    def _():
        gown[...] = g1_ref[0]

    @pl.when(k == last)
    def _():
        ring_last().wait_recv()
        last_g.wait()
        gown[...] = gbuf[...]

    swap_m(k).wait_recv()

    @pl.when(k == 0)
    def _():
        down_over.wait_recv()
        down_on.start()
        for copy in weight_copies(1):
            copy.start()
        to_core.wait()
        down_on.wait()
        for copy in weight_copies(3):
            copy.start()
        down_over.wait_send()
        for r in range(4):
            for copy in weight_copies(r):
                copy.wait()

    gs = (g0_ref.at[0], gown)
    x2 = jnp.concatenate([xbuf[k, j] for j in range(2)], axis=0)
    g2 = jnp.concatenate([g[...] for g in gs], axis=0)
    hg, hu = dot(x2, sg_ref[...]), dot(x2, su_ref[...])
    ab = dot(g2, sd_ref[...], (1, 1))
    s = jax.nn.sigmoid(hg)
    silu = hg * s
    act = (silu * hu).astype(BF)
    gi = (ab * hu * (s * (1.0 + hg * (1.0 - s)))).astype(BF)
    ui = (ab * silu).astype(BF)
    sgg_ref[...] += dot(x2, jnp.concatenate([gi, ui], axis=1), (0, 0))
    sdg_ref[...] += dot(act, g2, (0, 0))
    acts[k] = act
    dx = dot(gi, sg_ref[...], (1, 1)) + dot(ui, su_ref[...], (1, 1))
    totals = [dx[:tokens], dx[tokens:]]
    backs = [0.0, 0.0]
    line = lax.broadcasted_iota(jnp.int32, m_ref.shape, 0)
    short = lax.broadcasted_iota(jnp.int32, (total, tokens), 0)
    place = lax.broadcasted_iota(jnp.int32, (c, tokens), 0).astype(F32)

    def hits(i, j, x):
        code = jnp.where(line == total + 2 * e + x, (mbuf, nbuf)[j][i], 0.0)
        return jnp.sum(code, axis=0, keepdims=True) == place

    for x in range(2):
        col = 2 * e + x
        picks, weights, found = [], [], []
        for j in range(2):
            weight = jnp.where(line == col, (mbuf, nbuf)[j][k], 0.0)
            weight = jnp.sum(weight, axis=0, keepdims=True)
            hit = hits(k, j, x)
            pick = jnp.where(hit, 1.0, 0.0).astype(BF)
            found.append(hit)
            picks.append(pick)
            weights.append(jnp.sum(jnp.where(hit, weight, 0.0), axis=1, keepdims=True))
            xr_ref[x, 0, j * c : (j + 1) * c, :] = dot(pick, xbuf[k, j]).astype(BF)
            gr_ref[x, 0, j * c : (j + 1) * c, :] = dot(pick, gs[j][...]).astype(BF)
        w = jnp.concatenate(weights, axis=0)
        xr, gr = xr_ref[x, 0], gr_ref[x, 0]
        hgu = dot(xr, wgu[x], (1, 1))
        ab = dot(gr, wd[x], (1, 1))
        hg, hu = hgu[:, :inner], hgu[:, inner:]
        s = jax.nn.sigmoid(hg)
        silu = hg * s
        act = silu * hu
        wb = jnp.sum(act * ab, axis=1, keepdims=True)
        ab = ab * w
        gu_ref[x, 0, :, :inner] = (ab * hu * (s * (1.0 + hg * (1.0 - s)))).astype(BF)
        gu_ref[x, 0, :, inner:] = (ab * silu).astype(BF)
        wa_ref[x, 0] = (act * w).astype(BF)
        wacts[k, x] = wa_ref[x, 0]
        dxr = dot(gu_ref[x, 0], wgu[x]).astype(BF)
        for j in range(2):
            span = slice(j * c, (j + 1) * c)
            totals[j] = totals[j] + dot(picks[j], dxr[span], (0, 0))
            row = jnp.sum(jnp.where(found[j], wb[span], 0.0), axis=0, keepdims=True)
            backs[j] = backs[j] + jnp.where(short == col, row, 0.0)

    @pl.when(k < last)
    def _():
        ring_x(k).wait_send()
        swap_x(k).wait_send()

    @pl.when(k == last - 1)
    def _():
        ring_last().wait_send()

    for j in range(2):
        xbuf[k, j] = totals[j].astype(BF)
        bbuf[k, j] = backs[j]

    @pl.when(k >= 1)
    def _():
        swap_b(k).start()
        swap_r(k).start()

    def advance(i, first):
        swap_b(i).wait_recv()
        swap_r(i).wait_recv()
        here = xbuf[i, 0].astype(F32) + sbuf[i].astype(F32)
        small = bbuf[i, 0] + sbbuf[i]
        if not first:
            ring_b(i - 1).wait_recv()
            ring_t(i - 1).wait_recv()
            here = here + tbuf[i - 1].astype(F32)
            small = small + tbbuf[i - 1]
        xbuf[i, 0] = here.astype(BF)
        bbuf[i, 0] = small
        ring_b(i).start()
        ring_t(i).start()

    for i in range(1, last):

        @pl.when(k == i + 1)
        def _(i=i):
            advance(i, i == 1)

    def forward(i):
        out = dot(acts[i], sd_ref[...])
        outs = [out[:tokens], out[tokens:]]
        for x in range(2):
            rows = dot(wacts[i, x], wd[x]).astype(BF)
            for j in range(2):
                pick = jnp.where(hits(i, j, x), 1.0, 0.0).astype(BF)
                outs[j] = outs[j] + dot(pick, rows[j * c : (j + 1) * c], (0, 0))
        near_ref[i] = outs[0].astype(BF)
        far_ref[i] = outs[1].astype(BF)

    @pl.when(k == last)
    def _():
        swap_b(0).start()
        swap_r(0).start()
        for i in range(stages // 2 + 1):
            forward(i)
        advance(last, last == 1)
        for i in range(stages // 2 + 1, stages):
            forward(i)
        swap_b(0).wait_recv()
        swap_r(0).wait_recv()
        ring_b(last).wait_recv()
        ring_t(last).wait_recv()
        dx_ref[...] = xbuf[0, 0].astype(F32) + sbuf[0].astype(F32) + tbuf[last].astype(F32)
        wb_ref[...] = bbuf[0, 0] + sbbuf[0] + tbbuf[last]
        for i in range(stages):
            swap_r(i).wait_send()
            swap_b(i).wait_send()
            swap_m(i).wait_send()
        for i in range(1, stages):
            ring_t(i).wait_send()
            ring_b(i).wait_send()
            ring_m(i - 1).wait_send()


def dispatch(capacity, total, x, meta, g_near, g_far, experts, sg, su, sd):
    stages = g_near.shape[0]
    most = stages - 1
    tokens, width = x.shape
    lines = meta.shape[0]
    shared = sg.shape[1]
    hidden = experts[0].shape[1] // 3
    inner = 4 * hidden
    c2 = 2 * capacity
    once = pl.Buffered(1)
    dma = pltpu.SemaphoreType.DMA

    def fixed(shape):
        return pl.BlockSpec(shape, lambda k: (0,) * len(shape), pipeline_mode=once)

    def per_stage(shape):
        return pl.BlockSpec(shape, lambda k: (0, k, 0, 0), pipeline_mode=once)

    anywhere = pl.BlockSpec(memory_space=pl.ANY)
    return pl.pallas_call(
        functools.partial(dispatch_kernel, capacity, total),
        grid=(stages,),
        in_specs=[
            fixed((tokens, width)),
            fixed(meta.shape),
            pl.BlockSpec((1, tokens, width), lambda k: (k, 0, 0)),
            pl.BlockSpec((1, tokens, width), lambda k: (k - k // most, 0, 0)),
            anywhere,
        ]
        + [anywhere] * 3
        + [fixed(sg.shape), fixed(su.shape), fixed(sd.shape)],
        out_specs=[
            fixed((tokens, width)),
            fixed((total, tokens)),
            fixed((stages, tokens, width)),
            fixed((stages, tokens, width)),
            fixed((width, 2 * shared)),
            fixed((shared, width)),
            per_stage((2, 1, c2, width)),
            per_stage((2, 1, c2, width)),
            per_stage((2, 1, c2, 2 * inner)),
            per_stage((2, 1, c2, inner)),
            anywhere,
            anywhere,
            anywhere,
        ],
        out_shape=[
            jax.ShapeDtypeStruct((tokens, width), F32),
            jax.ShapeDtypeStruct((total, tokens), F32),
            jax.ShapeDtypeStruct((stages, tokens, width), BF),
            jax.ShapeDtypeStruct((stages, tokens, width), BF),
            jax.ShapeDtypeStruct((width, 2 * shared), F32),
            jax.ShapeDtypeStruct((shared, width), F32),
            jax.ShapeDtypeStruct((2, stages, c2, width), BF),
            jax.ShapeDtypeStruct((2, stages, c2, width), BF),
            jax.ShapeDtypeStruct((2, stages, c2, 2 * inner), BF),
            jax.ShapeDtypeStruct((2, stages, c2, inner), BF),
            jax.ShapeDtypeStruct(experts[1].shape, BF),
            jax.ShapeDtypeStruct((2, hidden, width), BF),
            jax.ShapeDtypeStruct((2, hidden, width), BF),
        ],
        scratch_shapes=[
            pltpu.VMEM((stages, 2, tokens, width), BF),
            pltpu.VMEM((stages, tokens, width), BF),
            pltpu.VMEM((stages, tokens, width), BF),
            pltpu.VMEM((stages, lines, tokens), F32),
            pltpu.VMEM((stages, lines, tokens), F32),
            pltpu.VMEM((stages, 2, total, tokens), F32),
            pltpu.VMEM((stages, total, tokens), F32),
            pltpu.VMEM((stages, total, tokens), F32),
            pltpu.VMEM((2, 2 * inner, width), BF),
            pltpu.VMEM((2, inner, width), BF),
            pltpu.VMEM((tokens, width), BF),
            pltpu.VMEM((tokens, width), BF),
            pltpu.VMEM((stages, 2 * tokens, shared), BF),
            pltpu.VMEM((stages, 2, c2, inner), BF),
        ]
        + [dma((stages,))] * 16
        + [dma((24,))]
        + [dma((4,))] * 2,
        compiler_params=pltpu.CompilerParams(
            vmem_limit_bytes=63 * MIB, collective_id=0, has_side_effects=True
        ),
        cost_estimate=pl.CostEstimate(
            flops=24 * c2 * stages * width * 4 * hidden,
            bytes_accessed=80 * MIB,
            transcendentals=stages * c2 * 8 * hidden,
        ),
    )(x, meta, g_near, g_far, g_near, *experts, sg, su, sd)[:10]


def expert_grad_kernel(
    xr_ref, gr_ref, gu_ref, wa_ref, near_ref, far_ref, keep, sendb, recvb, s_s, s_r
):
    s = pl.program_id(0)
    steps = sendb.shape[0]
    half = sendb.shape[1]
    h = lax.axis_index("hp")
    core = (lax.axis_index("ep"), h + 1 - 2 * lax.rem(h, 2))

    def over_core(n):
        return mesh_copy(sendb.at[n], recvb.at[n], s_s, s_r, n, core)

    @pl.when(s == 0)
    def _():
        greet([core])

    def give(v):
        sendb[s] = v[half:].astype(BF)
        over_core(s).start()
        keep[lax.rem(s, 2)] = v[:half].astype(BF)

    @pl.when((s < steps) & (lax.rem(s, 3) < 2))
    def _():
        give(dot(gu_ref[0], xr_ref[0], (0, 0)))

    @pl.when((s < steps) & (lax.rem(s, 3) == 2))
    def _():
        give(dot(wa_ref[0], gr_ref[0], (0, 0)))

    @pl.when(s > 0)
    def _():
        n = s - 1
        over_core(n).wait_recv()
        total = (keep[lax.rem(n, 2)].astype(F32) + recvb[n].astype(F32)).astype(BF)
        near_ref[0, 0] = total[: half // 2]
        far_ref[0, 0] = total[half // 2 :]

    @pl.when(s == steps)
    def _():
        for n in range(steps):
            over_core(n).wait_send()


def expert_grads(xr, gr, gu, wa, hidden):
    rows, width = xr.shape[1:]
    inner, steps = 4 * hidden, 6
    dma = pltpu.SemaphoreType.DMA

    def now(s):
        return s - s // steps

    def before(s):
        return s - 1 + (steps - s) // steps

    rows_in = pl.BlockSpec((1, rows, width), lambda s: (now(s) // 3, 0, 0))
    out = pl.BlockSpec((1, 1, hidden, width), lambda s: (before(s) // 3, before(s) % 3, 0, 0))
    near, far = pl.pallas_call(
        expert_grad_kernel,
        grid=(steps + 1,),
        in_specs=[
            rows_in,
            rows_in,
            pl.BlockSpec(
                (1, rows, inner), lambda s: (now(s) // 3, 0, now(s) % 3 - now(s) % 3 // 2)
            ),
            pl.BlockSpec((1, rows, inner), lambda s: (now(s) // 3, 0, 0)),
        ],
        out_specs=[out, out],
        out_shape=[jax.ShapeDtypeStruct((2, 3, hidden, width), BF)] * 2,
        scratch_shapes=[pltpu.VMEM((2, inner // 2, width), BF)]
        + [pltpu.VMEM((steps, inner // 2, width), BF)] * 2
        + [dma((steps,))] * 2,
        compiler_params=pltpu.CompilerParams(
            vmem_limit_bytes=60 * MIB, collective_id=4, has_side_effects=True
        ),
        cost_estimate=pl.CostEstimate(
            flops=12 * rows * inner * width, bytes_accessed=40 * MIB, transcendentals=0
        ),
    )(xr, gr, gu, wa)
    return (v.reshape(2, 3 * hidden, width) for v in (near, far))


def mesh_copy(src, dst, s, r, i, where):
    return pltpu.make_async_remote_copy(
        src_ref=src,
        dst_ref=dst,
        send_sem=s.at[i],
        recv_sem=r.at[i],
        device_id=where,
        device_id_type=pl.DeviceIdType.MESH,
    )


def greet(peers):
    barrier = pltpu.get_barrier_semaphore()
    for where in peers:
        pl.semaphore_signal(barrier, inc=1, device_id=where, device_id_type=pl.DeviceIdType.MESH)
    pl.semaphore_wait(barrier, len(peers))


def front_kernel(large, count, *refs):
    tok_ref, exp_ref, cot_ref = refs[0:3]
    ins = refs[3 : 3 + count]
    far_ref, expo_ref, g_ref = refs[3 + count : 6 + count]
    outs = refs[6 + count : 6 + 2 * count]
    y_s, y_r, c_s, c_r, f_s, f_r, p_s, p_r, q_s, q_r, l_sem, rg_s, rg_r = refs[6 + 2 * count :]
    stages = g_ref.shape[0]
    n = 2 * stages
    e, h = lax.axis_index("ep"), lax.axis_index("hp")
    x = lax.rem(e, 2)
    h_core, h_far = h + 1 - 2 * lax.rem(h, 2), lax.rem(h + 2, 4)
    core, far = (e, h_core), (e, h_far)
    right, left = (lax.rem(e + 2, n), h), (lax.rem(e + n - 2, n), h)
    pair = (e + 1 - 2 * x, h)
    greet((core, far, right, left, pair))

    def ring_g(k):
        src = cot_ref if k == 0 else g_ref.at[k]
        return mesh_copy(src, g_ref.at[k + 1], rg_s, rg_r, k, right)

    def part(i, other=False):
        rows = ins[i].shape[0] // 2
        return pl.ds((1 - x if other else x) * rows, rows)

    over_y, over_pair, onward, onward_too = [], [], [], []
    for i, v in enumerate(ins):
        o = outs[i]
        if i < large:
            mine, theirs = part(i), part(i, True)
            over_y.append(mesh_copy(v.at[mine], o.at[h, mine], y_s, y_r, i, far))
            got, rest = o.at[h_far, mine], o.at[h_far, theirs]
            over_pair.append(mesh_copy(got, got, p_s, p_r, i, pair))
            onward.append(mesh_copy(got, got, f_s, f_r, i, core))
            onward_too.append(mesh_copy(rest, rest, q_s, q_r, i, core))
        else:
            over_y.append(mesh_copy(v, o.at[h], y_s, y_r, i, far))
            onward.append(mesh_copy(o.at[h_far], o.at[h_far], f_s, f_r, i, core))
    over_y.append(mesh_copy(tok_ref, far_ref, y_s, y_r, count, far))
    over_core = [mesh_copy(v, outs[i].at[h], c_s, c_r, i, core) for i, v in enumerate(ins)]
    over_core.append(mesh_copy(exp_ref, expo_ref, c_s, c_r, count, core))
    local = [pltpu.make_async_copy(v, outs[i].at[h], l_sem.at[i]) for i, v in enumerate(ins)]
    local.append(pltpu.make_async_copy(cot_ref, g_ref.at[0], l_sem.at[count]))
    for copy in over_y:
        copy.start()
    ring_g(0).start()
    for copy in over_core + local:
        copy.start()
    for k in range(max(stages - 1, large)):
        if k < large:
            over_y[k].wait_recv()
            over_pair[k].start()
            onward[k].start()
        if k < stages - 1:
            ring_g(k).wait_recv()
            if k + 1 < stages - 1:
                ring_g(k + 1).start()
    for k in range(large, count):
        over_y[k].wait_recv()
        onward[k].start()
    over_y[count].wait_recv()
    for k in range(large):
        over_pair[k].wait_recv()
        onward_too[k].start()
    for copy in over_y + over_pair + [ring_g(k) for k in range(stages - 1)]:
        copy.wait_send()
    for copy in over_core + onward + onward_too + local:
        copy.wait()


def front(stages, tokens, experts, cotangent, blocks, large):
    count = len(blocks)
    anywhere, vmem = (pl.BlockSpec(memory_space=m) for m in (pl.ANY, pltpu.VMEM))
    dma = pltpu.SemaphoreType.DMA
    return pl.pallas_call(
        functools.partial(front_kernel, large, count),
        in_specs=[anywhere] * 2 + [vmem] * (1 + count),
        out_specs=[anywhere] * (3 + count),
        out_shape=[
            jax.ShapeDtypeStruct(tokens.shape, BF),
            jax.ShapeDtypeStruct(experts.shape, BF),
            jax.ShapeDtypeStruct((stages,) + cotangent.shape, BF),
        ]
        + [jax.ShapeDtypeStruct((4,) + v.shape, BF) for v in blocks],
        scratch_shapes=[dma((count + 1,))] * 4
        + [dma((count,))] * 6
        + [dma((count + 1,))]
        + [dma((stages,))] * 2,
        compiler_params=pltpu.CompilerParams(
            vmem_limit_bytes=32 * MIB, collective_id=1, has_side_effects=True
        ),
        cost_estimate=pl.CostEstimate(flops=0, bytes_accessed=120 * MIB, transcendentals=0),
    )(tokens, experts, cotangent, *blocks)


class SharedSum:
    def __init__(self, at, peers, ref, got, to_far, from_far, fin, s, r):
        c, y, x, z = at
        core, far, pair, up = peers
        self.at, self.fin = at, fin
        self.ref, self.got, self.to_far, self.from_far = ref, got, to_far, from_far
        self.core = mesh_copy(ref.at[:, 1 - c], got, s, r, 0, core)
        self.far = mesh_copy(to_far, from_far, s, r, 1, far)
        own = fin.at[x, z]
        self.up = [mesh_copy(own, own, s, r, 1 + k, up[k]) for k in range(1, 4)]
        self.pair = mesh_copy(fin.at[x], fin.at[x], s, r, 5, pair)
        self.all = [self.core, self.far, self.pair] + self.up

    def over_y(self):
        c, y, _, _ = self.at
        self.core.wait_recv()
        total = self.ref[1 - y, c].astype(F32) + self.got[1 - y].astype(F32)
        self.to_far[...] = total.astype(BF)
        self.far.start()

    def over_z(self):
        c, y, x, z = self.at
        self.far.wait_recv()
        total = self.ref[y, c].astype(F32) + self.got[y].astype(F32)
        self.fin[x, z] = (total + self.from_far[...].astype(F32)).astype(BF)
        for copy in self.up:
            copy.start()

    def over_x(self):
        for copy in self.up:
            copy.wait_recv()
        self.pair.start()


def back_kernel(
    q_ref,
    ka_ref,
    kb_ref,
    va_ref,
    vb_ref,
    d_ref,
    lse_ref,
    wq_ref,
    wk_ref,
    wv_ref,
    cos_ref,
    sin_ref,
    x_ref,
    tok_ref,
    ftok_ref,
    sg_ref,
    sd_ref,
    spread_ref,
    stack_ref,
    near_ref,
    mid_ref,
    away_ref,
    piece_ref,
    qp_ref,
    kp_ref,
    vp_ref,
    first_ref,
    share_ref,
    gain_ref,
    sgout_ref,
    suout_ref,
    sdout_ref,
    layer_ref,
    piece_far,
    sendb,
    recvb,
    nearb,
    kvacc,
    qacc,
    sg_c,
    sg_y,
    sg_yr,
    sg_fin,
    sd_c,
    sd_y,
    sd_yr,
    sd_fin,
    xgot,
    zsend,
    zgot,
    k_s,
    k_r,
    s_s,
    s_r,
    d_s,
    d_r,
    x_s,
    x_r,
    z_s,
    z_r,
    p_s,
    p_r,
):
    i = pl.program_id(0)
    heads = sendb.shape[0]
    rows, half = q_ref.shape[0], ka_ref.shape[0]
    e, h = lax.axis_index("ep"), lax.axis_index("hp")
    x, z = lax.rem(e, 2), e // 2
    c, y = lax.rem(h, 2), h // 2
    core, far = (e, h + 1 - 2 * c), (e, lax.rem(h + 2, 4))
    pair = (e + 1 - 2 * x, h)
    up = [None] + [(2 * lax.rem(z + s, 4) + x, h) for s in range(1, 4)]

    def over_core(n):
        return mesh_copy(sendb.at[n], recvb.at[n], k_s, k_r, n, core)

    def over_x(n):
        return mesh_copy(away_ref.at[n], xgot.at[n], x_s, x_r, n, pair)

    def home(n):
        return mesh_copy(zsend.at[n - 1], zgot.at[n - 1], z_s, z_r, n - 1, up[4 - n])

    hidden = piece_ref.shape[1] // 3
    pieces = []
    for n in range(6):
        place = (n // 3, pl.ds(n % 3 * hidden, hidden))
        pieces.append(mesh_copy(piece_ref.at[place], piece_far.at[place], p_s, p_r, n, far))
    at, peers = (c, y, x, z), (core, far, pair, up)
    sums = [
        SharedSum(at, peers, sg_ref, sg_c, sg_y, sg_yr, sg_fin, s_s, s_r),
        SharedSum(at, peers, sd_ref, sd_c, sd_y, sd_yr, sd_fin, d_s, d_r),
    ]

    def send_home(n):
        over_x(n).wait_recv()
        zsend[n - 1] = (near_ref[n].astype(F32) + xgot[n].astype(F32)).astype(BF)
        home(n).start()

    @pl.when(i == 0)
    def _():
        greet([core, far, pair] + up[1:])
        for n in (1, 2, 3, 0):
            over_x(n).start()
        for flow in sums:
            flow.core.start()
        pieces[0].start()
        kvacc[...] = jnp.zeros_like(kvacc)
        qacc[...] = jnp.zeros_like(qacc)

    @pl.when(i < heads)
    def _():
        q, d = q_ref[...], d_ref[...]
        cosine, sine = cos_ref[...], -sin_ref[...]
        s = jnp.concatenate([dot(q, ka_ref[...], (1, 1)), dot(q, kb_ref[...], (1, 1))], axis=1)
        s = jnp.where(score_mask(h, rows, 2 * half), s * HD ** (-0.5), -1e30)
        p = jnp.exp(s - lse_ref[:, 0:1])
        back = [dot(d, va_ref[...], (1, 1)), dot(d, vb_ref[...], (1, 1))]
        back = jnp.concatenate(back, axis=1)
        inner = jnp.sum(p * back, axis=1, keepdims=True)
        sb = (p * (back - inner) * HD ** (-0.5)).astype(BF)
        p = p.astype(BF)
        dq = dot(sb[:, :half], ka_ref[...]) + dot(sb[:, half:], kb_ref[...])
        dk = turned(dot(sb, q, (0, 0)), cosine, sine)
        dv = dot(p, d, (0, 0))
        nearb[lax.rem(i, 2), 0] = dk[:half]
        nearb[lax.rem(i, 2), 1] = dv[:half]
        sendb[i, 0] = dk[half:].astype(BF)
        sendb[i, 1] = dv[half:].astype(BF)
        over_core(i).start()
        raw = turned(dq, cosine[:rows], sine[:rows]).astype(BF)
        qp_ref[...] = dot(x_ref[:rows, :], raw, (0, 0)).astype(BF)
        qacc[...] += dot(raw, wq_ref[...], (1, 1))

    @pl.when(i > 0)
    def _():
        n = i - 1
        over_core(n).wait_recv()
        kept = lax.rem(n, 2)
        key = (nearb[kept, 0] + recvb[n, 0].astype(F32)).astype(BF)
        value = (nearb[kept, 1] + recvb[n, 1].astype(F32)).astype(BF)
        kp_ref[...] = dot(x_ref[...], key, (0, 0)).astype(BF)
        vp_ref[...] = dot(x_ref[...], value, (0, 0)).astype(BF)
        kvacc[...] += dot(key, wk_ref[...], (1, 1)) + dot(value, wv_ref[...], (1, 1))

    @pl.when(i == 1)
    def _():
        for flow in sums:
            flow.over_y()
        for copy in pieces[1:]:
            copy.start()

    @pl.when(i == 4)
    def _():
        send_home(1)

    @pl.when(i == 5)
    def _():
        for flow in sums:
            flow.over_z()

    @pl.when(i == 7)
    def _():
        send_home(2)

    @pl.when(i == heads - 1)
    def _():
        for flow in sums:
            flow.over_x()

    @pl.when(i == heads)
    def _():
        first_ref[...] = qacc[...] + kvacc[:rows, :]
        share_ref[...] = kvacc[rows:, :].astype(BF)
        gain = jnp.zeros((1, kvacc.shape[1]), F32)
        for ref, upstream in ((tok_ref, first_ref[...]), (ftok_ref, kvacc[rows:, :])):
            v = ref[...].astype(F32)
            gain = gain + jnp.sum(upstream * v * rms(v), axis=0, keepdims=True)
        gain_ref[...] = gain
        send_home(3)
        over_x(0).wait_recv()
        total = mid_ref[...] + near_ref[0].astype(F32) + xgot[0].astype(F32)
        for n in (1, 2, 3):
            home(n).wait_recv()
            total = total + zgot[n - 1].astype(F32)
        layer_ref[...] = total.astype(BF)
        for flow in sums:
            flow.pair.wait_recv()
        lanes = sg_fin.shape[3] // 2
        gate = more = down = 0.0
        for k in range(8):
            block = sg_fin[k % 2, k // 2]
            gate = gate + dot(block[:, :lanes], spread_ref[k])
            more = more + dot(block[:, lanes:], spread_ref[k])
            down = down + dot(stack_ref[k], sd_fin[k % 2, k // 2])
        sgout_ref[...] = gate
        suout_ref[...] = more
        sdout_ref[...] = down
        for copy in pieces:
            copy.wait()
        for flow in sums:
            for copy in flow.all:
                copy.wait_send()
        for n in range(4):
            over_x(n).wait_send()
        for n in (1, 2, 3):
            home(n).wait_send()
        for n in range(heads):
            over_core(n).wait_send()


def attend_back_and_sums(
    q, kv_a, kv_b, d, lse, weights, tables, first_in, pairs, sgg, sdg, spread, stack, near, middle, away, piece
):
    rows, width = q.shape
    half = kv_a.shape[1]
    stages = near.shape[0]
    dma = pltpu.SemaphoreType.DMA
    once = pl.Buffered(1)
    anywhere = pl.BlockSpec(memory_space=pl.ANY)

    def fixed(v):
        return pl.BlockSpec(v.shape, lambda i: (0,) * v.ndim, pipeline_mode=once)

    def now(i):
        return i - i // H

    def before(i):
        return i - 1 + (H - i) // H

    def head(rows_of, at=now):
        return pl.BlockSpec((rows_of, HD), lambda i: (0, at(i)))

    def kv(which):
        return pl.BlockSpec((None, half, HD), lambda i: (which, 0, now(i)))

    def shape(dims, dtype):
        return jax.ShapeDtypeStruct(dims, dtype)

    def buffers(dims):
        return [
            pltpu.VMEM((2,) + dims, BF),
            pltpu.VMEM(dims, BF),
            pltpu.VMEM(dims, BF),
            pltpu.VMEM((2, 4) + dims, BF),
        ]

    kept = [*tables, first_in, *pairs, sgg, sdg, spread, stack, near, middle]
    ends = [
        shape((rows, width), F32),
        shape((rows, width), BF),
        shape((1, width), F32),
        shape((width // 4, spread.shape[2]), F32),
        shape((width // 4, spread.shape[2]), F32),
        shape((stack.shape[1], width), F32),
        shape((rows, width), BF),
    ]
    return pl.pallas_call(
        back_kernel,
        grid=(H + 1,),
        in_specs=[head(rows), kv(0), kv(0), kv(1), kv(1), head(rows), head(rows)]
        + [head(width), head(width, before), head(width, before)]
        + [fixed(v) for v in kept]
        + [anywhere] * 2,
        out_specs=[head(width), head(width, before), head(width, before)]
        + [fixed(v) for v in ends]
        + [anywhere],
        out_shape=[shape((width, width), BF)] * 3 + ends + [shape(piece.shape, BF)],
        scratch_shapes=[
            pltpu.VMEM((H, 2, half, HD), BF),
            pltpu.VMEM((H, 2, half, HD), BF),
            pltpu.VMEM((2, 2, half, HD), F32),
            pltpu.VMEM((half, width), F32),
            pltpu.VMEM((rows, width), F32),
        ]
        + buffers(sgg.shape[2:])
        + buffers(sdg.shape[2:])
        + [
            pltpu.VMEM((stages, rows, width), BF),
            pltpu.VMEM((stages - 1, rows, width), BF),
            pltpu.VMEM((stages - 1, rows, width), BF),
        ]
        + [dma((H,))] * 2
        + [dma((6,))] * 4
        + [dma((stages,))] * 4
        + [dma((6,))] * 2,
        compiler_params=pltpu.CompilerParams(
            vmem_limit_bytes=60 * MIB, collective_id=3, has_side_effects=True
        ),
        cost_estimate=pl.CostEstimate(
            flops=22 * rows * width * width,
            bytes_accessed=60 * MIB,
            transcendentals=rows * 2 * half * H,
        ),
    )(q, kv_a, kv_b, kv_a, kv_b, d, lse, *weights, *kept, away, piece)


def tail_kernel(
    m0,
    m1,
    m2,
    m3,
    sm_ref,
    fb_ref,
    tok_ref,
    gain_ref,
    first_ref,
    mid_ref,
    out_ref,
    smout_ref,
    tokout_ref,
    crecv,
    ysend,
    yrecv,
    acc,
    xrecv,
    zrecv,
    fin,
    g_acc,
    g_recv,
    f_recv,
    c_s,
    c_r,
    y_s,
    y_r,
    x_s,
    x_r,
    z_s,
    z_r,
    za_s,
    za_r,
    xa_s,
    xa_r,
    g_s,
    g_r,
    f_s,
    f_r,
):
    mats = (m0, m1, m2, m3)
    chunks, part = acc.shape[0], acc.shape[3]
    half = m0.shape[3]
    e, h = lax.axis_index("ep"), lax.axis_index("hp")
    x, z = lax.rem(e, 2), e // 2
    c, y = lax.rem(h, 2), h // 2
    core, far = (e, h + 1 - 2 * c), (e, lax.rem(h + 2, 4))
    pair = (e + 1 - 2 * x, h)
    up = [None] + [(2 * lax.rem(z + s, 4) + x, h) for s in range(1, 4)]
    next_z = (2 * (z + 1 - 2 * lax.rem(z, 2)) + x, h)
    greet([core, far, pair] + up[1:])

    def rows(j):
        return pl.ds(j * part, part)

    def over_core(j, m):
        return mesh_copy(
            mats[m].at[:, 1 - c, :, rows(j), :],
            crecv.at[m, :, :, rows(j), :],
            c_s,
            c_r,
            4 * j + m,
            core,
        )

    def over_y(j):
        return mesh_copy(ysend.at[j], yrecv.at[j], y_s, y_r, j, far)

    def over_x(j):
        return mesh_copy(acc.at[j, :, 1 - x], xrecv.at[j], x_s, x_r, j, pair)

    def over_z(j, s):
        return mesh_copy(
            acc.at[j, lax.rem(z + s, 4), x], zrecv.at[j, s - 1], z_s, z_r, 3 * j + s - 1, up[s]
        )

    def back_z(j, s):
        return mesh_copy(fin.at[j, z, x], fin.at[j, z, x], za_s, za_r, 3 * j + s - 1, up[s])

    def back_x(j):
        return mesh_copy(fin.at[j, :, x], fin.at[j, :, x], xa_s, xa_r, j, pair)

    def add_core(j):
        for m in range(4):
            over_core(j, m).wait_recv()
            for at, to in ((y, acc), (1 - y, ysend)):
                total = mats[m][at, c, :, rows(j), :].astype(F32)
                to[j, m] = (total + crecv[m, at, :, rows(j), :].astype(F32)).astype(BF)
        over_y(j).start()

    def add_y(j):
        over_y(j).wait_recv()
        acc[j] = (acc[j].astype(F32) + yrecv[j].astype(F32)).astype(BF)
        over_x(j).start()

    def add_x(j):
        over_x(j).wait_recv()
        acc[j, :, x] = (acc[j, :, x].astype(F32) + xrecv[j].astype(F32)).astype(BF)
        for s in range(1, 4):
            over_z(j, s).start()

    def add_z(j):
        total = acc[j, z, x].astype(F32)
        for s in range(1, 4):
            over_z(j, s).wait_recv()
            total = total + zrecv[j, s - 1].astype(F32)
        fin[j, z, x] = total.astype(BF)
        for s in range(1, 4):
            back_z(j, s).start()

    def end_z(j):
        for s in range(1, 4):
            back_z(j, s).wait_recv()
        back_x(j).start()

    def end_x(j):
        back_x(j).wait_recv()
        for m in range(4):
            for i in range(2):
                out_ref[m, i * half + j * part : i * half + (j + 1) * part, :] = fin[j, m, i]

    route = (core, far, pair, next_z, up[2])
    small = [
        mesh_copy(g_acc.at[i], g_recv.at[i], g_s, g_r, i, route[i]) for i in range(len(route))
    ]

    back = mesh_copy(fb_ref, f_recv, f_s, f_r, 0, far)

    def side(t):
        if t == chunks - lead:
            back.start()
        if t % 2 == 1 and t // 2 < len(small):
            i = t // 2
            small[i].wait_recv()
            g_acc[i + 1] = g_acc[i] + g_recv[i]
            if i + 1 < len(small):
                small[i + 1].start()
        if t == chunks + 3:
            back.wait()
            first_back = first_ref[...] + f_recv[...].astype(F32)
            values = tok_ref[...].astype(F32)
            to_tokens = norm_back(values, rms(values), gain_ref[...], first_back)
            tokout_ref[...] = mid_ref[...] + to_tokens

    lead = 3
    g_acc[0] = sm_ref[...]
    for m in range(4):
        over_core(0, m).start()
    small[0].start()
    for j in range(1, chunks):
        for m in range(4):
            over_core(j, m).start()
    for j in range(lead):
        add_core(j)
    steps = (add_y, add_x, add_z, end_z, end_x)
    for t in range(chunks + len(steps) - 1):
        if t + lead < chunks:
            add_core(t + lead)
        for p in reversed(range(len(steps))):
            if 0 <= t - p < chunks:
                steps[p](t - p)
        side(t)
    smout_ref[...] = g_acc[len(small)]
    for copy in small:
        copy.wait_send()
    for j in range(chunks):
        for m in range(4):
            over_core(j, m).wait_send()
        for copy in (over_y(j), over_x(j), back_x(j)):
            copy.wait_send()
        for s in range(1, 4):
            over_z(j, s).wait_send()
            back_z(j, s).wait_send()


def tail(mats, small, share, tokens, gain, first_back, middle_back):
    width = mats[0].shape[1]
    half = width // 8
    part = 16
    chunks = half // part
    dma = pltpu.SemaphoreType.DMA
    vmem = pl.BlockSpec(memory_space=pltpu.VMEM)
    return pl.pallas_call(
        tail_kernel,
        in_specs=[vmem] * 10,
        out_specs=[vmem] * 3,
        out_shape=[
            jax.ShapeDtypeStruct((4, 2 * half, width), BF),
            jax.ShapeDtypeStruct(small.shape, F32),
            jax.ShapeDtypeStruct(tokens.shape, F32),
        ],
        scratch_shapes=[
            pltpu.VMEM((4, 2, 2, half, width), BF),
            pltpu.VMEM((chunks, 4, 2, part, width), BF),
            pltpu.VMEM((chunks, 4, 2, part, width), BF),
            pltpu.VMEM((chunks, 4, 2, part, width), BF),
            pltpu.VMEM((chunks, 4, part, width), BF),
            pltpu.VMEM((chunks, 3, part, width), BF),
            pltpu.VMEM((chunks, 4, 2, part, width), BF),
            pltpu.VMEM((6,) + small.shape, F32),
            pltpu.VMEM((5,) + small.shape, F32),
            pltpu.VMEM(share.shape, BF),
        ]
        + [dma((4 * chunks,))] * 2
        + [dma((chunks,))] * 4
        + [dma((3 * chunks,))] * 4
        + [dma((chunks,))] * 2
        + [dma((5,))] * 2
        + [dma((1,))] * 2,
        compiler_params=pltpu.CompilerParams(
            vmem_limit_bytes=60 * MIB, collective_id=2, has_side_effects=True
        ),
        cost_estimate=pl.CostEstimate(flops=0, bytes_accessed=300 * MIB, transcendentals=0),
    )(
        *[m.reshape(2, 2, 2, half, width) for m in mats],
        small,
        share,
        tokens,
        gain,
        first_back,
        middle_back,
    )


def rms(values):
    return lax.rsqrt(jnp.mean(values * values, axis=-1, keepdims=True) + epsilon)


def norm_back(values, inv, gain, upstream):
    weighted = upstream * gain
    inner = jnp.mean(weighted * values, axis=-1, keepdims=True)
    return weighted * inv - values * (inv * inv * inv * inner)


def rotary_tables(positions):
    exponent = jnp.arange(HD // 2, dtype=F32) * (2.0 / HD)
    theta = positions.astype(F32)[:, None] * jnp.power(10000.0, -exponent)[None, :]
    cosine, sine = jnp.cos(theta), jnp.sin(theta)
    return jnp.concatenate([cosine, cosine], axis=1), jnp.concatenate([-sine, sine], axis=1)


def per_device(
    tokens,
    attn_gain,
    query_weight,
    key_weight,
    value_weight,
    out_weight,
    ffn_gain,
    router_weight,
    shared_gate,
    shared_up,
    shared_down,
    expert_gate,
    expert_up,
    expert_down,
    routes,
    keep_mask,
    cotangent,
):
    e, h = lax.axis_index("ep"), lax.axis_index("hp")
    ep = lax.axis_size("ep")
    stages = ep // 2
    rows, width = tokens.shape
    top = routes.shape[1]
    total = router_weight.shape[1]
    capacity = -(-(5 * rows * top // (4 * total)) // 16) * 16
    e_arr, h_arr = jnp.full((1,), e, jnp.int32), jnp.full((1,), h, jnp.int32)

    units = shared_down.shape[0] // ep
    pad = -(-units // 16) * 16
    tiny = [attn_gain[:, None], ffn_gain[:, None], router_weight]
    small = jnp.concatenate(tiny + [jnp.zeros((width // 4, LANES - 2 - total), BF)], axis=1)

    unit = jnp.arange(LANES)
    to = (unit // pad) * (ep * units) + unit % pad
    to = jnp.where((unit < 4 * pad) & (unit % pad < units), to, -ep * units)
    column = jnp.arange(4 * ep * units)
    mine = (column[:, None] == (to + e * units)[None, :]).astype(BF)
    small = [small, dot(shared_gate, mine).astype(BF), dot(shared_up, mine).astype(BF)]
    small = jnp.concatenate(small, axis=1)
    sd = lax.dynamic_slice_in_dim(shared_down, e * units, units, axis=0)
    sd = jnp.pad(sd, ((0, pad - units), (0, 0)))
    blocks = [key_weight, value_weight, query_weight, out_weight, small, sd]
    experts = jnp.concatenate(
        [jnp.swapaxes(expert_gate, 1, 2), jnp.swapaxes(expert_up, 1, 2), expert_down], axis=1
    )
    fused = stages == 4
    if fused:
        far_tokens, experts_core, g_near, *blocks = front(
            stages, tokens, experts, cotangent, blocks, 4
        )
        own = experts[:, : 2 * expert_down.shape[1]]
        experts_far = swap_y(after(own, blocks[0]))
        g_far = swap_pair(g_near[: stages - 1])
    else:
        far_tokens = swap_y(tokens)
        blocks = [absolute(jnp.stack(gather_hp(v)), h, 0) for v in blocks]
        g_blocks = gather_ep(cotangent)
        experts = gather_hp(experts)
    k_w, v_w, q_w, o_w, small = (v.reshape(width, v.shape[2]) for v in blocks[:5])
    gain_one = small[:, 0].astype(F32)[None, :]
    gain_two = small[:, 1].astype(F32)[None, :]
    router = small[:, 2 : 2 + total]
    sg, su = small[:, LANES : 2 * LANES], small[:, 2 * LANES :]
    sd = blocks[5].reshape(4 * pad, width)
    if 4 * pad < LANES:
        sd = jnp.pad(sd, ((0, LANES - 4 * pad), (0, 0)))

    pos = jnp.arange(rows, dtype=jnp.int32)
    pos = jnp.concatenate([(h ^ i) * rows + pos for i in (0, 2, 1, 3)])
    cosine, sine = rotary_tables(pos)
    residual = tokens.astype(F32)
    table = cosine[: 2 * rows], sine[: 2 * rows]
    first_in, kv_a, query = project(tokens, far_tokens, gain_one, k_w, v_w, q_w, *table)
    kv_b = swap_core(kv_a)
    mixed, lse = attend(h_arr, query, kv_a, kv_b)
    routes, keep_mask, late = after((routes, keep_mask, jnp.arange(ep)), query)
    if fused:
        mixed = after(mixed, g_far)
    middle = residual + dot(mixed, o_w)
    inv_two = rms(middle)
    second_in = (middle * inv_two * gain_two).astype(BF)

    expert = jnp.arange(total, dtype=jnp.int32)
    hit_each = routes[:, :, None] == expert[None, None, :]
    hit = jnp.any(hit_each, axis=1)
    kept = jnp.sum(jnp.where(hit_each, keep_mask[:, :, None], 0), axis=1)
    below = (jnp.arange(rows)[:, None] > jnp.arange(rows)[None, :]).astype(BF)
    place = jnp.where(hit, dot(below, hit.astype(BF)), -1.0)
    kept = kept.astype(F32)

    logits = jnp.where(hit, dot(second_in, router), -1e30)
    gates_of = jnp.where(hit, jnp.exp(logits - jnp.max(logits, axis=1, keepdims=True)), 0.0)
    gates_of = gates_of / jnp.sum(gates_of, axis=1, keepdims=True)
    pair_weight = gates_of * kept
    flat = (2, ep * capacity)

    hidden = expert_down.shape[1]

    def expert_grad(left, right):
        return jnp.einsum("xna,xnb->xab", left, right, preferred_element_type=F32)

    if fused:
        meta = jnp.concatenate([pair_weight.T, place.T], axis=0)
        experts = [experts, experts_far, experts_core]
        dx_sum, weight_back, near, far, sgg, sdg, xr, gr, gu, wa = dispatch(
            capacity, total, second_in, meta, g_near, g_far, experts, sg, su, sd
        )
        weight_back = weight_back.T
        xr, gr, gu, wa = (v.reshape(flat + (v.shape[-1],)) for v in (xr, gr, gu, wa))
        piece_near, piece_sum = expert_grads(xr, gr, gu, wa, hidden)
    else:
        x_ext = jnp.concatenate(
            [
                second_in,
                pair_weight.astype(BF),
                place.astype(BF),
                jnp.zeros((rows, LANES - 2 * total), BF),
            ],
            axis=1,
        )
        x_blocks = gather_ep(after(x_ext, g_blocks))
        carry = (jnp.zeros((width, 2 * LANES), F32), jnp.zeros((LANES, width), F32))
        bufs, dx_parts = None, []
        gates, ups = (
            [jnp.swapaxes(v[:, i * hidden : (i + 1) * hidden], 1, 2) for v in experts]
            for i in (0, 1)
        )
        downs = [v[:, 2 * hidden :] for v in experts]
        for k in range(stages):
            dx, carry, bufs = expert_stage(
                k,
                stages,
                capacity,
                total,
                e_arr,
                x_blocks[k],
                g_blocks[k],
                gates,
                ups,
                downs,
                sg,
                su,
                sd,
                carry,
                bufs,
            )
            dx_parts.append(dx)
        dx_sum = scatter_ep(dx_parts)
        weight_back = (
            dx_sum[:, width : width + total] + dx_sum[:, width + total : width + 2 * total]
        )
        dx_sum = dx_sum[:, :width]
        sgg, sdg = carry
        sa, xr, gr, gi, ui, wa = bufs
        out_parts = [
            expert_out(k, capacity, total, e_arr, x_blocks[k], wa, sa, downs, sd)
            for k in range(stages)
        ]
        xr, gr = xr.reshape(flat + (width,)), gr.reshape(flat + (width,))
        gi, ui, wa = (v.reshape((4,) + flat + (v.shape[-1],)) for v in (gi, ui, wa))
        routed = scatter_ep(after(out_parts, dx_sum))
        expert_sum = scatter_hp(
            [
                jnp.concatenate(
                    [
                        expert_grad(gi[r], xr),
                        expert_grad(ui[r], xr),
                        expert_grad(wa[r], gr),
                    ],
                    axis=1,
                )
                for r in range(4)
            ]
        )

    grad_out = cotangent.astype(F32)
    gate_back = weight_back * kept
    chosen_back = gates_of * (gate_back - jnp.sum(gates_of * gate_back, axis=1, keepdims=True))
    logits_back = chosen_back.astype(BF)
    router_part = dot(logits_back, second_in, (0, 0))
    second_back = dx_sum + dot(logits_back, router, (1, 1))
    gain_two_part = jnp.sum(second_back * middle * inv_two, axis=0)
    middle_back = grad_out + norm_back(middle, inv_two, gain_two, second_back)
    attn_back = middle_back.astype(BF)
    counts_part = jnp.pad(jnp.sum(kept, axis=0), (0, width - total))

    mixed_back = dot(attn_back, o_w, (1, 1)).astype(BF)
    out_part = dot(mixed, attn_back, (0, 0))
    sgg = sgg.reshape(4, width // 4, 2 * LANES)
    sdg = sdg[: 4 * pad].reshape(4, pad, width)
    block = late[:, None, None] * units
    spread = (to[None, :, None] + block == column[None, None, :]).astype(BF)

    def small_sums(gain_one_part):
        lines = [router_part, gain_two_part[None, :], counts_part[None, :], gain_one_part]
        return jnp.concatenate(lines + [jnp.zeros((-(total + 3) % 8, width), F32)], axis=0)

    if fused:
        sdg = sdg.astype(BF)
        at = jnp.where(jnp.arange(pad) < units, jnp.arange(pad), -ep * units)[None, None, :]
        stack = (at + block == jnp.arange(ep * units)[None, :, None]).astype(BF)
        (
            q_part,
            k_part,
            v_part,
            first_back,
            share,
            gain_one_part,
            sgate_grad,
            sup_grad,
            sdown_grad,
            layer,
            piece_far,
        ) = attend_back_and_sums(
            query,
            kv_a,
            kv_b,
            mixed_back,
            lse,
            (q_w, k_w, v_w),
            (cosine, sine),
            first_in,
            (tokens, far_tokens),
            sgg.astype(BF).reshape(2, 2, width // 4, 2 * LANES),
            sdg.reshape(2, 2, pad, width),
            spread,
            stack,
            near,
            middle,
            far,
            piece_sum,
        )
        out, sums, tokens_grad = tail(
            [q_part, k_part, v_part, out_part.astype(BF)],
            small_sums(gain_one_part),
            share,
            tokens,
            gain_one,
            first_back,
            middle_back,
        )
        grads = [out[i].astype(F32) for i in range(4)]
        spans = [slice(i * hidden, (i + 1) * hidden) for i in range(3)]
        gate_grad, up_grad, down_grad = (
            piece_near[:, a].astype(F32) + piece_far[:, a].astype(F32) for a in spans
        )
    else:
        query_raw, near_back, far_back = attend_back(
            h_arr, query, kv_a, kv_b, mixed_back, lse, cosine, sine
        )
        kv_raw = (near_back + swap_core(far_back).astype(F32)).astype(BF)
        key_raw, value_raw = kv_raw[0], kv_raw[1]
        kv_back = dot(key_raw, k_w, (1, 1)) + dot(value_raw, v_w, (1, 1))
        q_part = dot(first_in[:rows], query_raw, (0, 0))
        k_part = dot(first_in, key_raw, (0, 0))
        v_part = dot(first_in, value_raw, (0, 0))
        first_back = kv_back[:rows] + dot(query_raw, q_w, (1, 1))
        gain_one_part = jnp.zeros((1, width), F32)
        for values, upstream in ((tokens, first_back), (far_tokens, kv_back[rows:])):
            values = values.astype(F32)
            gain_one_part += jnp.sum(upstream * values * rms(values), axis=0, keepdims=True)

        def over_hp(v):
            return scatter_hp(jnp.split(relative(v, h, 0), 4, axis=0))

        grads = [sum_ep(over_hp(v), e) for v in (q_part, k_part, v_part, out_part)]
        sums = sum_all_small(small_sums(gain_one_part))
        first_back = first_back + swap_y(kv_back[rows:].astype(BF)).astype(F32)
        tokens_grad = middle_back + norm_back(residual, rms(residual), gain_one, first_back)
        sgg, sdg = (spread_ep(over_hp(v)[0].astype(BF), e) for v in (sgg, sdg))
        sgate_grad, sup_grad = (
            jnp.einsum("kra,kan->rn", v, spread, preferred_element_type=F32)
            for v in (sgg[:, :, :LANES], sgg[:, :, LANES:])
        )
        sdown_grad = sdg[:, :units].reshape(ep * units, width).astype(F32)
        layer = (middle + routed).astype(BF)
        gate_grad, up_grad, down_grad = jnp.split(expert_sum, 3, axis=1)
    gate_grad, up_grad = jnp.swapaxes(gate_grad, 1, 2), jnp.swapaxes(up_grad, 1, 2)

    def own(v, n):
        return lax.dynamic_slice_in_dim(v, h * n, n, axis=0)

    return (
        layer,
        tokens_grad,
        own(sums[total + 2], width // 4),
        *grads,
        own(sums[total], width // 4),
        own(sums[:total].T, width // 4),
        sgate_grad,
        sup_grad,
        sdown_grad,
        gate_grad,
        up_grad,
        down_grad,
        own(sums[total + 1], total // 4).astype(jnp.int32),
    )


def solution(mesh):
    row, ep_hp = P("hp", None), P(("ep", "hp"), None)
    return jax.shard_map(
        per_device,
        mesh=mesh,
        in_specs=(
            ep_hp,
            P("hp"),
            row,
            row,
            row,
            row,
            P("hp"),
            row,
            row,
            row,
            row,
            P("ep", None, "hp"),
            P("ep", None, "hp"),
            P("ep", "hp", None),
            ep_hp,
            ep_hp,
            ep_hp,
        ),
        out_specs=(
            ep_hp,
            ep_hp,
            P("hp"),
            row,
            row,
            row,
            row,
            P("hp"),
            row,
            row,
            row,
            row,
            P("ep", None, "hp"),
            P("ep", None, "hp"),
            P("ep", "hp", None),
            P("hp"),
        ),
        check_vma=False,
    )
```

```python
import functools

import jax
import jax.numpy as jnp
from jax import lax
from jax.experimental import pallas as pl
from jax.experimental.pallas import tpu as pltpu
from jax.sharding import PartitionSpec as P

H = 10
HD = 128
LANES = 128
BF = jnp.bfloat16
F32 = jnp.float32
epsilon = 1e-06
MIB = 1 << 20


def dot(left, right, over=(1, 0)):
    return lax.dot_general(
        left, right, (((over[0],), (over[1],)), ((), ())), preferred_element_type=F32
    )


def swap_core(v):
    return lax.ppermute(v, "hp", [(i, i ^ 1) for i in range(4)])


def swap_y(v):
    return lax.ppermute(v, "hp", [(i, i ^ 2) for i in range(4)])


def swap_pair(v):
    n = lax.axis_size("ep")
    return lax.ppermute(v, "ep", [(i, i ^ 1) for i in range(n)])


def ring(v):
    n = lax.axis_size("ep")
    return lax.ppermute(v, "ep", [(i, (i + 2) % n) for i in range(n)])


def shift(v, steps):
    n = lax.axis_size("ep")
    return lax.ppermute(v, "ep", [(i, (i + 2 * steps) % n) for i in range(n)])


def after(v, *others):
    return lax.optimization_barrier((v, others))[0]


def gather_hp(v):
    far = swap_y(v)
    return [v, far, swap_core(v), swap_core(far)]


def scatter_hp(parts):
    near = swap_core(parts[2].astype(BF)).astype(F32) + parts[0].astype(F32)
    over = swap_core(parts[3].astype(BF)).astype(F32) + parts[1].astype(F32)
    return near + swap_y(over.astype(BF)).astype(F32)


def crossed(b, h):
    odd, high = (h & 1) == 1, (h & 2) == 2
    c = [jnp.where(odd, b[i ^ 1], b[i]) for i in range(4)]
    return [jnp.where(high, c[i ^ 2], c[i]) for i in range(4)]


def relative(v, h, axis):
    c = crossed(jnp.split(v, 4, axis=axis), h)
    return jnp.concatenate([c[0], c[2], c[1], c[3]], axis=axis)


def absolute(v, h, axis):
    b = jnp.split(v, 4, axis=axis)
    return jnp.concatenate(crossed([b[0], b[2], b[1], b[3]], h), axis=axis)


def gather_ep(v):
    stages = lax.axis_size("ep") // 2
    own, out = v, []
    for k in range(stages):
        out.append((own, swap_pair(own)))
        if k < stages - 1:
            own = ring(own)
    return out


def scatter_ep(parts):
    stages = len(parts)
    total = None
    for k in list(range(1, stages)) + [0]:
        here = parts[k][0].astype(F32) + swap_pair(parts[k][1]).astype(F32)
        if total is not None:
            here = here + total.astype(F32)
        total = here if k == 0 else ring(here.astype(BF))
    return total


def spread_ep(v, e):
    n = lax.axis_size("ep")
    stages = n // 2
    x, z = e & 1, e >> 1
    column = lax.dynamic_update_index_in_dim(jnp.zeros((stages,) + v.shape, v.dtype), v, z, 0)
    for step in range(1, stages):
        column = lax.dynamic_update_index_in_dim(
            column, shift(v, step), (z + stages - step) % stages, 0
        )
    far = swap_pair(column)
    both = [jnp.where(x == 0, column, far), jnp.where(x == 0, far, column)]
    return jnp.stack(both, axis=1).reshape((n,) + v.shape)


def sum_ep(v, e):
    n = lax.axis_size("ep")
    stages = n // 2
    x, z = e & 1, e >> 1
    halves = v.reshape(2, v.shape[0] // 2, v.shape[1])
    mine = lax.dynamic_index_in_dim(halves, x, 0, False)
    other = lax.dynamic_index_in_dim(halves, 1 - x, 0, False)
    mine = mine + swap_pair(other.astype(BF)).astype(F32)
    chunks = mine.reshape(stages, mine.shape[0] // stages, mine.shape[1])
    low = chunks.astype(BF)
    total = lax.dynamic_index_in_dim(chunks, z, 0, False)
    for step in range(1, stages):
        part = lax.dynamic_index_in_dim(low, (z + step) % stages, 0, False)
        total = total + shift(part, step).astype(F32)
    total = total.astype(BF)
    half = lax.dynamic_update_index_in_dim(jnp.zeros(chunks.shape, BF), total, z, 0)
    for step in range(1, stages):
        half = lax.dynamic_update_index_in_dim(
            half, shift(total, step), (z + stages - step) % stages, 0
        )
    half = half.reshape(mine.shape)
    far = swap_pair(half)
    low = jnp.where(x == 0, half, far)
    high = jnp.where(x == 0, far, half)
    return jnp.concatenate([low, high], axis=0).astype(F32)


def sum_all_small(v):
    v = v + swap_core(v)
    v = v + swap_y(v)
    n = lax.axis_size("ep")
    bit = 1
    while bit < n:
        v = v + lax.ppermute(v, "ep", [(i, i ^ bit) for i in range(n)])
        bit *= 2
    return v


def score_mask(h, rows, cols):
    at = lax.broadcasted_iota(jnp.int32, (rows, cols), 0) + h * rows
    key = lax.broadcasted_iota(jnp.int32, (rows, cols), 1)
    block = key // rows
    other = jnp.where(
        block == 0, h, jnp.where(block == 1, h ^ 2, jnp.where(block == 2, h ^ 1, h ^ 3))
    )
    return other * rows + key % rows <= at


def turned(v, cosine, sine):
    return v * cosine + pltpu.roll(v, HD // 2, 1) * sine


def project_kernel(
    t_ref, f_ref, gain_ref, k_ref, v_ref, q_ref, cos_ref, sin_ref, x_ref, kv_ref, query_ref
):
    rows = query_ref.shape[0]

    @pl.when(pl.program_id(0) == 0)
    def _():
        for i, ref in enumerate((t_ref, f_ref)):
            v = ref[...].astype(F32)
            x_ref[i * rows : (i + 1) * rows, :] = (v * rms(v) * gain_ref[...]).astype(BF)

    x = x_ref[...]
    cosine, sine = cos_ref[...], sin_ref[...]
    keys, query = dot(x, k_ref[...]), dot(x[:rows], q_ref[...])
    kv_ref[1] = dot(x, v_ref[...]).astype(BF)
    for i in range(k_ref.shape[1] // HD):
        span = slice(i * HD, (i + 1) * HD)
        kv_ref[0, :, span] = turned(keys[:, span], cosine, sine).astype(BF)
        query_ref[:, span] = turned(query[:, span], cosine[:rows], sine[:rows]).astype(BF)


def project(tokens, far, gain, k_w, v_w, q_w, cosine, sine):
    rows, width = tokens.shape
    two, block = 2 * rows, 2 * HD
    cols = pl.BlockSpec((width, block), lambda i: (0, i))

    def fixed(v):
        return pl.BlockSpec(v.shape, lambda i: (0, 0))

    return pl.pallas_call(
        project_kernel,
        grid=(width // block,),
        in_specs=[fixed(tokens), fixed(far), fixed(gain), cols, cols, cols]
        + [pl.BlockSpec((two, HD), lambda i: (0, 0))] * 2,
        out_specs=[
            pl.BlockSpec((two, width), lambda i: (0, 0)),
            pl.BlockSpec((2, two, block), lambda i: (0, 0, i)),
            pl.BlockSpec((rows, block), lambda i: (0, i)),
        ],
        out_shape=[
            jax.ShapeDtypeStruct((two, width), BF),
            jax.ShapeDtypeStruct((2, two, width), BF),
            jax.ShapeDtypeStruct((rows, width), BF),
        ],
        compiler_params=pltpu.CompilerParams(vmem_limit_bytes=40 * MIB),
        cost_estimate=pl.CostEstimate(flops=0, bytes_accessed=0, transcendentals=0),
    )(tokens, far, gain, k_w, v_w, q_w, cosine, sine)


def attend_kernel(h_ref, q_ref, ka_ref, kb_ref, va_ref, vb_ref, o_ref, lse_ref):
    rows = q_ref.shape[0]
    half = ka_ref.shape[0]
    q = q_ref[...]
    s = jnp.concatenate([dot(q, ka_ref[...], (1, 1)), dot(q, kb_ref[...], (1, 1))], axis=1)
    s = jnp.where(score_mask(h_ref[0], rows, 2 * half), s * HD ** (-0.5), -1e30)
    top = jnp.max(s, axis=1, keepdims=True)
    p = jnp.exp(s - top)
    total = jnp.sum(p, axis=1, keepdims=True)
    p = (p * (1.0 / total)).astype(BF)
    o = dot(p[:, :half], va_ref[...]) + dot(p[:, half:], vb_ref[...])
    o_ref[...] = o.astype(BF)
    lse_ref[...] = jnp.broadcast_to(top + jnp.log(total), lse_ref.shape)


def attend_back_kernel(
    h_ref,
    q_ref,
    ka_ref,
    kb_ref,
    va_ref,
    vb_ref,
    d_ref,
    lse_ref,
    cos_ref,
    sin_ref,
    dq_ref,
    da_ref,
    db_ref,
):
    rows = q_ref.shape[0]
    half = ka_ref.shape[0]
    q, d = q_ref[...], d_ref[...]
    cosine, sine = cos_ref[...], -sin_ref[...]
    s = jnp.concatenate([dot(q, ka_ref[...], (1, 1)), dot(q, kb_ref[...], (1, 1))], axis=1)
    s = jnp.where(score_mask(h_ref[0], rows, 2 * half), s * HD ** (-0.5), -1e30)
    p = jnp.exp(s - lse_ref[:, 0:1])
    back = jnp.concatenate([dot(d, va_ref[...], (1, 1)), dot(d, vb_ref[...], (1, 1))], axis=1)
    inner = jnp.sum(p * back, axis=1, keepdims=True)
    sb = (p * (back - inner) * HD ** (-0.5)).astype(BF)
    p = p.astype(BF)
    dq = dot(sb[:, :half], ka_ref[...]) + dot(sb[:, half:], kb_ref[...])
    dq_ref[...] = turned(dq, cosine[:rows], sine[:rows]).astype(BF)
    dk = turned(dot(sb, q, (0, 0)), cosine, sine)
    dv = dot(p, d, (0, 0))
    da_ref[0] = dk[:half]
    da_ref[1] = dv[:half]
    db_ref[0] = dk[half:].astype(BF)
    db_ref[1] = dv[half:].astype(BF)


def head_spec(rows):
    return pl.BlockSpec((rows, HD), lambda i, h: (0, i))


def kv_spec(rows, which):
    return pl.BlockSpec((None, rows, HD), lambda i, h: (which, 0, i))


def attend(h, q, kv_a, kv_b):
    rows, width = q.shape
    half = kv_a.shape[1]
    return pl.pallas_call(
        attend_kernel,
        grid_spec=pltpu.PrefetchScalarGridSpec(
            num_scalar_prefetch=1,
            grid=(H,),
            in_specs=[
                head_spec(rows),
                kv_spec(half, 0),
                kv_spec(half, 0),
                kv_spec(half, 1),
                kv_spec(half, 1),
            ],
            out_specs=[head_spec(rows), head_spec(rows)],
        ),
        out_shape=[
            jax.ShapeDtypeStruct((rows, width), BF),
            jax.ShapeDtypeStruct((rows, width), F32),
        ],
        compiler_params=pltpu.CompilerParams(vmem_limit_bytes=40 * MIB),
        cost_estimate=pl.CostEstimate(flops=0, bytes_accessed=0, transcendentals=0),
    )(h, q, kv_a, kv_b, kv_a, kv_b)


def attend_back(h, q, kv_a, kv_b, d, lse, cosine, sine):
    rows, width = q.shape
    half = kv_a.shape[1]
    flops = 10 * rows * 2 * half * width
    table = pl.BlockSpec((2 * half, HD), lambda i, h: (0, 0))
    both = pl.BlockSpec((2, half, HD), lambda i, h: (0, 0, i))
    return pl.pallas_call(
        attend_back_kernel,
        grid_spec=pltpu.PrefetchScalarGridSpec(
            num_scalar_prefetch=1,
            grid=(H,),
            in_specs=[
                head_spec(rows),
                kv_spec(half, 0),
                kv_spec(half, 0),
                kv_spec(half, 1),
                kv_spec(half, 1),
                head_spec(rows),
                head_spec(rows),
                table,
                table,
            ],
            out_specs=[head_spec(rows), both, both],
        ),
        out_shape=[
            jax.ShapeDtypeStruct((rows, width), BF),
            jax.ShapeDtypeStruct((2, half, width), F32),
            jax.ShapeDtypeStruct((2, half, width), BF),
        ],
        compiler_params=pltpu.CompilerParams(vmem_limit_bytes=40 * MIB),
        cost_estimate=pl.CostEstimate(
            flops=flops, bytes_accessed=16 * MIB, transcendentals=rows * 2 * half * H
        ),
    )(h, q, kv_a, kv_b, kv_a, kv_b, d, lse, cosine, sine)


def pick_matrix(meta, col, capacity):
    lane = lax.broadcasted_iota(jnp.int32, meta.shape, 1)
    code = jnp.sum(jnp.where(lane == col, meta.astype(F32), 0.0), axis=1, keepdims=True)
    place = lax.broadcasted_iota(jnp.int32, (meta.shape[0], capacity), 1).astype(F32)
    return jnp.where(code == place, 1.0, 0.0).astype(BF)


def expert_kernel(capacity, total, olds, e_ref, x0_ref, x1_ref, g0_ref, g1_ref, *refs):
    gates, ups, downs = refs[0:4], refs[4:8], refs[8:12]
    sg_ref, su_ref, sd_ref, sgg_old, sdg_old = refs[12:17]
    (
        dx0_ref,
        dx1_ref,
        sgg_ref,
        sdg_ref,
        sa_ref,
        xr_ref,
        gr_ref,
        gi_ref,
        ui_ref,
        wa_ref,
    ) = refs[17 + olds :]
    xs, gs, dxs = (x0_ref, x1_ref), (g0_ref, g1_ref), (dx0_ref, dx1_ref)
    width = sg_ref.shape[0]
    tokens = x0_ref.shape[0]
    c = capacity
    x2 = jnp.concatenate([r[:, :width] for r in xs], axis=0)
    g2 = jnp.concatenate([r[:, :width] for r in gs], axis=0)
    hg, hu = dot(x2, sg_ref[...]), dot(x2, su_ref[...])
    ab = dot(g2, sd_ref[...], (1, 1))
    s = jax.nn.sigmoid(hg)
    silu = hg * s
    act = (silu * hu).astype(BF)
    gi = (ab * hu * (s * (1.0 + hg * (1.0 - s)))).astype(BF)
    ui = (ab * silu).astype(BF)
    sa_ref[0] = act
    gu = jnp.concatenate([gi, ui], axis=1)
    sgg_ref[...] = sgg_old[...] + dot(x2, gu, (0, 0))
    sdg_ref[...] = sdg_old[...] + dot(act, g2, (0, 0))
    dx = dot(gi, sg_ref[...], (1, 1)) + dot(ui, su_ref[...], (1, 1))
    totals = [dx[:tokens], dx[tokens:]]
    metas = [0.0, 0.0]
    lane = lax.broadcasted_iota(jnp.int32, (2 * c, LANES), 1)
    for x in range(2):
        col = 2 * e_ref[0] + x
        picks, weights = [], []
        for j in range(2):
            pick = pick_matrix(xs[j][:, width:], total + col, c)
            picks.append(pick)
            rows = dot(pick, xs[j][...], (0, 0))
            xr_ref[x, 0, j * c : (j + 1) * c, :] = rows[:, :width].astype(BF)
            weights.append(rows[:, width:])
            gr_ref[x, 0, j * c : (j + 1) * c, :] = dot(pick, gs[j][:, :width], (0, 0)).astype(BF)
        w = jnp.concatenate(weights, axis=0)
        w = jnp.sum(jnp.where(lane == col, w, 0.0), axis=1, keepdims=True)
        xr, gr = xr_ref[x, 0], gr_ref[x, 0]
        dxr = jnp.zeros((2 * c, width), F32)
        wb = jnp.zeros((2 * c, 1), F32)
        for r in range(4):
            wg, wu, wd = gates[r][x], ups[r][x], downs[r][x]
            hg, hu = dot(xr, wg), dot(xr, wu)
            ab = dot(gr, wd, (1, 1))
            s = jax.nn.sigmoid(hg)
            silu = hg * s
            act = silu * hu
            wb = wb + jnp.sum(act * ab, axis=1, keepdims=True)
            ab = ab * w
            gi = (ab * hu * (s * (1.0 + hg * (1.0 - s)))).astype(BF)
            ui = (ab * silu).astype(BF)
            gi_ref[r, x, 0] = gi
            ui_ref[r, x, 0] = ui
            wa_ref[r, x, 0] = (act * w).astype(BF)
            dxr = dxr + dot(gi, wg, (1, 1)) + dot(ui, wu, (1, 1))
        dxr = dxr.astype(BF)
        high = wb.astype(BF).astype(F32)
        meta = jnp.where(lane == col, high, 0.0) + jnp.where(lane == total + col, wb - high, 0.0)
        meta = meta.astype(BF)
        for j in range(2):
            span = slice(j * c, (j + 1) * c)
            totals[j] = totals[j] + dot(picks[j], dxr[span])
            metas[j] = metas[j] + dot(picks[j], meta[span])
    for j in range(2):
        dxs[j][:, :width] = totals[j].astype(BF)
        dxs[j][:, width:] = metas[j].astype(BF)


def expert_out_kernel(capacity, total, e_ref, x0_ref, x1_ref, wa_ref, sa_ref, *refs):
    downs, sd_ref, outs = refs[0:4], refs[4], refs[5:7]
    width = sd_ref.shape[1]
    tokens = x0_ref.shape[0]
    c = capacity
    xs = (x0_ref, x1_ref)
    shared = dot(sa_ref[0], sd_ref[...])
    totals = [shared[:tokens], shared[tokens:]]
    for x in range(2):
        rows = jnp.zeros((2 * c, width), F32)
        for r in range(4):
            rows = rows + dot(wa_ref[r, x, 0], downs[r][x])
        rows = rows.astype(BF)
        for j in range(2):
            pick = pick_matrix(xs[j][...], total + 2 * e_ref[0] + x, c)
            totals[j] = totals[j] + dot(pick, rows[j * c : (j + 1) * c])
    for j in range(2):
        outs[j][...] = totals[j].astype(BF)


def whole(shape):
    return pl.BlockSpec(shape, lambda i, e: (0,) * len(shape), pipeline_mode=pl.Buffered(1))


def expert_stage(
    k, stages, capacity, total, e, x_pair, g_pair, gates, ups, downs, sg, su, sd, carry, bufs
):
    tokens, wide = x_pair[0].shape
    width = sg.shape[0]
    hidden = gates[0].shape[2]
    c2 = 2 * capacity
    shared = sg.shape[1]
    olds = 0 if bufs is None else 6
    shapes = [
        ((stages, 2 * tokens, shared), (1, 2 * tokens, shared), (k, 0, 0)),
        ((2, stages, c2, width), (2, 1, c2, width), (0, k, 0, 0)),
        ((2, stages, c2, width), (2, 1, c2, width), (0, k, 0, 0)),
        ((4, 2, stages, c2, hidden), (4, 2, 1, c2, hidden), (0, 0, k, 0, 0)),
        ((4, 2, stages, c2, hidden), (4, 2, 1, c2, hidden), (0, 0, k, 0, 0)),
        ((4, 2, stages, c2, hidden), (4, 2, 1, c2, hidden), (0, 0, k, 0, 0)),
    ]

    def at(block, where):
        return pl.BlockSpec(block, lambda i, e: where)

    ins = [e, *x_pair, *g_pair, *gates, *ups, *downs, sg, su, sd, *carry]
    in_specs = [whole(v.shape) for v in ins[1:]]
    alias = {}
    if bufs is not None:
        for n, b in enumerate(bufs):
            alias[len(ins)] = 4 + n
            ins.append(b)
            in_specs.append(pl.BlockSpec(memory_space=pl.ANY))
    out_shape = [jax.ShapeDtypeStruct((tokens, wide), BF)] * 2 + [
        jax.ShapeDtypeStruct(v.shape, v.dtype) for v in carry
    ]
    out_specs = [whole((tokens, wide))] * 2 + [whole(v.shape) for v in carry]
    for full, block, where in shapes:
        out_shape.append(jax.ShapeDtypeStruct(full, BF))
        out_specs.append(at(block, where))
    outs = pl.pallas_call(
        functools.partial(expert_kernel, capacity, total, olds),
        grid_spec=pltpu.PrefetchScalarGridSpec(
            num_scalar_prefetch=1, grid=(1,), in_specs=in_specs, out_specs=out_specs
        ),
        out_shape=out_shape,
        input_output_aliases=alias,
        compiler_params=pltpu.CompilerParams(vmem_limit_bytes=60 * MIB),
        cost_estimate=pl.CostEstimate(
            flops=20 * c2 * width * 4 * hidden, bytes_accessed=24 * MIB, transcendentals=c2 * 8 * hidden
        ),
    )(*ins)
    return outs[0:2], outs[2:4], outs[4:]


def expert_out(k, capacity, total, e, x_pair, wa, sa, downs, sd):
    tokens = x_pair[0].shape[0]
    width = sd.shape[1]
    c2 = wa.shape[3]
    last = x_pair[0].shape[1] // LANES - 1
    meta = pl.BlockSpec((tokens, LANES), lambda i, e: (0, last))
    return pl.pallas_call(
        functools.partial(expert_out_kernel, capacity, total),
        grid_spec=pltpu.PrefetchScalarGridSpec(
            num_scalar_prefetch=1,
            grid=(1,),
            in_specs=[
                meta,
                meta,
                pl.BlockSpec((4, 2, 1, c2, wa.shape[4]), lambda i, e: (0, 0, k, 0, 0)),
                pl.BlockSpec((1,) + sa.shape[1:], lambda i, e: (k, 0, 0)),
            ]
            + [whole(d.shape) for d in downs]
            + [whole(sd.shape)],
            out_specs=[whole((tokens, width))] * 2,
        ),
        out_shape=[jax.ShapeDtypeStruct((tokens, width), BF)] * 2,
        compiler_params=pltpu.CompilerParams(vmem_limit_bytes=40 * MIB),
        cost_estimate=pl.CostEstimate(
            flops=4 * c2 * width * 4 * wa.shape[4], bytes_accessed=10 * MIB, transcendentals=0
        ),
    )(e, *x_pair, wa, sa, *downs, sd)


def dispatch_kernel(capacity, total, x_ref, m_ref, g0_ref, g1_ref, g_all, *refs):
    experts = refs[0:3]
    sg_ref, su_ref, sd_ref = refs[3:6]
    dx_ref, wb_ref, near_ref, far_ref, sgg_ref, sdg_ref = refs[6:12]
    xr_ref, gr_ref, gu_ref, wa_ref, last_ref, down_far, down_last = refs[12:19]
    xbuf, sbuf, tbuf, mbuf, nbuf, bbuf, sbbuf, tbbuf, wgu, wd, gbuf, gown, acts, wacts = refs[19:33]
    (
        rx_s,
        rx_r,
        sx_s,
        sx_r,
        sr_s,
        sr_r,
        rt_s,
        rt_r,
        rm_s,
        rm_r,
        sm_s,
        sm_r,
        sb_s,
        sb_r,
        rb_s,
        rb_r,
        w_sem,
        l_s,
        l_r,
    ) = refs[33:]
    experts = experts + (last_ref,)
    k = pl.program_id(0)
    stages = xbuf.shape[0]
    tokens, width = x_ref.shape[0], sg_ref.shape[0]
    hidden = experts[0].shape[1] // 3
    inner = 4 * hidden
    c = capacity
    last = stages - 1
    e, h = lax.axis_index("ep"), lax.axis_index("hp")
    n = 2 * stages
    right, left = (lax.rem(e + 2, n), h), (lax.rem(e + n - 2, n), h)
    pair = (e + 1 - 2 * lax.rem(e, 2), h)
    core = (e, h + 1 - 2 * lax.rem(h, 2))
    y_far = (e, lax.rem(h + 2, 4))

    def ring_x(i):
        return mesh_copy(xbuf.at[i, 0], xbuf.at[i + 1, 0], rx_s, rx_r, i, right)

    def ring_last():
        return mesh_copy(xbuf.at[last - 1, 1], xbuf.at[last, 1], rx_s, rx_r, last, right)

    def swap_x(i):
        return mesh_copy(xbuf.at[i, 0], xbuf.at[i, 1], sx_s, sx_r, i, pair)

    def ring_m(i):
        return mesh_copy(mbuf.at[i], mbuf.at[i + 1], rm_s, rm_r, i, right)

    def swap_m(i):
        return mesh_copy(mbuf.at[i], nbuf.at[i], sm_s, sm_r, i, pair)

    def swap_r(i):
        return mesh_copy(xbuf.at[i, 1], sbuf.at[i], sr_s, sr_r, i, pair)

    def ring_t(i):
        return mesh_copy(xbuf.at[i, 0], tbuf.at[i], rt_s, rt_r, i, right)

    def swap_b(i):
        return mesh_copy(bbuf.at[i, 1], sbbuf.at[i], sb_s, sb_r, i, pair)

    def ring_b(i):
        return mesh_copy(bbuf.at[i, 0], tbbuf.at[i], rb_s, rb_r, i, right)

    to_core = mesh_copy(experts[1], last_ref, l_s, l_r, 0, core)
    down_over = mesh_copy(
        experts[0].at[:, pl.ds(2 * hidden, hidden), :], down_far, l_s, l_r, 1, y_far
    )
    down_on = mesh_copy(down_far, down_last, l_s, l_r, 2, core)
    last_g = mesh_copy(g_all.at[last], gbuf, l_s, l_r, 3, pair)

    def weight_copies(r):
        copies = []
        for x in range(2):
            for i, (to, at) in enumerate(((wgu, 0), (wgu, inner), (wd, 0))):
                if i == 2 and r % 2 == 1:
                    src = (down_far if r == 1 else down_last).at[x]
                else:
                    src = experts[r].at[x, pl.ds(i * hidden, hidden), :]
                copies.append(
                    pltpu.make_async_copy(
                        src,
                        to.at[x, pl.ds(at + r * hidden, hidden), :],
                        w_sem.at[6 * r + 3 * x + i],
                    )
                )
        return copies

    @pl.when(k == 0)
    def _():
        xbuf[0, 0] = x_ref[...]
        mbuf[0] = m_ref[...]
        greet((right, left, pair, core, y_far))
        down_over.start()
        ring_m(0).start()
        swap_m(0).start()
        ring_x(0).start()
        swap_x(0).start()
        to_core.start()
        for r in (0, 2):
            for copy in weight_copies(r):
                copy.start()
        sgg_ref[...] = jnp.zeros_like(sgg_ref)
        sdg_ref[...] = jnp.zeros_like(sdg_ref)

    @pl.when(k < last)
    def _():
        ring_m(k).wait_recv()
        swap_m(k + 1).start()
        ring_x(k).wait_recv()

    @pl.when(k < last - 1)
    def _():
        ring_m(k + 1).start()
        ring_x(k + 1).start()
        swap_x(k + 1).start()

    @pl.when(k < last)
    def _():
        swap_x(k).wait_recv()

    @pl.when(k == 0)
    def _():
        last_g.start()

    @pl.when(k == last - 1)
    def _():
        ring_last().start()

    @pl.when(k < last)
    def _():
        gown[...] = g1_ref[0]

    @pl.when(k == last)
    def _():
        ring_last().wait_recv()
        last_g.wait()
        gown[...] = gbuf[...]

    swap_m(k).wait_recv()

    @pl.when(k == 0)
    def _():
        down_over.wait_recv()
        down_on.start()
        for copy in weight_copies(1):
            copy.start()
        to_core.wait()
        down_on.wait()
        for copy in weight_copies(3):
            copy.start()
        down_over.wait_send()
        for r in range(4):
            for copy in weight_copies(r):
                copy.wait()

    gs = (g0_ref.at[0], gown)
    x2 = jnp.concatenate([xbuf[k, j] for j in range(2)], axis=0)
    g2 = jnp.concatenate([g[...] for g in gs], axis=0)
    hg, hu = dot(x2, sg_ref[...]), dot(x2, su_ref[...])
    ab = dot(g2, sd_ref[...], (1, 1))
    s = jax.nn.sigmoid(hg)
    silu = hg * s
    act = (silu * hu).astype(BF)
    gi = (ab * hu * (s * (1.0 + hg * (1.0 - s)))).astype(BF)
    ui = (ab * silu).astype(BF)
    sgg_ref[...] += dot(x2, jnp.concatenate([gi, ui], axis=1), (0, 0))
    sdg_ref[...] += dot(act, g2, (0, 0))
    acts[k] = act
    dx = dot(gi, sg_ref[...], (1, 1)) + dot(ui, su_ref[...], (1, 1))
    totals = [dx[:tokens], dx[tokens:]]
    backs = [0.0, 0.0]
    line = lax.broadcasted_iota(jnp.int32, m_ref.shape, 0)
    short = lax.broadcasted_iota(jnp.int32, (total, tokens), 0)
    place = lax.broadcasted_iota(jnp.int32, (c, tokens), 0).astype(F32)

    def hits(i, j, x):
        code = jnp.where(line == total + 2 * e + x, (mbuf, nbuf)[j][i], 0.0)
        return jnp.sum(code, axis=0, keepdims=True) == place

    for x in range(2):
        col = 2 * e + x
        picks, weights, found = [], [], []
        for j in range(2):
            weight = jnp.where(line == col, (mbuf, nbuf)[j][k], 0.0)
            weight = jnp.sum(weight, axis=0, keepdims=True)
            hit = hits(k, j, x)
            pick = jnp.where(hit, 1.0, 0.0).astype(BF)
            found.append(hit)
            picks.append(pick)
            weights.append(jnp.sum(jnp.where(hit, weight, 0.0), axis=1, keepdims=True))
            xr_ref[x, 0, j * c : (j + 1) * c, :] = dot(pick, xbuf[k, j]).astype(BF)
            gr_ref[x, 0, j * c : (j + 1) * c, :] = dot(pick, gs[j][...]).astype(BF)
        w = jnp.concatenate(weights, axis=0)
        xr, gr = xr_ref[x, 0], gr_ref[x, 0]
        hgu = dot(xr, wgu[x], (1, 1))
        ab = dot(gr, wd[x], (1, 1))
        hg, hu = hgu[:, :inner], hgu[:, inner:]
        s = jax.nn.sigmoid(hg)
        silu = hg * s
        act = silu * hu
        wb = jnp.sum(act * ab, axis=1, keepdims=True)
        ab = ab * w
        gu_ref[x, 0, :, :inner] = (ab * hu * (s * (1.0 + hg * (1.0 - s)))).astype(BF)
        gu_ref[x, 0, :, inner:] = (ab * silu).astype(BF)
        wa_ref[x, 0] = (act * w).astype(BF)
        wacts[k, x] = wa_ref[x, 0]
        dxr = dot(gu_ref[x, 0], wgu[x]).astype(BF)
        for j in range(2):
            span = slice(j * c, (j + 1) * c)
            totals[j] = totals[j] + dot(picks[j], dxr[span], (0, 0))
            row = jnp.sum(jnp.where(found[j], wb[span], 0.0), axis=0, keepdims=True)
            backs[j] = backs[j] + jnp.where(short == col, row, 0.0)

    @pl.when(k < last)
    def _():
        ring_x(k).wait_send()
        swap_x(k).wait_send()

    @pl.when(k == last - 1)
    def _():
        ring_last().wait_send()

    for j in range(2):
        xbuf[k, j] = totals[j].astype(BF)
        bbuf[k, j] = backs[j]

    @pl.when(k >= 1)
    def _():
        swap_b(k).start()
        swap_r(k).start()

    def advance(i, first):
        swap_b(i).wait_recv()
        swap_r(i).wait_recv()
        here = xbuf[i, 0].astype(F32) + sbuf[i].astype(F32)
        small = bbuf[i, 0] + sbbuf[i]
        if not first:
            ring_b(i - 1).wait_recv()
            ring_t(i - 1).wait_recv()
            here = here + tbuf[i - 1].astype(F32)
            small = small + tbbuf[i - 1]
        xbuf[i, 0] = here.astype(BF)
        bbuf[i, 0] = small
        ring_b(i).start()
        ring_t(i).start()

    for i in range(1, last):

        @pl.when(k == i + 1)
        def _(i=i):
            advance(i, i == 1)

    def forward(i):
        out = dot(acts[i], sd_ref[...])
        outs = [out[:tokens], out[tokens:]]
        for x in range(2):
            rows = dot(wacts[i, x], wd[x]).astype(BF)
            for j in range(2):
                pick = jnp.where(hits(i, j, x), 1.0, 0.0).astype(BF)
                outs[j] = outs[j] + dot(pick, rows[j * c : (j + 1) * c], (0, 0))
        near_ref[i] = outs[0].astype(BF)
        far_ref[i] = outs[1].astype(BF)

    @pl.when(k == last)
    def _():
        swap_b(0).start()
        swap_r(0).start()
        for i in range(stages // 2 + 1):
            forward(i)
        advance(last, last == 1)
        for i in range(stages // 2 + 1, stages):
            forward(i)
        swap_b(0).wait_recv()
        swap_r(0).wait_recv()
        ring_b(last).wait_recv()
        ring_t(last).wait_recv()
        dx_ref[...] = xbuf[0, 0].astype(F32) + sbuf[0].astype(F32) + tbuf[last].astype(F32)
        wb_ref[...] = bbuf[0, 0] + sbbuf[0] + tbbuf[last]
        for i in range(stages):
            swap_r(i).wait_send()
            swap_b(i).wait_send()
            swap_m(i).wait_send()
        for i in range(1, stages):
            ring_t(i).wait_send()
            ring_b(i).wait_send()
            ring_m(i - 1).wait_send()


def dispatch(capacity, total, x, meta, g_near, g_far, experts, sg, su, sd):
    stages = g_near.shape[0]
    most = stages - 1
    tokens, width = x.shape
    lines = meta.shape[0]
    shared = sg.shape[1]
    hidden = experts[0].shape[1] // 3
    inner = 4 * hidden
    c2 = 2 * capacity
    once = pl.Buffered(1)
    dma = pltpu.SemaphoreType.DMA

    def fixed(shape):
        return pl.BlockSpec(shape, lambda k: (0,) * len(shape), pipeline_mode=once)

    def per_stage(shape):
        return pl.BlockSpec(shape, lambda k: (0, k, 0, 0), pipeline_mode=once)

    anywhere = pl.BlockSpec(memory_space=pl.ANY)
    return pl.pallas_call(
        functools.partial(dispatch_kernel, capacity, total),
        grid=(stages,),
        in_specs=[
            fixed((tokens, width)),
            fixed(meta.shape),
            pl.BlockSpec((1, tokens, width), lambda k: (k, 0, 0)),
            pl.BlockSpec((1, tokens, width), lambda k: (k - k // most, 0, 0)),
            anywhere,
        ]
        + [anywhere] * 3
        + [fixed(sg.shape), fixed(su.shape), fixed(sd.shape)],
        out_specs=[
            fixed((tokens, width)),
            fixed((total, tokens)),
            fixed((stages, tokens, width)),
            fixed((stages, tokens, width)),
            fixed((width, 2 * shared)),
            fixed((shared, width)),
            per_stage((2, 1, c2, width)),
            per_stage((2, 1, c2, width)),
            per_stage((2, 1, c2, 2 * inner)),
            per_stage((2, 1, c2, inner)),
            anywhere,
            anywhere,
            anywhere,
        ],
        out_shape=[
            jax.ShapeDtypeStruct((tokens, width), F32),
            jax.ShapeDtypeStruct((total, tokens), F32),
            jax.ShapeDtypeStruct((stages, tokens, width), BF),
            jax.ShapeDtypeStruct((stages, tokens, width), BF),
            jax.ShapeDtypeStruct((width, 2 * shared), F32),
            jax.ShapeDtypeStruct((shared, width), F32),
            jax.ShapeDtypeStruct((2, stages, c2, width), BF),
            jax.ShapeDtypeStruct((2, stages, c2, width), BF),
            jax.ShapeDtypeStruct((2, stages, c2, 2 * inner), BF),
            jax.ShapeDtypeStruct((2, stages, c2, inner), BF),
            jax.ShapeDtypeStruct(experts[1].shape, BF),
            jax.ShapeDtypeStruct((2, hidden, width), BF),
            jax.ShapeDtypeStruct((2, hidden, width), BF),
        ],
        scratch_shapes=[
            pltpu.VMEM((stages, 2, tokens, width), BF),
            pltpu.VMEM((stages, tokens, width), BF),
            pltpu.VMEM((stages, tokens, width), BF),
            pltpu.VMEM((stages, lines, tokens), F32),
            pltpu.VMEM((stages, lines, tokens), F32),
            pltpu.VMEM((stages, 2, total, tokens), F32),
            pltpu.VMEM((stages, total, tokens), F32),
            pltpu.VMEM((stages, total, tokens), F32),
            pltpu.VMEM((2, 2 * inner, width), BF),
            pltpu.VMEM((2, inner, width), BF),
            pltpu.VMEM((tokens, width), BF),
            pltpu.VMEM((tokens, width), BF),
            pltpu.VMEM((stages, 2 * tokens, shared), BF),
            pltpu.VMEM((stages, 2, c2, inner), BF),
        ]
        + [dma((stages,))] * 16
        + [dma((24,))]
        + [dma((4,))] * 2,
        compiler_params=pltpu.CompilerParams(
            vmem_limit_bytes=63 * MIB, collective_id=0, has_side_effects=True
        ),
        cost_estimate=pl.CostEstimate(
            flops=24 * c2 * stages * width * 4 * hidden,
            bytes_accessed=80 * MIB,
            transcendentals=stages * c2 * 8 * hidden,
        ),
    )(x, meta, g_near, g_far, g_near, *experts, sg, su, sd)[:10]


def expert_grad_kernel(
    xr_ref, gr_ref, gu_ref, wa_ref, near_ref, far_ref, keep, sendb, recvb, s_s, s_r
):
    s = pl.program_id(0)
    steps = sendb.shape[0]
    half = sendb.shape[1]
    h = lax.axis_index("hp")
    core = (lax.axis_index("ep"), h + 1 - 2 * lax.rem(h, 2))

    def over_core(n):
        return mesh_copy(sendb.at[n], recvb.at[n], s_s, s_r, n, core)

    @pl.when(s == 0)
    def _():
        greet([core])

    def give(v):
        sendb[s] = v[half:].astype(BF)
        over_core(s).start()
        keep[lax.rem(s, 2)] = v[:half].astype(BF)

    @pl.when((s < steps) & (lax.rem(s, 3) < 2))
    def _():
        give(dot(gu_ref[0], xr_ref[0], (0, 0)))

    @pl.when((s < steps) & (lax.rem(s, 3) == 2))
    def _():
        give(dot(wa_ref[0], gr_ref[0], (0, 0)))

    @pl.when(s > 0)
    def _():
        n = s - 1
        over_core(n).wait_recv()
        total = (keep[lax.rem(n, 2)].astype(F32) + recvb[n].astype(F32)).astype(BF)
        near_ref[0, 0] = total[: half // 2]
        far_ref[0, 0] = total[half // 2 :]

    @pl.when(s == steps)
    def _():
        for n in range(steps):
            over_core(n).wait_send()


def expert_grads(xr, gr, gu, wa, hidden):
    rows, width = xr.shape[1:]
    inner, steps = 4 * hidden, 6
    dma = pltpu.SemaphoreType.DMA

    def now(s):
        return s - s // steps

    def before(s):
        return s - 1 + (steps - s) // steps

    rows_in = pl.BlockSpec((1, rows, width), lambda s: (now(s) // 3, 0, 0))
    out = pl.BlockSpec((1, 1, hidden, width), lambda s: (before(s) // 3, before(s) % 3, 0, 0))
    near, far = pl.pallas_call(
        expert_grad_kernel,
        grid=(steps + 1,),
        in_specs=[
            rows_in,
            rows_in,
            pl.BlockSpec(
                (1, rows, inner), lambda s: (now(s) // 3, 0, now(s) % 3 - now(s) % 3 // 2)
            ),
            pl.BlockSpec((1, rows, inner), lambda s: (now(s) // 3, 0, 0)),
        ],
        out_specs=[out, out],
        out_shape=[jax.ShapeDtypeStruct((2, 3, hidden, width), BF)] * 2,
        scratch_shapes=[pltpu.VMEM((2, inner // 2, width), BF)]
        + [pltpu.VMEM((steps, inner // 2, width), BF)] * 2
        + [dma((steps,))] * 2,
        compiler_params=pltpu.CompilerParams(
            vmem_limit_bytes=60 * MIB, collective_id=4, has_side_effects=True
        ),
        cost_estimate=pl.CostEstimate(
            flops=12 * rows * inner * width, bytes_accessed=40 * MIB, transcendentals=0
        ),
    )(xr, gr, gu, wa)
    return (v.reshape(2, 3 * hidden, width) for v in (near, far))


def mesh_copy(src, dst, s, r, i, where):
    return pltpu.make_async_remote_copy(
        src_ref=src,
        dst_ref=dst,
        send_sem=s.at[i],
        recv_sem=r.at[i],
        device_id=where,
        device_id_type=pl.DeviceIdType.MESH,
    )


def greet(peers):
    barrier = pltpu.get_barrier_semaphore()
    for where in peers:
        pl.semaphore_signal(barrier, inc=1, device_id=where, device_id_type=pl.DeviceIdType.MESH)
    pl.semaphore_wait(barrier, len(peers))


def front_kernel(large, count, *refs):
    tok_ref, exp_ref, cot_ref = refs[0:3]
    ins = refs[3 : 3 + count]
    far_ref, expo_ref, g_ref = refs[3 + count : 6 + count]
    outs = refs[6 + count : 6 + 2 * count]
    y_s, y_r, c_s, c_r, f_s, f_r, p_s, p_r, q_s, q_r, l_sem, rg_s, rg_r = refs[6 + 2 * count :]
    stages = g_ref.shape[0]
    n = 2 * stages
    e, h = lax.axis_index("ep"), lax.axis_index("hp")
    x = lax.rem(e, 2)
    h_core, h_far = h + 1 - 2 * lax.rem(h, 2), lax.rem(h + 2, 4)
    core, far = (e, h_core), (e, h_far)
    right, left = (lax.rem(e + 2, n), h), (lax.rem(e + n - 2, n), h)
    pair = (e + 1 - 2 * x, h)
    greet((core, far, right, left, pair))

    def ring_g(k):
        src = cot_ref if k == 0 else g_ref.at[k]
        return mesh_copy(src, g_ref.at[k + 1], rg_s, rg_r, k, right)

    def part(i, other=False):
        rows = ins[i].shape[0] // 2
        return pl.ds((1 - x if other else x) * rows, rows)

    over_y, over_pair, onward, onward_too = [], [], [], []
    for i, v in enumerate(ins):
        o = outs[i]
        if i < large:
            mine, theirs = part(i), part(i, True)
            over_y.append(mesh_copy(v.at[mine], o.at[h, mine], y_s, y_r, i, far))
            got, rest = o.at[h_far, mine], o.at[h_far, theirs]
            over_pair.append(mesh_copy(got, got, p_s, p_r, i, pair))
            onward.append(mesh_copy(got, got, f_s, f_r, i, core))
            onward_too.append(mesh_copy(rest, rest, q_s, q_r, i, core))
        else:
            over_y.append(mesh_copy(v, o.at[h], y_s, y_r, i, far))
            onward.append(mesh_copy(o.at[h_far], o.at[h_far], f_s, f_r, i, core))
    over_y.append(mesh_copy(tok_ref, far_ref, y_s, y_r, count, far))
    over_core = [mesh_copy(v, outs[i].at[h], c_s, c_r, i, core) for i, v in enumerate(ins)]
    over_core.append(mesh_copy(exp_ref, expo_ref, c_s, c_r, count, core))
    local = [pltpu.make_async_copy(v, outs[i].at[h], l_sem.at[i]) for i, v in enumerate(ins)]
    local.append(pltpu.make_async_copy(cot_ref, g_ref.at[0], l_sem.at[count]))
    for copy in over_y:
        copy.start()
    ring_g(0).start()
    for copy in over_core + local:
        copy.start()
    for k in range(max(stages - 1, large)):
        if k < large:
            over_y[k].wait_recv()
            over_pair[k].start()
            onward[k].start()
        if k < stages - 1:
            ring_g(k).wait_recv()
            if k + 1 < stages - 1:
                ring_g(k + 1).start()
    for k in range(large, count):
        over_y[k].wait_recv()
        onward[k].start()
    over_y[count].wait_recv()
    for k in range(large):
        over_pair[k].wait_recv()
        onward_too[k].start()
    for copy in over_y + over_pair + [ring_g(k) for k in range(stages - 1)]:
        copy.wait_send()
    for copy in over_core + onward + onward_too + local:
        copy.wait()


def front(stages, tokens, experts, cotangent, blocks, large):
    count = len(blocks)
    anywhere, vmem = (pl.BlockSpec(memory_space=m) for m in (pl.ANY, pltpu.VMEM))
    dma = pltpu.SemaphoreType.DMA
    return pl.pallas_call(
        functools.partial(front_kernel, large, count),
        in_specs=[anywhere] * 2 + [vmem] * (1 + count),
        out_specs=[anywhere] * (3 + count),
        out_shape=[
            jax.ShapeDtypeStruct(tokens.shape, BF),
            jax.ShapeDtypeStruct(experts.shape, BF),
            jax.ShapeDtypeStruct((stages,) + cotangent.shape, BF),
        ]
        + [jax.ShapeDtypeStruct((4,) + v.shape, BF) for v in blocks],
        scratch_shapes=[dma((count + 1,))] * 4
        + [dma((count,))] * 6
        + [dma((count + 1,))]
        + [dma((stages,))] * 2,
        compiler_params=pltpu.CompilerParams(
            vmem_limit_bytes=32 * MIB, collective_id=1, has_side_effects=True
        ),
        cost_estimate=pl.CostEstimate(flops=0, bytes_accessed=120 * MIB, transcendentals=0),
    )(tokens, experts, cotangent, *blocks)


class SharedSum:
    def __init__(self, at, peers, ref, got, to_far, from_far, fin, s, r):
        c, y, x, z = at
        core, far, pair, up = peers
        self.at, self.fin = at, fin
        self.ref, self.got, self.to_far, self.from_far = ref, got, to_far, from_far
        self.core = mesh_copy(ref.at[:, 1 - c], got, s, r, 0, core)
        self.far = mesh_copy(to_far, from_far, s, r, 1, far)
        own = fin.at[x, z]
        self.up = [mesh_copy(own, own, s, r, 1 + k, up[k]) for k in range(1, 4)]
        self.pair = mesh_copy(fin.at[x], fin.at[x], s, r, 5, pair)
        self.all = [self.core, self.far, self.pair] + self.up

    def over_y(self):
        c, y, _, _ = self.at
        self.core.wait_recv()
        total = self.ref[1 - y, c].astype(F32) + self.got[1 - y].astype(F32)
        self.to_far[...] = total.astype(BF)
        self.far.start()

    def over_z(self):
        c, y, x, z = self.at
        self.far.wait_recv()
        total = self.ref[y, c].astype(F32) + self.got[y].astype(F32)
        self.fin[x, z] = (total + self.from_far[...].astype(F32)).astype(BF)
        for copy in self.up:
            copy.start()

    def over_x(self):
        for copy in self.up:
            copy.wait_recv()
        self.pair.start()


def back_kernel(
    q_ref,
    ka_ref,
    kb_ref,
    va_ref,
    vb_ref,
    d_ref,
    lse_ref,
    wq_ref,
    wk_ref,
    wv_ref,
    cos_ref,
    sin_ref,
    x_ref,
    tok_ref,
    ftok_ref,
    sg_ref,
    sd_ref,
    spread_ref,
    stack_ref,
    near_ref,
    mid_ref,
    away_ref,
    piece_ref,
    qp_ref,
    kp_ref,
    vp_ref,
    first_ref,
    share_ref,
    gain_ref,
    sgout_ref,
    suout_ref,
    sdout_ref,
    layer_ref,
    piece_far,
    sendb,
    recvb,
    nearb,
    kvacc,
    qacc,
    sg_c,
    sg_y,
    sg_yr,
    sg_fin,
    sd_c,
    sd_y,
    sd_yr,
    sd_fin,
    xgot,
    zsend,
    zgot,
    k_s,
    k_r,
    s_s,
    s_r,
    d_s,
    d_r,
    x_s,
    x_r,
    z_s,
    z_r,
    p_s,
    p_r,
):
    i = pl.program_id(0)
    heads = sendb.shape[0]
    rows, half = q_ref.shape[0], ka_ref.shape[0]
    e, h = lax.axis_index("ep"), lax.axis_index("hp")
    x, z = lax.rem(e, 2), e // 2
    c, y = lax.rem(h, 2), h // 2
    core, far = (e, h + 1 - 2 * c), (e, lax.rem(h + 2, 4))
    pair = (e + 1 - 2 * x, h)
    up = [None] + [(2 * lax.rem(z + s, 4) + x, h) for s in range(1, 4)]

    def over_core(n):
        return mesh_copy(sendb.at[n], recvb.at[n], k_s, k_r, n, core)

    def over_x(n):
        return mesh_copy(away_ref.at[n], xgot.at[n], x_s, x_r, n, pair)

    def home(n):
        return mesh_copy(zsend.at[n - 1], zgot.at[n - 1], z_s, z_r, n - 1, up[4 - n])

    hidden = piece_ref.shape[1] // 3
    pieces = []
    for n in range(6):
        place = (n // 3, pl.ds(n % 3 * hidden, hidden))
        pieces.append(mesh_copy(piece_ref.at[place], piece_far.at[place], p_s, p_r, n, far))
    at, peers = (c, y, x, z), (core, far, pair, up)
    sums = [
        SharedSum(at, peers, sg_ref, sg_c, sg_y, sg_yr, sg_fin, s_s, s_r),
        SharedSum(at, peers, sd_ref, sd_c, sd_y, sd_yr, sd_fin, d_s, d_r),
    ]

    def send_home(n):
        over_x(n).wait_recv()
        zsend[n - 1] = (near_ref[n].astype(F32) + xgot[n].astype(F32)).astype(BF)
        home(n).start()

    @pl.when(i == 0)
    def _():
        greet([core, far, pair] + up[1:])
        for n in (1, 2, 3, 0):
            over_x(n).start()
        for flow in sums:
            flow.core.start()
        pieces[0].start()
        kvacc[...] = jnp.zeros_like(kvacc)
        qacc[...] = jnp.zeros_like(qacc)

    @pl.when(i < heads)
    def _():
        q, d = q_ref[...], d_ref[...]
        cosine, sine = cos_ref[...], -sin_ref[...]
        s = jnp.concatenate([dot(q, ka_ref[...], (1, 1)), dot(q, kb_ref[...], (1, 1))], axis=1)
        s = jnp.where(score_mask(h, rows, 2 * half), s * HD ** (-0.5), -1e30)
        p = jnp.exp(s - lse_ref[:, 0:1])
        back = [dot(d, va_ref[...], (1, 1)), dot(d, vb_ref[...], (1, 1))]
        back = jnp.concatenate(back, axis=1)
        inner = jnp.sum(p * back, axis=1, keepdims=True)
        sb = (p * (back - inner) * HD ** (-0.5)).astype(BF)
        p = p.astype(BF)
        dq = dot(sb[:, :half], ka_ref[...]) + dot(sb[:, half:], kb_ref[...])
        dk = turned(dot(sb, q, (0, 0)), cosine, sine)
        dv = dot(p, d, (0, 0))
        nearb[lax.rem(i, 2), 0] = dk[:half]
        nearb[lax.rem(i, 2), 1] = dv[:half]
        sendb[i, 0] = dk[half:].astype(BF)
        sendb[i, 1] = dv[half:].astype(BF)
        over_core(i).start()
        raw = turned(dq, cosine[:rows], sine[:rows]).astype(BF)
        qp_ref[...] = dot(x_ref[:rows, :], raw, (0, 0)).astype(BF)
        qacc[...] += dot(raw, wq_ref[...], (1, 1))

    @pl.when(i > 0)
    def _():
        n = i - 1
        over_core(n).wait_recv()
        kept = lax.rem(n, 2)
        key = (nearb[kept, 0] + recvb[n, 0].astype(F32)).astype(BF)
        value = (nearb[kept, 1] + recvb[n, 1].astype(F32)).astype(BF)
        kp_ref[...] = dot(x_ref[...], key, (0, 0)).astype(BF)
        vp_ref[...] = dot(x_ref[...], value, (0, 0)).astype(BF)
        kvacc[...] += dot(key, wk_ref[...], (1, 1)) + dot(value, wv_ref[...], (1, 1))

    @pl.when(i == 1)
    def _():
        for flow in sums:
            flow.over_y()
        for copy in pieces[1:]:
            copy.start()

    @pl.when(i == 4)
    def _():
        send_home(1)

    @pl.when(i == 5)
    def _():
        for flow in sums:
            flow.over_z()

    @pl.when(i == 7)
    def _():
        send_home(2)

    @pl.when(i == heads - 1)
    def _():
        for flow in sums:
            flow.over_x()

    @pl.when(i == heads)
    def _():
        first_ref[...] = qacc[...] + kvacc[:rows, :]
        share_ref[...] = kvacc[rows:, :].astype(BF)
        gain = jnp.zeros((1, kvacc.shape[1]), F32)
        for ref, upstream in ((tok_ref, first_ref[...]), (ftok_ref, kvacc[rows:, :])):
            v = ref[...].astype(F32)
            gain = gain + jnp.sum(upstream * v * rms(v), axis=0, keepdims=True)
        gain_ref[...] = gain
        send_home(3)
        over_x(0).wait_recv()
        total = mid_ref[...] + near_ref[0].astype(F32) + xgot[0].astype(F32)
        for n in (1, 2, 3):
            home(n).wait_recv()
            total = total + zgot[n - 1].astype(F32)
        layer_ref[...] = total.astype(BF)
        for flow in sums:
            flow.pair.wait_recv()
        lanes = sg_fin.shape[3] // 2
        gate = more = down = 0.0
        for k in range(8):
            block = sg_fin[k % 2, k // 2]
            gate = gate + dot(block[:, :lanes], spread_ref[k])
            more = more + dot(block[:, lanes:], spread_ref[k])
            down = down + dot(stack_ref[k], sd_fin[k % 2, k // 2])
        sgout_ref[...] = gate
        suout_ref[...] = more
        sdout_ref[...] = down
        for copy in pieces:
            copy.wait()
        for flow in sums:
            for copy in flow.all:
                copy.wait_send()
        for n in range(4):
            over_x(n).wait_send()
        for n in (1, 2, 3):
            home(n).wait_send()
        for n in range(heads):
            over_core(n).wait_send()


def attend_back_and_sums(
    q, kv_a, kv_b, d, lse, weights, tables, first_in, pairs, sgg, sdg, spread, stack, near, middle, away, piece
):
    rows, width = q.shape
    half = kv_a.shape[1]
    stages = near.shape[0]
    dma = pltpu.SemaphoreType.DMA
    once = pl.Buffered(1)
    anywhere = pl.BlockSpec(memory_space=pl.ANY)

    def fixed(v):
        return pl.BlockSpec(v.shape, lambda i: (0,) * v.ndim, pipeline_mode=once)

    def now(i):
        return i - i // H

    def before(i):
        return i - 1 + (H - i) // H

    def head(rows_of, at=now):
        return pl.BlockSpec((rows_of, HD), lambda i: (0, at(i)))

    def kv(which):
        return pl.BlockSpec((None, half, HD), lambda i: (which, 0, now(i)))

    def shape(dims, dtype):
        return jax.ShapeDtypeStruct(dims, dtype)

    def buffers(dims):
        return [
            pltpu.VMEM((2,) + dims, BF),
            pltpu.VMEM(dims, BF),
            pltpu.VMEM(dims, BF),
            pltpu.VMEM((2, 4) + dims, BF),
        ]

    kept = [*tables, first_in, *pairs, sgg, sdg, spread, stack, near, middle]
    ends = [
        shape((rows, width), F32),
        shape((rows, width), BF),
        shape((1, width), F32),
        shape((width // 4, spread.shape[2]), F32),
        shape((width // 4, spread.shape[2]), F32),
        shape((stack.shape[1], width), F32),
        shape((rows, width), BF),
    ]
    return pl.pallas_call(
        back_kernel,
        grid=(H + 1,),
        in_specs=[head(rows), kv(0), kv(0), kv(1), kv(1), head(rows), head(rows)]
        + [head(width), head(width, before), head(width, before)]
        + [fixed(v) for v in kept]
        + [anywhere] * 2,
        out_specs=[head(width), head(width, before), head(width, before)]
        + [fixed(v) for v in ends]
        + [anywhere],
        out_shape=[shape((width, width), BF)] * 3 + ends + [shape(piece.shape, BF)],
        scratch_shapes=[
            pltpu.VMEM((H, 2, half, HD), BF),
            pltpu.VMEM((H, 2, half, HD), BF),
            pltpu.VMEM((2, 2, half, HD), F32),
            pltpu.VMEM((half, width), F32),
            pltpu.VMEM((rows, width), F32),
        ]
        + buffers(sgg.shape[2:])
        + buffers(sdg.shape[2:])
        + [
            pltpu.VMEM((stages, rows, width), BF),
            pltpu.VMEM((stages - 1, rows, width), BF),
            pltpu.VMEM((stages - 1, rows, width), BF),
        ]
        + [dma((H,))] * 2
        + [dma((6,))] * 4
        + [dma((stages,))] * 4
        + [dma((6,))] * 2,
        compiler_params=pltpu.CompilerParams(
            vmem_limit_bytes=60 * MIB, collective_id=3, has_side_effects=True
        ),
        cost_estimate=pl.CostEstimate(
            flops=22 * rows * width * width,
            bytes_accessed=60 * MIB,
            transcendentals=rows * 2 * half * H,
        ),
    )(q, kv_a, kv_b, kv_a, kv_b, d, lse, *weights, *kept, away, piece)


def tail_kernel(
    m0,
    m1,
    m2,
    m3,
    sm_ref,
    fb_ref,
    tok_ref,
    gain_ref,
    first_ref,
    mid_ref,
    out_ref,
    smout_ref,
    tokout_ref,
    crecv,
    ysend,
    yrecv,
    acc,
    xrecv,
    zrecv,
    fin,
    g_acc,
    g_recv,
    f_recv,
    c_s,
    c_r,
    y_s,
    y_r,
    x_s,
    x_r,
    z_s,
    z_r,
    za_s,
    za_r,
    xa_s,
    xa_r,
    g_s,
    g_r,
    f_s,
    f_r,
):
    mats = (m0, m1, m2, m3)
    chunks, part = acc.shape[0], acc.shape[3]
    half = m0.shape[3]
    e, h = lax.axis_index("ep"), lax.axis_index("hp")
    x, z = lax.rem(e, 2), e // 2
    c, y = lax.rem(h, 2), h // 2
    core, far = (e, h + 1 - 2 * c), (e, lax.rem(h + 2, 4))
    pair = (e + 1 - 2 * x, h)
    up = [None] + [(2 * lax.rem(z + s, 4) + x, h) for s in range(1, 4)]
    next_z = (2 * (z + 1 - 2 * lax.rem(z, 2)) + x, h)
    greet([core, far, pair] + up[1:])

    def rows(j):
        return pl.ds(j * part, part)

    def over_core(j, m):
        return mesh_copy(
            mats[m].at[:, 1 - c, :, rows(j), :],
            crecv.at[m, :, :, rows(j), :],
            c_s,
            c_r,
            4 * j + m,
            core,
        )

    def over_y(j):
        return mesh_copy(ysend.at[j], yrecv.at[j], y_s, y_r, j, far)

    def over_x(j):
        return mesh_copy(acc.at[j, :, 1 - x], xrecv.at[j], x_s, x_r, j, pair)

    def over_z(j, s):
        return mesh_copy(
            acc.at[j, lax.rem(z + s, 4), x], zrecv.at[j, s - 1], z_s, z_r, 3 * j + s - 1, up[s]
        )

    def back_z(j, s):
        return mesh_copy(fin.at[j, z, x], fin.at[j, z, x], za_s, za_r, 3 * j + s - 1, up[s])

    def back_x(j):
        return mesh_copy(fin.at[j, :, x], fin.at[j, :, x], xa_s, xa_r, j, pair)

    def add_core(j):
        for m in range(4):
            over_core(j, m).wait_recv()
            for at, to in ((y, acc), (1 - y, ysend)):
                total = mats[m][at, c, :, rows(j), :].astype(F32)
                to[j, m] = (total + crecv[m, at, :, rows(j), :].astype(F32)).astype(BF)
        over_y(j).start()

    def add_y(j):
        over_y(j).wait_recv()
        acc[j] = (acc[j].astype(F32) + yrecv[j].astype(F32)).astype(BF)
        over_x(j).start()

    def add_x(j):
        over_x(j).wait_recv()
        acc[j, :, x] = (acc[j, :, x].astype(F32) + xrecv[j].astype(F32)).astype(BF)
        for s in range(1, 4):
            over_z(j, s).start()

    def add_z(j):
        total = acc[j, z, x].astype(F32)
        for s in range(1, 4):
            over_z(j, s).wait_recv()
            total = total + zrecv[j, s - 1].astype(F32)
        fin[j, z, x] = total.astype(BF)
        for s in range(1, 4):
            back_z(j, s).start()

    def end_z(j):
        for s in range(1, 4):
            back_z(j, s).wait_recv()
        back_x(j).start()

    def end_x(j):
        back_x(j).wait_recv()
        for m in range(4):
            for i in range(2):
                out_ref[m, i * half + j * part : i * half + (j + 1) * part, :] = fin[j, m, i]

    route = (core, far, pair, next_z, up[2])
    small = [
        mesh_copy(g_acc.at[i], g_recv.at[i], g_s, g_r, i, route[i]) for i in range(len(route))
    ]

    back = mesh_copy(fb_ref, f_recv, f_s, f_r, 0, far)

    def side(t):
        if t == chunks - lead:
            back.start()
        if t % 2 == 1 and t // 2 < len(small):
            i = t // 2
            small[i].wait_recv()
            g_acc[i + 1] = g_acc[i] + g_recv[i]
            if i + 1 < len(small):
                small[i + 1].start()
        if t == chunks + 3:
            back.wait()
            first_back = first_ref[...] + f_recv[...].astype(F32)
            values = tok_ref[...].astype(F32)
            to_tokens = norm_back(values, rms(values), gain_ref[...], first_back)
            tokout_ref[...] = mid_ref[...] + to_tokens

    lead = 3
    g_acc[0] = sm_ref[...]
    for m in range(4):
        over_core(0, m).start()
    small[0].start()
    for j in range(1, chunks):
        for m in range(4):
            over_core(j, m).start()
    for j in range(lead):
        add_core(j)
    steps = (add_y, add_x, add_z, end_z, end_x)
    for t in range(chunks + len(steps) - 1):
        if t + lead < chunks:
            add_core(t + lead)
        for p in reversed(range(len(steps))):
            if 0 <= t - p < chunks:
                steps[p](t - p)
        side(t)
    smout_ref[...] = g_acc[len(small)]
    for copy in small:
        copy.wait_send()
    for j in range(chunks):
        for m in range(4):
            over_core(j, m).wait_send()
        for copy in (over_y(j), over_x(j), back_x(j)):
            copy.wait_send()
        for s in range(1, 4):
            over_z(j, s).wait_send()
            back_z(j, s).wait_send()


def tail(mats, small, share, tokens, gain, first_back, middle_back):
    width = mats[0].shape[1]
    half = width // 8
    part = 16
    chunks = half // part
    dma = pltpu.SemaphoreType.DMA
    vmem = pl.BlockSpec(memory_space=pltpu.VMEM)
    return pl.pallas_call(
        tail_kernel,
        in_specs=[vmem] * 10,
        out_specs=[vmem] * 3,
        out_shape=[
            jax.ShapeDtypeStruct((4, 2 * half, width), BF),
            jax.ShapeDtypeStruct(small.shape, F32),
            jax.ShapeDtypeStruct(tokens.shape, F32),
        ],
        scratch_shapes=[
            pltpu.VMEM((4, 2, 2, half, width), BF),
            pltpu.VMEM((chunks, 4, 2, part, width), BF),
            pltpu.VMEM((chunks, 4, 2, part, width), BF),
            pltpu.VMEM((chunks, 4, 2, part, width), BF),
            pltpu.VMEM((chunks, 4, part, width), BF),
            pltpu.VMEM((chunks, 3, part, width), BF),
            pltpu.VMEM((chunks, 4, 2, part, width), BF),
            pltpu.VMEM((6,) + small.shape, F32),
            pltpu.VMEM((5,) + small.shape, F32),
            pltpu.VMEM(share.shape, BF),
        ]
        + [dma((4 * chunks,))] * 2
        + [dma((chunks,))] * 4
        + [dma((3 * chunks,))] * 4
        + [dma((chunks,))] * 2
        + [dma((5,))] * 2
        + [dma((1,))] * 2,
        compiler_params=pltpu.CompilerParams(
            vmem_limit_bytes=60 * MIB, collective_id=2, has_side_effects=True
        ),
        cost_estimate=pl.CostEstimate(flops=0, bytes_accessed=300 * MIB, transcendentals=0),
    )(
        *[m.reshape(2, 2, 2, half, width) for m in mats],
        small,
        share,
        tokens,
        gain,
        first_back,
        middle_back,
    )


def rms(values):
    return lax.rsqrt(jnp.mean(values * values, axis=-1, keepdims=True) + epsilon)


def norm_back(values, inv, gain, upstream):
    weighted = upstream * gain
    inner = jnp.mean(weighted * values, axis=-1, keepdims=True)
    return weighted * inv - values * (inv * inv * inv * inner)


def rotary_tables(positions):
    exponent = jnp.arange(HD // 2, dtype=F32) * (2.0 / HD)
    theta = positions.astype(F32)[:, None] * jnp.power(10000.0, -exponent)[None, :]
    cosine, sine = jnp.cos(theta), jnp.sin(theta)
    return jnp.concatenate([cosine, cosine], axis=1), jnp.concatenate([-sine, sine], axis=1)


def per_device(
    tokens,
    attn_gain,
    query_weight,
    key_weight,
    value_weight,
    out_weight,
    ffn_gain,
    router_weight,
    shared_gate,
    shared_up,
    shared_down,
    expert_gate,
    expert_up,
    expert_down,
    routes,
    keep_mask,
    cotangent,
):
    e, h = lax.axis_index("ep"), lax.axis_index("hp")
    ep = lax.axis_size("ep")
    stages = ep // 2
    rows, width = tokens.shape
    top = routes.shape[1]
    total = router_weight.shape[1]
    capacity = -(-(5 * rows * top // (4 * total)) // 16) * 16
    e_arr, h_arr = jnp.full((1,), e, jnp.int32), jnp.full((1,), h, jnp.int32)

    units = shared_down.shape[0] // ep
    pad = -(-units // 16) * 16
    tiny = [attn_gain[:, None], ffn_gain[:, None], router_weight]
    small = jnp.concatenate(tiny + [jnp.zeros((width // 4, LANES - 2 - total), BF)], axis=1)

    unit = jnp.arange(LANES)
    to = (unit // pad) * (ep * units) + unit % pad
    to = jnp.where((unit < 4 * pad) & (unit % pad < units), to, -ep * units)
    column = jnp.arange(4 * ep * units)
    mine = (column[:, None] == (to + e * units)[None, :]).astype(BF)
    small = [small, dot(shared_gate, mine).astype(BF), dot(shared_up, mine).astype(BF)]
    small = jnp.concatenate(small, axis=1)
    sd = lax.dynamic_slice_in_dim(shared_down, e * units, units, axis=0)
    sd = jnp.pad(sd, ((0, pad - units), (0, 0)))
    blocks = [key_weight, value_weight, query_weight, out_weight, small, sd]
    experts = jnp.concatenate(
        [jnp.swapaxes(expert_gate, 1, 2), jnp.swapaxes(expert_up, 1, 2), expert_down], axis=1
    )
    fused = stages == 4
    if fused:
        far_tokens, experts_core, g_near, *blocks = front(
            stages, tokens, experts, cotangent, blocks, 4
        )
        own = experts[:, : 2 * expert_down.shape[1]]
        experts_far = swap_y(after(own, blocks[0]))
        g_far = swap_pair(g_near[: stages - 1])
    else:
        far_tokens = swap_y(tokens)
        blocks = [absolute(jnp.stack(gather_hp(v)), h, 0) for v in blocks]
        g_blocks = gather_ep(cotangent)
        experts = gather_hp(experts)
    k_w, v_w, q_w, o_w, small = (v.reshape(width, v.shape[2]) for v in blocks[:5])
    gain_one = small[:, 0].astype(F32)[None, :]
    gain_two = small[:, 1].astype(F32)[None, :]
    router = small[:, 2 : 2 + total]
    sg, su = small[:, LANES : 2 * LANES], small[:, 2 * LANES :]
    sd = blocks[5].reshape(4 * pad, width)
    if 4 * pad < LANES:
        sd = jnp.pad(sd, ((0, LANES - 4 * pad), (0, 0)))

    pos = jnp.arange(rows, dtype=jnp.int32)
    pos = jnp.concatenate([(h ^ i) * rows + pos for i in (0, 2, 1, 3)])
    cosine, sine = rotary_tables(pos)
    residual = tokens.astype(F32)
    table = cosine[: 2 * rows], sine[: 2 * rows]
    first_in, kv_a, query = project(tokens, far_tokens, gain_one, k_w, v_w, q_w, *table)
    kv_b = swap_core(kv_a)
    mixed, lse = attend(h_arr, query, kv_a, kv_b)
    routes, keep_mask, late = after((routes, keep_mask, jnp.arange(ep)), query)
    if fused:
        mixed = after(mixed, g_far)
    middle = residual + dot(mixed, o_w)
    inv_two = rms(middle)
    second_in = (middle * inv_two * gain_two).astype(BF)

    expert = jnp.arange(total, dtype=jnp.int32)
    hit_each = routes[:, :, None] == expert[None, None, :]
    hit = jnp.any(hit_each, axis=1)
    kept = jnp.sum(jnp.where(hit_each, keep_mask[:, :, None], 0), axis=1)
    below = (jnp.arange(rows)[:, None] > jnp.arange(rows)[None, :]).astype(BF)
    place = jnp.where(hit, dot(below, hit.astype(BF)), -1.0)
    kept = kept.astype(F32)

    logits = jnp.where(hit, dot(second_in, router), -1e30)
    gates_of = jnp.where(hit, jnp.exp(logits - jnp.max(logits, axis=1, keepdims=True)), 0.0)
    gates_of = gates_of / jnp.sum(gates_of, axis=1, keepdims=True)
    pair_weight = gates_of * kept
    flat = (2, ep * capacity)

    hidden = expert_down.shape[1]

    def expert_grad(left, right):
        return jnp.einsum("xna,xnb->xab", left, right, preferred_element_type=F32)

    if fused:
        meta = jnp.concatenate([pair_weight.T, place.T], axis=0)
        experts = [experts, experts_far, experts_core]
        dx_sum, weight_back, near, far, sgg, sdg, xr, gr, gu, wa = dispatch(
            capacity, total, second_in, meta, g_near, g_far, experts, sg, su, sd
        )
        weight_back = weight_back.T
        xr, gr, gu, wa = (v.reshape(flat + (v.shape[-1],)) for v in (xr, gr, gu, wa))
        piece_near, piece_sum = expert_grads(xr, gr, gu, wa, hidden)
    else:
        x_ext = jnp.concatenate(
            [
                second_in,
                pair_weight.astype(BF),
                place.astype(BF),
                jnp.zeros((rows, LANES - 2 * total), BF),
            ],
            axis=1,
        )
        x_blocks = gather_ep(after(x_ext, g_blocks))
        carry = (jnp.zeros((width, 2 * LANES), F32), jnp.zeros((LANES, width), F32))
        bufs, dx_parts = None, []
        gates, ups = (
            [jnp.swapaxes(v[:, i * hidden : (i + 1) * hidden], 1, 2) for v in experts]
            for i in (0, 1)
        )
        downs = [v[:, 2 * hidden :] for v in experts]
        for k in range(stages):
            dx, carry, bufs = expert_stage(
                k,
                stages,
                capacity,
                total,
                e_arr,
                x_blocks[k],
                g_blocks[k],
                gates,
                ups,
                downs,
                sg,
                su,
                sd,
                carry,
                bufs,
            )
            dx_parts.append(dx)
        dx_sum = scatter_ep(dx_parts)
        weight_back = (
            dx_sum[:, width : width + total] + dx_sum[:, width + total : width + 2 * total]
        )
        dx_sum = dx_sum[:, :width]
        sgg, sdg = carry
        sa, xr, gr, gi, ui, wa = bufs
        out_parts = [
            expert_out(k, capacity, total, e_arr, x_blocks[k], wa, sa, downs, sd)
            for k in range(stages)
        ]
        xr, gr = xr.reshape(flat + (width,)), gr.reshape(flat + (width,))
        gi, ui, wa = (v.reshape((4,) + flat + (v.shape[-1],)) for v in (gi, ui, wa))
        routed = scatter_ep(after(out_parts, dx_sum))
        expert_sum = scatter_hp(
            [
                jnp.concatenate(
                    [
                        expert_grad(gi[r], xr),
                        expert_grad(ui[r], xr),
                        expert_grad(wa[r], gr),
                    ],
                    axis=1,
                )
                for r in range(4)
            ]
        )

    grad_out = cotangent.astype(F32)
    gate_back = weight_back * kept
    chosen_back = gates_of * (gate_back - jnp.sum(gates_of * gate_back, axis=1, keepdims=True))
    logits_back = chosen_back.astype(BF)
    router_part = dot(logits_back, second_in, (0, 0))
    second_back = dx_sum + dot(logits_back, router, (1, 1))
    gain_two_part = jnp.sum(second_back * middle * inv_two, axis=0)
    middle_back = grad_out + norm_back(middle, inv_two, gain_two, second_back)
    attn_back = middle_back.astype(BF)
    counts_part = jnp.pad(jnp.sum(kept, axis=0), (0, width - total))

    mixed_back = dot(attn_back, o_w, (1, 1)).astype(BF)
    out_part = dot(mixed, attn_back, (0, 0))
    sgg = sgg.reshape(4, width // 4, 2 * LANES)
    sdg = sdg[: 4 * pad].reshape(4, pad, width)
    block = late[:, None, None] * units
    spread = (to[None, :, None] + block == column[None, None, :]).astype(BF)

    def small_sums(gain_one_part):
        lines = [router_part, gain_two_part[None, :], counts_part[None, :], gain_one_part]
        return jnp.concatenate(lines + [jnp.zeros((-(total + 3) % 8, width), F32)], axis=0)

    if fused:
        sdg = sdg.astype(BF)
        at = jnp.where(jnp.arange(pad) < units, jnp.arange(pad), -ep * units)[None, None, :]
        stack = (at + block == jnp.arange(ep * units)[None, :, None]).astype(BF)
        (
            q_part,
            k_part,
            v_part,
            first_back,
            share,
            gain_one_part,
            sgate_grad,
            sup_grad,
            sdown_grad,
            layer,
            piece_far,
        ) = attend_back_and_sums(
            query,
            kv_a,
            kv_b,
            mixed_back,
            lse,
            (q_w, k_w, v_w),
            (cosine, sine),
            first_in,
            (tokens, far_tokens),
            sgg.astype(BF).reshape(2, 2, width // 4, 2 * LANES),
            sdg.reshape(2, 2, pad, width),
            spread,
            stack,
            near,
            middle,
            far,
            piece_sum,
        )
        out, sums, tokens_grad = tail(
            [q_part, k_part, v_part, out_part.astype(BF)],
            small_sums(gain_one_part),
            share,
            tokens,
            gain_one,
            first_back,
            middle_back,
        )
        grads = [out[i].astype(F32) for i in range(4)]
        spans = [slice(i * hidden, (i + 1) * hidden) for i in range(3)]
        gate_grad, up_grad, down_grad = (
            piece_near[:, a].astype(F32) + piece_far[:, a].astype(F32) for a in spans
        )
    else:
        query_raw, near_back, far_back = attend_back(
            h_arr, query, kv_a, kv_b, mixed_back, lse, cosine, sine
        )
        kv_raw = (near_back + swap_core(far_back).astype(F32)).astype(BF)
        key_raw, value_raw = kv_raw[0], kv_raw[1]
        kv_back = dot(key_raw, k_w, (1, 1)) + dot(value_raw, v_w, (1, 1))
        q_part = dot(first_in[:rows], query_raw, (0, 0))
        k_part = dot(first_in, key_raw, (0, 0))
        v_part = dot(first_in, value_raw, (0, 0))
        first_back = kv_back[:rows] + dot(query_raw, q_w, (1, 1))
        gain_one_part = jnp.zeros((1, width), F32)
        for values, upstream in ((tokens, first_back), (far_tokens, kv_back[rows:])):
            values = values.astype(F32)
            gain_one_part += jnp.sum(upstream * values * rms(values), axis=0, keepdims=True)

        def over_hp(v):
            return scatter_hp(jnp.split(relative(v, h, 0), 4, axis=0))

        grads = [sum_ep(over_hp(v), e) for v in (q_part, k_part, v_part, out_part)]
        sums = sum_all_small(small_sums(gain_one_part))
        first_back = first_back + swap_y(kv_back[rows:].astype(BF)).astype(F32)
        tokens_grad = middle_back + norm_back(residual, rms(residual), gain_one, first_back)
        sgg, sdg = (spread_ep(over_hp(v)[0].astype(BF), e) for v in (sgg, sdg))
        sgate_grad, sup_grad = (
            jnp.einsum("kra,kan->rn", v, spread, preferred_element_type=F32)
            for v in (sgg[:, :, :LANES], sgg[:, :, LANES:])
        )
        sdown_grad = sdg[:, :units].reshape(ep * units, width).astype(F32)
        layer = (middle + routed).astype(BF)
        gate_grad, up_grad, down_grad = jnp.split(expert_sum, 3, axis=1)
    gate_grad, up_grad = jnp.swapaxes(gate_grad, 1, 2), jnp.swapaxes(up_grad, 1, 2)

    def own(v, n):
        return lax.dynamic_slice_in_dim(v, h * n, n, axis=0)

    return (
        layer,
        tokens_grad,
        own(sums[total + 2], width // 4),
        *grads,
        own(sums[total], width // 4),
        own(sums[:total].T, width // 4),
        sgate_grad,
        sup_grad,
        sdown_grad,
        gate_grad,
        up_grad,
        down_grad,
        own(sums[total + 1], total // 4).astype(jnp.int32),
    )


def solution(mesh):
    row, ep_hp = P("hp", None), P(("ep", "hp"), None)
    return jax.shard_map(
        per_device,
        mesh=mesh,
        in_specs=(
            ep_hp,
            P("hp"),
            row,
            row,
            row,
            row,
            P("hp"),
            row,
            row,
            row,
            row,
            P("ep", None, "hp"),
            P("ep", None, "hp"),
            P("ep", "hp", None),
            ep_hp,
            ep_hp,
            ep_hp,
        ),
        out_specs=(
            ep_hp,
            ep_hp,
            P("hp"),
            row,
            row,
            row,
            row,
            P("hp"),
            row,
            row,
            row,
            row,
            P("ep", None, "hp"),
            P("ep", None, "hp"),
            P("ep", "hp", None),
            P("hp"),
        ),
        check_vma=False,
    )
```
